32 devices in a mesh: section: 2 (over x), seq: 16 (over z, y, core).
Axes of the slice: x: 2, y: 2, z: 4, core: 2. Of those that a mesh axis runs over, the one named last changes fastest.
Arguments:
- inputs: bfloat16 [2, 4096, 768], P(None, 'seq'), may hold values from -6 to 6
- cotangent: bfloat16 [2, 4096, 768], P(None, 'seq'), may hold values from -6 to 6
- documents: int32 [2, 4096], replicated, may hold values from 0 to 2, as said below
- w_qkv: float32 [2, 768, 2304], P('section', 'seq'), may hold values from -0.21875 to 0.21875
- w_out: float32 [2, 768, 768], P('section', 'seq'), may hold values from -1.75 to 1.75
- w_up: float32 [2, 768, 3072], P('section', 'seq'), may hold values from -0.21875 to 0.21875
- w_down: float32 [2, 3072, 768], P('section', 'seq'), may hold values from -0.109375 to 0.109375
- norm_gains: float32 [2, 2, 768], P('section', None, 'seq'), may hold values from 0.5 to 1.5
- biases: float32 [2, 6, 768], P('section', None, 'seq'), may hold values from -3 to 3
- up_bias: float32 [2, 3072], P('section', 'seq'), may hold values from -3 to 3
Outputs:
- layer_outputs: bfloat16 [2, 2, 4096, 768], P('section', None, 'seq')
- input_grads: float32 [2, 2, 4096, 768], P('section', None, 'seq')
- grad_qkv: float32 [2, 768, 2304], P('section', 'seq')
- grad_out: float32 [2, 768, 768], P('section', 'seq')
- grad_up: float32 [2, 768, 3072], P('section', 'seq')
- grad_down: float32 [2, 3072, 768], P('section', 'seq')
- grad_gains: float32 [2, 2, 768], P('section', None, 'seq')
- grad_biases: float32 [2, 6, 768], P('section', None, 'seq')
- grad_up_bias: float32 [2, 3072], P('section', 'seq')
The draws below stay inside these ranges and needn't reach their ends.
Inputs may be any that keep to these rules, and one draw needn't show every extreme that they name: `documents`: in each micro-batch the ids start at 0, never fall and rise by at most one from a tile to the next; a slide is the run of tiles that share an id, and the last id of every micro-batch is the largest.
All inputs are finite; a program needn't handle non-finite values.
Results may differ from the reference program's by a relative error of at most 0.012.
The reference program's roundings to bfloat16 on the way count: a program that leaves them out, or rounds other values in their place, can miss the bound.
Values may be sent and summed in bfloat16 or wider, within the bound.
No kernel may reach another device: no remote copies, remote signals or barrier semaphores. Data moves between devices by JAX's collectives and lax.ppermute only.
A program may use at most 512 MiB of HBM per device.

```python
import jax
import jax.numpy as jnp
from jax import lax

D = 768
HEADS = 16
FF = 3072
HEAD_DIM = 48
TOK_DEV = 256
MICRO = 2
SEG0 = 1024
BRANCHES = 5
TOKENS = 4096


def draw_documents(key, part):
    key = jax.random.fold_in(key, 7)
    offset_key, place_key = jax.random.split(key)
    block_len = 8 * TOK_DEV
    block_count = TOKENS // block_len
    positions = jnp.arange(TOKENS)
    block_of = positions // block_len
    chosen = jax.random.randint(place_key, (), 0, MICRO)
    offsets = jax.random.randint(offset_key, (MICRO, block_count), 1, block_len)
    cut_rows = (jnp.arange(MICRO) != chosen)[:, None]
    boundary = ((positions % block_len)[None, :] == offsets[:, block_of]) & cut_rows
    return jnp.cumsum(boundary.astype(jnp.int32), axis=1).astype(jnp.int32)


def block_levels(rng, extent, cuts, least, top_value):
    factor_of = 1.0
    for dim, shards_of in cuts:
        draws = jax.random.uniform(jax.random.fold_in(jax.random.fold_in(rng, 6), dim), (shards_of,), jnp.float32, least / len(cuts), top_value / len(cuts))
        factor_of = factor_of * jnp.repeat(jnp.exp(draws), extent[dim] // shards_of).reshape((-1,) + (1,) * (len(extent) - 1 - dim))
    return factor_of


def centred(key, shape, scale, most, shards=(), held_as=jnp.bfloat16):
    entries = jax.random.normal(key, shape, jnp.float32) * scale
    if len(shards) > 0:
        entries = block_levels(key, shape, shards, -0.22, 0.18) * entries
    return jnp.clip(entries, min=-most, max=most).astype(held_as)


def setup_inputs(seed: int = 0) -> dict:
    seeds = jax.random.split(jax.random.key(seed), 11)
    return {
        "inputs": centred(seeds[0], (MICRO, TOKENS, D), 1.0, 6.0, ((1, 16),)),
        "cotangent": centred(seeds[1], (MICRO, TOKENS, D), 1.0, 6.0, ((1, 16),)),
        "documents": draw_documents(jax.random.fold_in(seeds[10], 71), 0),
        "w_qkv": centred(seeds[3], (2, D, 3 * D), D ** -0.5, 0.21875, ((0, 2), (1, 16)), jnp.float32),
        "w_out": centred(seeds[4], (2, D, D), (D // 64) ** -0.5, 1.75, ((0, 2), (1, 16)), jnp.float32),
        "w_up": centred(seeds[5], (2, D, FF), D ** -0.5, 0.21875, ((0, 2), (1, 16)), jnp.float32),
        "w_down": centred(seeds[6], (2, FF, D), FF ** -0.5, 0.109375, ((0, 2), (1, 16)), jnp.float32),
        "norm_gains": jnp.clip(1.0 + 0.1 * jax.random.normal(seeds[7], (2, 2, D), jnp.float32), 0.5, 1.5),
        "biases": centred(seeds[8], (2, 6, D), 0.3, 3.0, ((0, 2), (2, 16)), jnp.float32),
        "up_bias": centred(seeds[9], (2, FF), 0.3, 3.0, ((0, 2), (1, 16)), jnp.float32),
    }


@jax.custom_vjp
def low(v):
    return lax.optimization_barrier(v.astype(jnp.bfloat16)).astype(jnp.float32)

@jax.custom_vjp
def low_back(v):
    return v

def low_keep(v):
    return (low(v), None)

def low_pass(kept, grad):
    return (grad,)

def back_keep(v):
    return (v, None)

def back_low(kept, grad):
    return (low(grad),)
low.defvjp(low_keep, low_pass)
low_back.defvjp(back_keep, back_low)
epsilon = 1e-05
masked_score = -1e+30
highest = lax.Precision.HIGHEST

def layer_norm(values, gain_row, shift_row):
    center = values - lax.optimization_barrier(jnp.mean(values, axis=-1, keepdims=True))
    spread = lax.optimization_barrier(jnp.mean(center * center, axis=-1, keepdims=True))
    return center * lax.rsqrt(spread + epsilon) * gain_row + shift_row

def product(left, right):
    return jnp.dot(left, right, precision=highest, preferred_element_type=jnp.float32)

def branch(queries, key_part, values, documents, level_id):
    token_count = queries.shape[0]
    dilation = 2 ** level_id
    segment = min(SEG0 * dilation, token_count)
    groups = token_count // segment
    picked = segment // dilation
    offsets = jnp.arange(HEADS) % dilation
    pick_grid = (jnp.arange(dilation)[:, None] == offsets[None, :]).astype(jnp.float32)

    def select(tensor):
        shaped = tensor.reshape(groups, picked, dilation, HEADS, HEAD_DIM)
        return jnp.einsum('gprhd,rh->gphd', shaped, pick_grid, precision=highest)
    doc_sel = jnp.take(documents.reshape(groups, picked, dilation), offsets, axis=2)

    def segment_block(pieces):
        query_part, key_block, value_part, doc_part = pieces
        scores = jnp.einsum('qhd,khd->hqk', query_part, key_block, precision=highest) * HEAD_DIM ** (-0.5)
        scores = low_back(scores)
        heads_doc = doc_part.T
        scores = jnp.where(heads_doc[:, :, None] == heads_doc[:, None, :], scores, masked_score)
        row_max = lax.optimization_barrier(jnp.max(scores, axis=-1, keepdims=True))
        weights = jnp.exp(scores - row_max)
        row_total = lax.optimization_barrier(jnp.sum(weights, axis=-1, keepdims=True))
        prob_rows = weights / row_total
        summary = (row_max + jnp.log(row_total))[:, :, 0]
        result = jnp.einsum('hqk,khd->qhd', low(prob_rows), value_part, precision=highest)
        return (low_back(result), summary.T)
    outputs, summaries = lax.map(jax.checkpoint(segment_block), (select(queries), select(key_part), select(values), doc_sel))
    full_out = jnp.einsum('gphd,rh->gprhd', outputs, pick_grid, precision=highest).reshape(token_count, HEADS, HEAD_DIM)
    full_sum = jnp.where(pick_grid[None, None] > 0, summaries[:, :, None, :], masked_score).reshape(token_count, HEADS)
    return (full_out, full_sum)

def attend(queries, key_part, values, documents):
    token_count = queries.shape[0]
    shape_heads = (token_count, HEADS, HEAD_DIM)
    branch_parts = [branch(queries.reshape(shape_heads), key_part.reshape(shape_heads), values.reshape(shape_heads), documents, level_id) for level_id in range(BRANCHES)]
    summaries = jnp.stack([member[1] for member in branch_parts])
    row_max = lax.optimization_barrier(jnp.max(summaries, axis=0))
    shares = jnp.exp(summaries - row_max)
    shares = shares / lax.optimization_barrier(jnp.sum(shares, axis=0))
    merged = sum((shares[level_id][:, :, None] * branch_parts[level_id][0] for level_id in range(BRANCHES)))
    return merged.reshape(token_count, HEADS * HEAD_DIM)

def layer_step(hidden, documents, weights):
    w_qkv, w_out, w_up, w_down, gains, biases, up_bias = [low(member) for member in weights]
    normed = low(layer_norm(hidden, gains[0], biases[0]))
    mixed_rows = product(normed, w_qkv)
    queries = low(low_back(mixed_rows[:, :D] + biases[1]))
    key_part = low(low_back(mixed_rows[:, D:2 * D]))
    values = low(low_back(mixed_rows[:, 2 * D:] + biases[2]))
    attended = low(attend(queries, key_part, values, documents))
    branch_out = low_back(product(attended, w_out) + biases[3])
    middle = hidden + branch_out
    normed_two = low(layer_norm(middle, gains[1], biases[4]))
    upward = low_back(product(normed_two, w_up) + up_bias)
    activated = low(jax.nn.gelu(upward, approximate=False))
    downward = low_back(product(activated, w_down) + biases[5])
    return middle + downward

def reference(inputs, cotangent, documents, w_qkv, w_out, w_up, w_down, norm_gains, biases, up_bias):
    params = tuple((member.astype(jnp.float32) for member in (w_qkv, w_out, w_up, w_down, norm_gains, biases, up_bias)))
    totals = [jnp.zeros_like(member) for member in params]
    first_list, final_list, grad_first, grad_second = ([], [], [], [])
    for batch_id in range(MICRO):
        documents_now = documents[batch_id]

        def forward(start_rows, delta_rows, *weights):
            first_out = low(layer_step(start_rows, documents_now, [member[0] for member in weights]))
            middle_rows = low_back(first_out + delta_rows)
            return (layer_step(middle_rows, documents_now, [member[1] for member in weights]), first_out)
        start_rows = inputs[batch_id].astype(jnp.float32)
        final_out, pullback, first_out = jax.vjp(forward, start_rows, jnp.zeros_like(start_rows), *params, has_aux=True)
        gradients = pullback(cotangent[batch_id].astype(jnp.float32))
        grad_first.append(gradients[0])
        grad_second.append(gradients[1])
        totals = [earlier + latter for earlier, latter in zip(totals, gradients[2:])]
        first_list.append(first_out.astype(jnp.bfloat16))
        final_list.append(final_out.astype(jnp.bfloat16))
    layer_outputs = jnp.stack([jnp.stack(first_list), jnp.stack(final_list)])
    input_grads = jnp.stack([jnp.stack(grad_first), jnp.stack(grad_second)])
    return (layer_outputs, input_grads, totals[0], totals[1], totals[2], totals[3], totals[4], totals[5], totals[6])
```

```python
import functools
import math

import jax
import jax.numpy as jnp
import numpy as np
from jax import lax
from jax.experimental import pallas as pl
from jax.experimental.pallas import tpu as pltpu
from jax.sharding import PartitionSpec as P

D = 768
HEADS = 16
HEAD_DIM = 48
SEG0 = 1024
BRANCHES = 5


epsilon = 1e-05
masked_score = -1e30
highest = lax.Precision.HIGHEST


def swapped(value, axis, apart):
    mask = 2**apart
    pairs = [(source, source ^ mask) for source in range(lax.axis_size(axis))]
    return lax.ppermute(value, axis, pairs)


def for_sending(array):
    return jax.tree.map(lambda a: a.astype(jnp.bfloat16) if a.dtype == jnp.float32 else a, array)


def passed_along(array, axis, by):
    peers = lax.axis_size(axis)
    pairs = [(i, i + by) for i in range(peers) if 0 <= i + by < peers]
    return lax.ppermute(array, axis, pairs)


def layer_norm_parts(values, gain_row, shift_row):
    center = values - jnp.mean(values, axis=-1, keepdims=True)
    spread = jnp.mean(center * center, axis=-1, keepdims=True)
    return center * lax.rsqrt(spread + epsilon) * gain_row + shift_row


def exact_gelu(values):
    return jax.nn.gelu(values, approximate=False)


def inner_rows(left, right):
    return jnp.einsum("ta,tb->ab", left, right, preferred_element_type=jnp.float32)


def geometry(tokens_dev, devices):
    groups = [
        min(SEG0 * 2**level_id, tokens_dev * devices) // tokens_dev for level_id in range(BRANCHES)
    ]
    return (groups, max(groups).bit_length() - 1)


def first_level(groups, step_id):
    return min((level_id for level_id in range(BRANCHES) if groups[level_id] > 2**step_id))


def pick_grid(level_id, dtype):
    dilation = 2**level_id
    return (jnp.arange(dilation)[:, None] == (jnp.arange(HEADS) % dilation)[None, :]).astype(dtype)


def select_rows(tensor, level_id):
    dilation = 2**level_id
    shaped = tensor.reshape((tensor.shape[0] // dilation, dilation) + tensor.shape[1:])
    if tensor.dtype == jnp.bfloat16:
        chosen = jnp.einsum(
            "jrh...,rh->jh...",
            shaped,
            pick_grid(level_id, jnp.bfloat16),
            preferred_element_type=jnp.float32,
        )
        return chosen.astype(jnp.bfloat16)
    return jnp.einsum(
        "jrh...,rh->jh...", shaped, pick_grid(level_id, jnp.float32), precision=highest
    )


def spread_rows(tensor, level_id):
    dilation = 2**level_id
    spread = jnp.einsum(
        "jh...,rh->jrh...", tensor, pick_grid(level_id, jnp.float32), precision=highest
    )
    return spread.reshape((tensor.shape[0] * dilation,) + tensor.shape[1:])


def spread_sums(tensor, level_id):
    dilation = 2**level_id
    grid = pick_grid(level_id, jnp.float32)
    spread = jnp.where(grid[None] > 0, tensor[:, None, :], masked_score)
    return spread.reshape(tensor.shape[0] * dilation, HEADS)


def doc_tables(documents_now, level_id, group, tokens_dev, seq_place):
    dilation = 2**level_id
    offsets = np.arange(HEADS) % dilation
    own_docs = lax.dynamic_slice_in_dim(documents_now, seq_place * tokens_dev, tokens_dev)
    own_docs = own_docs.reshape(tokens_dev // dilation, dilation)[:, offsets]
    seg_start = seq_place // group * group * tokens_dev
    seg_docs = lax.dynamic_slice_in_dim(documents_now, seg_start, group * tokens_dev)
    seg_docs = seg_docs.reshape(group * tokens_dev // dilation, dilation)[:, offsets]
    return (own_docs, seg_docs)


def head_bits(level_id):
    return jnp.arange(HEADS) >> level_id & 1


def halve(buffer, level_id):
    pairs = buffer.reshape(buffer.shape[0], buffer.shape[1] // 2, 2, HEADS, HEAD_DIM)
    chosen = head_bits(level_id)[None, None, :, None] == 1
    return jnp.where(chosen, pairs[:, :, 1], pairs[:, :, 0])


def widen(buffer, level_id):
    chosen = head_bits(level_id)[None, None, :, None] == 1
    empty = jnp.zeros_like(buffer)
    upper_part = jnp.where(chosen, buffer, empty)
    lower_part = jnp.where(chosen, empty, buffer)
    stacked = jnp.stack([lower_part, upper_part], axis=2)
    return stacked.reshape(buffer.shape[0], buffer.shape[1] * 2, HEADS, HEAD_DIM)


def thin_to(buffer, low_level, high_level):
    for level_id in range(low_level, high_level):
        buffer = halve(buffer, level_id)
    return buffer


def widen_to(buffer, low_level, high_level):
    for level_id in reversed(range(low_level, high_level)):
        buffer = widen(buffer, level_id)
    return buffer


def gather_keys(own_rows, groups, step_count, seq_place):
    results = [None] * BRANCHES
    current = own_rows
    level_now = 0
    for level_id in range(BRANCHES):
        pass
    for step_id in range(step_count):
        target = first_level(groups, step_id)
        current = thin_to(current, level_now, target)
        level_now = target
        row_count = current.shape[1]
        flat_rows = current.reshape(2, row_count, HEADS * HEAD_DIM)
        incoming = swapped(flat_rows, "seq", step_id).reshape(current.shape)
        upper_half = seq_place >> step_id & 1 == 1
        current = jnp.where(
            upper_half,
            jnp.concatenate([incoming, current], axis=1),
            jnp.concatenate([current, incoming], axis=1),
        )
        for level_id in range(BRANCHES):
            if groups[level_id] == 2 ** (step_id + 1):
                results[level_id] = thin_to(current, level_now, level_id)
    return results


def scatter_keys(key_grads, groups, step_count, seq_place):
    carried = None
    for step_id in reversed(range(step_count)):
        level_now = first_level(groups, step_id)
        total_grad = None
        if carried is not None:
            total_grad = widen_to(carried, level_now, first_level(groups, step_id + 1))
        for level_id in range(BRANCHES):
            if groups[level_id] == 2 ** (step_id + 1):
                branch_term = widen_to(key_grads[level_id], level_now, level_id)
                total_grad = branch_term if total_grad is None else total_grad + branch_term
        half_rows = total_grad.shape[1] // 2
        upper_half = seq_place >> step_id & 1 == 1
        own_half = jnp.where(upper_half, total_grad[:, half_rows:], total_grad[:, :half_rows])
        theirs = jnp.where(upper_half, total_grad[:, :half_rows], total_grad[:, half_rows:])
        flat_rows = theirs.reshape(2, half_rows, HEADS * HEAD_DIM)
        incoming = (
            swapped(for_sending(flat_rows), "seq", step_id)
            .astype(flat_rows.dtype)
            .reshape(own_half.shape)
        )
        carried = own_half + incoming
    own_grad = widen_to(carried, 0, first_level(groups, 0))
    for level_id in range(BRANCHES):
        pass
    return own_grad


def head_blocks(level_id):
    block_size = min(HEADS, 4 * 2**level_id)
    return (HEADS // block_size, block_size)


def to_blocks(tensor, block_count, block_size):
    moved = jnp.moveaxis(tensor, 1, 0)
    return moved.reshape((block_count, block_size) + moved.shape[1:])


def from_blocks(tensor):
    joined = tensor.reshape((tensor.shape[0] * tensor.shape[1],) + tensor.shape[2:])
    return jnp.moveaxis(joined, 0, 1)


def score_block(query_block, key_block, query_doc, key_doc):
    scores = jnp.einsum(
        "hqd,hkd->hqk", query_block, key_block, preferred_element_type=jnp.float32
    ) * HEAD_DIM ** (-0.5)
    return jnp.where(query_doc[:, :, None] == key_doc[:, None, :], scores, masked_score)


def forward_block(pieces):
    query_block, key_block, value_block, query_doc, key_doc = pieces
    scores = score_block(query_block, key_block, query_doc, key_doc)
    row_max = jnp.max(scores, axis=-1, keepdims=True)
    weights = jnp.exp(scores - row_max)
    row_total = jnp.sum(weights, axis=-1, keepdims=True)
    prob_rows = (weights / row_total).astype(jnp.bfloat16)
    result = jnp.einsum("hqk,hkd->hqd", prob_rows, value_block, preferred_element_type=jnp.float32)
    return (result, (row_max + jnp.log(row_total))[:, :, 0])


def backward_block(pieces):
    query_block, key_block, value_block, query_doc, key_doc, summary, out_grad, summary_grad = (
        pieces
    )
    scores = score_block(query_block, key_block, query_doc, key_doc)
    prob_rows = jnp.exp(scores - summary[:, :, None])
    prob_grad = jnp.einsum(
        "hqd,hkd->hqk", out_grad, value_block, preferred_element_type=jnp.float32
    )
    score_grad = prob_rows * (
        prob_grad
        - jnp.sum(prob_rows * prob_grad, axis=-1, keepdims=True)
        + summary_grad[:, :, None]
    )
    score_grad = score_grad.astype(jnp.bfloat16)
    score_scale = HEAD_DIM ** (-0.5)
    query_grad = (
        jnp.einsum("hqk,hkd->hqd", score_grad, key_block, preferred_element_type=jnp.float32)
        * score_scale
    )
    key_grad = (
        jnp.einsum("hqk,hqd->hkd", score_grad, query_block, preferred_element_type=jnp.float32)
        * score_scale
    )
    value_grad = jnp.einsum(
        "hqk,hqd->hkd", prob_rows.astype(jnp.bfloat16), out_grad, preferred_element_type=jnp.float32
    )
    return (query_grad, key_grad, value_grad)


def branch_forward(query_sel, key_value, query_docs, key_docs, level_id):
    block_count, block_size = head_blocks(level_id)
    pieces = (
        to_blocks(query_sel, block_count, block_size),
        to_blocks(key_value[0], block_count, block_size),
        to_blocks(key_value[1], block_count, block_size),
        to_blocks(query_docs, block_count, block_size),
        to_blocks(key_docs, block_count, block_size),
    )
    results, summaries = lax.map(forward_block, pieces)
    return (from_blocks(results), from_blocks(summaries))


def branch_backward(
    query_sel, key_value, query_docs, key_docs, summary, out_grad, summary_grad, level_id
):
    block_count, block_size = head_blocks(level_id)
    pieces = (
        to_blocks(query_sel, block_count, block_size),
        to_blocks(key_value[0], block_count, block_size),
        to_blocks(key_value[1], block_count, block_size),
        to_blocks(query_docs, block_count, block_size),
        to_blocks(key_docs, block_count, block_size),
        to_blocks(summary, block_count, block_size),
        to_blocks(out_grad, block_count, block_size),
        to_blocks(summary_grad, block_count, block_size),
    )
    query_grad, key_grad, value_grad = lax.map(backward_block, pieces)
    return (from_blocks(query_grad), jnp.stack([from_blocks(key_grad), from_blocks(value_grad)]))


def layer_forward(hidden, params, documents_now, groups, step_count, seq_place):
    w_qkv, w_out, w_up, w_down, gains, biases, up_bias = params
    gains = gains.astype(jnp.float32)
    biases = biases.astype(jnp.float32)
    tokens_dev = hidden.shape[0]
    normed = layer_norm_parts(hidden, gains[0], biases[0]).astype(jnp.bfloat16)
    mixed_rows = jnp.dot(normed, w_qkv, preferred_element_type=jnp.float32)
    queries = (mixed_rows[:, :D] + biases[1]).astype(jnp.bfloat16)
    key_part = mixed_rows[:, D : 2 * D].astype(jnp.bfloat16)
    values = (mixed_rows[:, 2 * D :] + biases[2]).astype(jnp.bfloat16)
    own_rows = jnp.stack([key_part, values]).reshape(2, tokens_dev, HEADS, HEAD_DIM)
    gathered = gather_keys(own_rows, groups, step_count, seq_place)
    query_heads = queries.reshape(tokens_dev, HEADS, HEAD_DIM)
    picked, branch_outs, branch_sums = ([], [], [])
    for level_id in range(BRANCHES):
        query_sel = select_rows(query_heads, level_id)
        query_docs, key_docs = doc_tables(
            documents_now, level_id, groups[level_id], tokens_dev, seq_place
        )
        result, summary = branch_forward(
            query_sel, gathered[level_id], query_docs, key_docs, level_id
        )
        picked.append(query_sel)
        branch_outs.append(result)
        branch_sums.append(summary)
    full_sums = jnp.stack(
        [spread_sums(branch_sums[level_id], level_id) for level_id in range(BRANCHES)]
    )
    row_max = jnp.max(full_sums, axis=0)
    shares = jnp.exp(full_sums - row_max)
    shares = shares / jnp.sum(shares, axis=0)
    merged = sum(
        (
            shares[level_id][:, :, None] * spread_rows(branch_outs[level_id], level_id)
            for level_id in range(BRANCHES)
        )
    )
    attended = merged.reshape(tokens_dev, D).astype(jnp.bfloat16)
    middle = hidden + jnp.dot(attended, w_out, preferred_element_type=jnp.float32) + biases[3]
    normed_two = layer_norm_parts(middle, gains[1], biases[4]).astype(jnp.bfloat16)
    upward = jnp.dot(normed_two, w_up, preferred_element_type=jnp.float32) + up_bias.astype(
        jnp.float32
    )
    activated = exact_gelu(upward).astype(jnp.bfloat16)
    result = middle + jnp.dot(activated, w_down, preferred_element_type=jnp.float32) + biases[5]
    kept_values = (
        hidden,
        normed,
        picked,
        gathered,
        branch_sums,
        branch_outs,
        shares,
        merged,
        attended,
        middle,
        normed_two,
        upward,
        activated,
    )
    return (result, kept_values)


def layer_backward(incoming, kept_values, params, documents_now, groups, step_count, seq_place):
    w_qkv, w_out, w_up, w_down, gains, biases, up_bias = params
    gains = gains.astype(jnp.float32)
    biases = biases.astype(jnp.float32)
    (
        hidden,
        normed,
        picked,
        gathered,
        branch_sums,
        branch_outs,
        shares,
        merged,
        attended,
        middle,
        normed_two,
        upward,
        activated,
    ) = kept_values
    tokens_dev = hidden.shape[0]
    down_grad = incoming.astype(jnp.bfloat16)
    grad_down = inner_rows(activated, down_grad)
    grad_bias_down = jnp.sum(down_grad.astype(jnp.float32), axis=0)
    act_grad = jnp.einsum("tb,ab->ta", down_grad, w_down, preferred_element_type=jnp.float32)
    gelu_pulled = jax.vjp(exact_gelu, upward)
    up_grad = gelu_pulled[1](act_grad)[0].astype(jnp.bfloat16)
    grad_up = inner_rows(normed_two, up_grad)
    grad_up_bias = jnp.sum(up_grad.astype(jnp.float32), axis=0)
    norm_two_grad = jnp.einsum("tb,ab->ta", up_grad, w_up, preferred_element_type=jnp.float32)
    norm_pulled = jax.vjp(layer_norm_parts, middle, gains[1], biases[4])
    middle_part, grad_gain_two, grad_shift_two = norm_pulled[1](norm_two_grad)
    middle_grad = incoming + middle_part
    branch_grad = middle_grad.astype(jnp.bfloat16)
    grad_out = inner_rows(attended, branch_grad)
    grad_bias_out = jnp.sum(branch_grad.astype(jnp.float32), axis=0)
    merged_grad = jnp.einsum("tb,ab->ta", branch_grad, w_out, preferred_element_type=jnp.float32)
    merged_grad = merged_grad.reshape(tokens_dev, HEADS, HEAD_DIM)
    query_grad = jnp.zeros((tokens_dev, HEADS, HEAD_DIM), jnp.float32)
    key_grads = []
    for level_id in range(BRANCHES):
        share_sel = select_rows(shares[level_id], level_id)
        merged_sel = select_rows(merged, level_id)
        grad_sel = select_rows(merged_grad, level_id)
        out_grad = (share_sel[:, :, None] * grad_sel).astype(jnp.bfloat16)
        summary_grad = share_sel * (
            jnp.sum(grad_sel * branch_outs[level_id], axis=-1)
            - jnp.sum(grad_sel * merged_sel, axis=-1)
        )
        query_docs, key_docs = doc_tables(
            documents_now, level_id, groups[level_id], tokens_dev, seq_place
        )
        query_part, key_value_grad = branch_backward(
            picked[level_id],
            gathered[level_id],
            query_docs,
            key_docs,
            branch_sums[level_id],
            out_grad,
            summary_grad,
            level_id,
        )
        query_grad = query_grad + spread_rows(query_part, level_id)
        key_grads.append(key_value_grad)
    own_grad = scatter_keys(key_grads, groups, step_count, seq_place)
    mixed_grad = jnp.concatenate(
        [
            query_grad.reshape(tokens_dev, D),
            own_grad[0].reshape(tokens_dev, D),
            own_grad[1].reshape(tokens_dev, D),
        ],
        axis=1,
    ).astype(jnp.bfloat16)
    grad_qkv = inner_rows(normed, mixed_grad)
    grad_bias_query = jnp.sum(mixed_grad[:, :D].astype(jnp.float32), axis=0)
    grad_bias_value = jnp.sum(mixed_grad[:, 2 * D :].astype(jnp.float32), axis=0)
    normed_grad = jnp.einsum("tb,ab->ta", mixed_grad, w_qkv, preferred_element_type=jnp.float32)
    norm_pulled = jax.vjp(layer_norm_parts, hidden, gains[0], biases[0])
    hidden_part, grad_gain_one, grad_shift_one = norm_pulled[1](normed_grad)
    start_grad = middle_grad + hidden_part
    gradients = (
        grad_qkv,
        grad_out,
        grad_up,
        grad_down,
        jnp.stack([grad_gain_one, grad_gain_two]),
        jnp.stack(
            [
                grad_shift_one,
                grad_bias_query,
                grad_bias_value,
                grad_bias_out,
                grad_shift_two,
                grad_bias_down,
            ]
        ),
        grad_up_bias,
    )
    return (start_grad, gradients)


def body(inputs, cotangent, documents, w_qkv, w_out, w_up, w_down, norm_gains, biases, up_bias):
    section_id = lax.axis_index("section")
    seq_place = lax.axis_index("seq")
    devices = lax.axis_size("seq")
    micro = inputs.shape[0]
    tokens_dev = inputs.shape[1]
    groups, step_count = geometry(tokens_dev, devices)
    params = (
        lax.all_gather(w_qkv[0].astype(jnp.bfloat16), "seq", axis=0, tiled=True),
        lax.all_gather(w_out[0].astype(jnp.bfloat16), "seq", axis=0, tiled=True),
        lax.all_gather(w_up[0].astype(jnp.bfloat16), "seq", axis=0, tiled=True),
        lax.all_gather(w_down[0].astype(jnp.bfloat16), "seq", axis=0, tiled=True),
        lax.all_gather(norm_gains[0].astype(jnp.bfloat16), "seq", axis=1, tiled=True),
        lax.all_gather(biases[0].astype(jnp.bfloat16), "seq", axis=1, tiled=True),
        lax.all_gather(up_bias[0].astype(jnp.bfloat16), "seq", axis=0, tiled=True),
    )
    empty_rows = jnp.zeros((tokens_dev, D), jnp.bfloat16)
    received = empty_rows
    saved = []
    produced = []
    for tick_id in range(micro + 1):
        batch_index = jnp.clip(tick_id - section_id, 0, micro - 1)
        documents_now = lax.dynamic_index_in_dim(documents, batch_index, 0, keepdims=False)
        fresh_rows = inputs[tick_id] if tick_id < micro else empty_rows
        start_rows = jnp.where(section_id == 0, fresh_rows, received).astype(jnp.float32)
        result, kept_values = layer_forward(
            start_rows, params, documents_now, groups, step_count, seq_place
        )
        sent_rows = result.astype(jnp.bfloat16)
        produced.append(sent_rows)
        saved.append((kept_values, documents_now))
        if tick_id < micro:
            received = passed_along(sent_rows, "section", 1)
    back_received = empty_rows
    start_grads = []
    sent_grads = []
    totals = None
    shards = None
    for tick_id in range(micro + 1):
        earlier_save = saved[max(tick_id - 1, 0)]
        later_save = saved[min(tick_id + 1, micro)]
        kept_values, documents_now = jax.tree.map(
            lambda earlier, latter: jnp.where(section_id == 0, earlier, latter),
            earlier_save,
            later_save,
        )
        fresh_rows = cotangent[tick_id] if tick_id < micro else empty_rows
        incoming = jnp.where(section_id == 1, fresh_rows, back_received).astype(jnp.float32)
        start_grad, gradients = layer_backward(
            incoming, kept_values, params, documents_now, groups, step_count, seq_place
        )
        sent_rows = start_grad.astype(jnp.bfloat16)
        start_grads.append(start_grad)
        sent_grads.append(sent_rows.astype(jnp.float32))
        if tick_id < micro:
            back_received = passed_along(sent_rows, "section", -1)
        totals = (
            list(gradients)
            if totals is None
            else [earlier + latter for earlier, latter in zip(totals, gradients)]
        )
    shards = (
        lax.psum_scatter(totals[0], "seq", scatter_dimension=0, tiled=True),
        lax.psum_scatter(totals[1], "seq", scatter_dimension=0, tiled=True),
        lax.psum_scatter(totals[2], "seq", scatter_dimension=0, tiled=True),
        lax.psum_scatter(totals[3], "seq", scatter_dimension=0, tiled=True),
        lax.psum_scatter(totals[4], "seq", scatter_dimension=1, tiled=True),
        lax.psum_scatter(totals[5], "seq", scatter_dimension=1, tiled=True),
        lax.psum_scatter(totals[6], "seq", scatter_dimension=0, tiled=True),
    )
    layer_outputs = jnp.stack(
        [
            jnp.where(section_id == 0, produced[batch_id], produced[batch_id + 1])
            for batch_id in range(micro)
        ]
    )[None]
    input_grads = jnp.stack(
        [
            jnp.where(section_id == 0, start_grads[batch_id + 1], sent_grads[batch_id])
            for batch_id in range(micro)
        ]
    )[None]
    return (
        layer_outputs,
        input_grads,
        shards[0][None],
        shards[1][None],
        shards[2][None],
        shards[3][None],
        shards[4][None],
        shards[5][None],
        shards[6][None],
    )


HD = 48
AUG = 128
IDS = 32
SRC = 16
TOK = 256
ROOT = HD ** -0.5
C2 = ROOT * math.log2(math.e)
AWAY = -(2.0 ** 100)
BLOCKS = (16, 8, 4, 2, 1)
FIRST = (0, 16, 24, 28, 30)
F32, BF16 = jnp.float32, jnp.bfloat16

def nt(a, b):
    return lax.dot_general(a, b, (((1,), (1,)), ((), ())), preferred_element_type=F32)

def nn(a, b):
    return jnp.dot(a, b, preferred_element_type=F32)

def eye(n):
    return (lax.broadcasted_iota(jnp.int32, (n, n), 0) == lax.broadcasted_iota(jnp.int32, (n, n), 1)).astype(BF16)

def pack_grid(c):
    col = lax.broadcasted_iota(jnp.int32, (256, 128), 1)
    row = lax.broadcasted_iota(jnp.int32, (256, 128), 0)
    return (row == (col // c) * (2 * c) + col % c).astype(BF16)

def spread_grid(c):
    row = lax.broadcasted_iota(jnp.int32, (128, 256), 0)
    col = lax.broadcasted_iota(jnp.int32, (128, 256), 1)
    return (col == (row // c) * (2 * c) + row % c).astype(BF16)

def split3(v):
    hi = v.astype(BF16)
    r = v - hi.astype(F32)
    mid = r.astype(BF16)
    lo = (r - mid.astype(F32)).astype(BF16)
    return hi, mid, lo

def spread(v, grid):
    hi, mid, lo = split3(v)
    return nn(hi, grid) + nn(mid, grid) + nn(lo, grid)

def pack_levels(stack):
    for level in range(1, 5):
        c = TOK >> level
        def step(g, _, level=level, c=c):
            a = stack[FIRST[level - 1] + 2 * g]
            b = stack[FIRST[level - 1] + 2 * g + 1]
            if level == 1:
                pa, pb = a[:, :128], b[:, :128]
            else:
                grid = pack_grid(c)
                pa, pb = nn(a, grid).astype(BF16), nn(b, grid).astype(BF16)
            stack[FIRST[level] + g] = jnp.concatenate([pa, pb], axis=1)
            return 0
        lax.fori_loop(0, BLOCKS[level], step, 0)

def marks(doc_row, away):
    ids = lax.broadcasted_iota(jnp.int32, (IDS, TOK), 0).astype(F32)
    same = ids == doc_row
    return (jnp.where(same, 0.0, AWAY) if away else jnp.where(same, 1.0, 0.0)).astype(BF16)

def fwd_kernel(x_ref, docs_ref, o_ref, ob_ref, lse_ref, fm, ktm, part, *, kc):
    pad = jnp.zeros((AUG - HD - IDS, TOK), BF16)
    def load(s, _):
        x = x_ref[s]
        d = docs_ref[s]
        fm[s] = jnp.concatenate([x[0:HD], marks(d, False), pad, x[HD:2 * HD], marks(d, True), pad, x[2 * HD:]], axis=0)
        return 0
    lax.fori_loop(0, SRC, load, 0)
    pack_levels(fm)
    iden = eye(TOK)
    def turn(i, _):
        ktm[i] = nt(iden, fm[i, AUG:2 * AUG, :]).astype(BF16)
        return 0
    lax.fori_loop(0, 31, turn, 0)

    def block(i, kfirst, count):
        q = fm[i, 0:AUG, :]
        scores = []
        for t in range(count):
            scores.append(nn(ktm[kfirst + t], q))
        top = functools.reduce(jnp.maximum, [jnp.max(s, axis=0, keepdims=True) for s in scores])
        total = jnp.zeros((1, TOK), F32)
        out = jnp.zeros((HD, TOK), F32)
        for t in range(count):
            p = jnp.exp2((scores[t] - top) * C2)
            total = total + jnp.sum(p, axis=0, keepdims=True)
            out = out + nn(fm[kfirst + t, 2 * AUG:2 * AUG + HD, :], p.astype(BF16))
        part[i, 0:HD] = out
        part[i, HD:HD + 8] = jnp.broadcast_to(total, (8, TOK))
        part[i, HD + 8:HD + 16] = jnp.broadcast_to(top * C2, (8, TOK))
    def main(i, _):
        block(i, (i // 4) * 4, 4)
        return 0
    lax.fori_loop(0, 28, main, 0)
    block(28, 28, 2)
    block(29, 28, 2)
    block(30, 30, 1)

    for level in range(4, 0, -1):
        c = TOK >> level
        def join(g, _, level=level, c=c):
            child = FIRST[level] + g
            grid = spread_grid(c) if level > 1 else None
            for half in range(2):
                mine = FIRST[level - 1] + 2 * g + half
                got = part[child, :, half * 128:half * 128 + 128]
                if level > 1:
                    got = spread(got, grid)
                else:
                    got = jnp.concatenate([got, jnp.zeros_like(got)], axis=1)
                own = part[mine]
                cl, cm = got[HD:HD + 1], got[HD + 8:HD + 9]
                cm = jnp.where(cl > 0, cm, AWAY)
                ol, om = own[HD:HD + 1], own[HD + 8:HD + 9]
                top = jnp.maximum(cm, om)
                wc, wo = jnp.exp2(cm - top), jnp.exp2(om - top)
                part[mine, 0:HD] = got[0:HD] * wc + own[0:HD] * wo
                part[mine, HD:HD + 8] = jnp.broadcast_to(cl * wc + ol * wo, (8, TOK))
                part[mine, HD + 8:HD + 16] = jnp.broadcast_to(top, (8, TOK))
            return 0
        lax.fori_loop(0, BLOCKS[level], join, 0)
    def finish(s, _):
        own = part[s]
        l, m = own[HD:HD + 1], own[HD + 8:HD + 9]
        out = own[0:HD] / l
        o_ref[s] = out
        ob_ref[s] = out.astype(BF16)
        lse_ref[s] = m + jnp.log2(l)
        return 0
    lax.fori_loop(0, SRC, finish, 0)

def attn_fwd(x, docs):
    return pl.pallas_call(
        functools.partial(fwd_kernel, kc=256),
        out_shape=(jax.ShapeDtypeStruct((SRC, HD, TOK), F32), jax.ShapeDtypeStruct((SRC, HD, TOK), BF16), jax.ShapeDtypeStruct((SRC, 1, TOK), F32)),
        in_specs=[pl.BlockSpec(memory_space=pltpu.VMEM)] * 2,
        out_specs=[pl.BlockSpec(memory_space=pltpu.VMEM)] * 3,
        scratch_shapes=[
            pltpu.VMEM((31, 2 * AUG + HD, TOK), BF16),
            pltpu.VMEM((31, TOK, AUG), BF16),
            pltpu.VMEM((31, HD + 16, TOK), F32),
        ],
        compiler_params=pltpu.CompilerParams(vmem_limit_bytes=50 * 2**20),
        name="attend",
    )(x, docs)

def bwd_kernel(x_ref, g_ref, docs_ref, o_ref, lse_ref, e_ref, fm, tm, eq, ek, ev):
    pad = jnp.zeros((AUG - HD - IDS - 16, TOK), BF16)
    pad2 = jnp.zeros((AUG - HD - 16, TOK), BF16)
    row16 = lax.broadcasted_iota(jnp.int32, (16, TOK), 0)
    ones = jnp.where(row16 < 3, 1.0, 0.0).astype(BF16)
    def three(v):
        hi, mid, lo = split3(v)
        hi, mid, lo = hi.astype(F32), mid.astype(F32), lo.astype(F32)
        return jnp.where(row16 == 0, hi, jnp.where(row16 == 1, mid, jnp.where(row16 == 2, lo, 0.0))).astype(BF16)
    def load(s, _):
        x = x_ref[s]
        d = docs_ref[s]
        g = g_ref[s]
        dot = jnp.sum(g.astype(F32) * o_ref[s], axis=0, keepdims=True)
        low = three(lse_ref[s] * (-1.0 / C2))
        off = three(-dot)
        fm[s] = jnp.concatenate([
            x[0:HD], marks(d, False), low, pad,
            g, off, pad2,
            x[HD:2 * HD], marks(d, True), ones, pad,
            x[2 * HD:], ones, pad2], axis=0)
        return 0
    lax.fori_loop(0, SRC, load, 0)
    pack_levels(fm)
    iden = eye(TOK)
    def turn(i, _):
        tm[i] = nt(iden, fm[i]).astype(BF16)
        return 0
    lax.fori_loop(0, 31, turn, 0)
    def zero(i, _):
        ek[i] = jnp.zeros((TOK, AUG), F32)
        ev[i] = jnp.zeros((TOK, AUG), F32)
        return 0
    lax.fori_loop(0, 31, zero, 0)

    def block(i, kfirst, count):
        q = fm[i, 0:AUG, :]
        g = fm[i, AUG:2 * AUG, :]
        qt = tm[i, :, 0:AUG]
        gt = tm[i, :, AUG:2 * AUG]
        acc = jnp.zeros((HD, TOK), F32)
        for t in range(count):
            k = kfirst + t
            p = jnp.exp2(nn(tm[k, :, 2 * AUG:3 * AUG], q) * C2)
            es = (p * nn(tm[k, :, 3 * AUG:], g)).astype(BF16)
            ev[k] += nn(p.astype(BF16), gt)
            ek[k] += nn(es, qt)
            acc = acc + nn(fm[k, 2 * AUG:2 * AUG + HD, :], es)
        eq[i] = acc
    def main(i, _):
        block(i, (i // 4) * 4, 4)
        return 0
    lax.fori_loop(0, 28, main, 0)
    block(28, 28, 2)
    block(29, 28, 2)
    block(30, 30, 1)

    for level in range(4, 0, -1):
        c = TOK >> level
        def join(g, _, level=level, c=c):
            child = FIRST[level] + g
            grid = spread_grid(c) if level > 1 else None
            for half in range(2):
                mine = FIRST[level - 1] + 2 * g + half
                got = eq[child, :, half * 128:half * 128 + 128]
                if level > 1:
                    eq[mine] += spread(got, grid)
                else:
                    eq[mine, :, 0:128] += got
                for s in range(128 // c):
                    ek[mine, 2 * c * s:2 * c * s + c, :] += ek[child, half * 128 + c * s:half * 128 + c * s + c, :]
                    ev[mine, 2 * c * s:2 * c * s + c, :] += ev[child, half * 128 + c * s:half * 128 + c * s + c, :]
            return 0
        lax.fori_loop(0, BLOCKS[level], join, 0)
    small = (lax.broadcasted_iota(jnp.int32, (HD, AUG), 0) == lax.broadcasted_iota(jnp.int32, (HD, AUG), 1)).astype(BF16)
    def finish(s, _):
        a = (eq[s] * ROOT).astype(BF16)
        b = nt(small, (ek[s] * ROOT).astype(BF16)).astype(BF16)
        v = nt(small, ev[s].astype(BF16)).astype(BF16)
        e_ref[s] = jnp.concatenate([a, b, v], axis=0)
        return 0
    lax.fori_loop(0, SRC, finish, 0)

def attn_bwd(x, g, docs, o, lse):
    return pl.pallas_call(
        bwd_kernel,
        out_shape=jax.ShapeDtypeStruct((SRC, 3 * HD, TOK), BF16),
        in_specs=[pl.BlockSpec(memory_space=pltpu.VMEM)] * 5,
        out_specs=pl.BlockSpec(memory_space=pltpu.VMEM),
        scratch_shapes=[
            pltpu.VMEM((31, 4 * AUG, TOK), BF16),
            pltpu.VMEM((31, TOK, 4 * AUG), BF16),
            pltpu.VMEM((31, HD, TOK), F32),
            pltpu.VMEM((31, TOK, AUG), F32),
            pltpu.VMEM((31, TOK, AUG), F32),
        ],
        compiler_params=pltpu.CompilerParams(vmem_limit_bytes=56 * 2**20),
        name="attend_back",
    )(x, g, docs, o, lse)


def layer_norm(values, gain_row, shift_row):
    center = values - jnp.mean(values, axis=-1, keepdims=True)
    scale = lax.rsqrt(jnp.mean(center * center, axis=-1, keepdims=True) + epsilon)
    unit = center * scale
    return unit, scale, (unit * gain_row + shift_row).astype(BF16)


def layer_norm_back(grad, unit, scale, gain_row):
    pulled = grad * gain_row
    return (
        pulled
        - jnp.mean(pulled, axis=-1, keepdims=True)
        - unit * jnp.mean(pulled * unit, axis=-1, keepdims=True)
    ) * scale


def gelu_parts(values):
    share = 0.5 * (1.0 + lax.erf(values * math.sqrt(0.5)))
    slope = share + values * jnp.exp(-0.5 * values * values) * (1.0 / math.sqrt(2 * math.pi))
    return (values * share).astype(BF16), slope


def head_order():
    block = np.array([int(f"{k:04b}"[::-1], 2) for k in range(16)])
    heads = np.arange(HEADS)[:, None, None]
    residue = (heads + block[None, :, None]) % 16
    return (np.arange(16)[None, None, :] * 16 + residue).reshape(HEADS, TOK)


def cube_forward(hidden, params, order, docs, trade):
    w_qkv, w_out, w_up, w_down, gains, biases, up_bias = params
    unit_one, scale_one, normed = layer_norm(hidden, gains[0], biases[0])
    mixed = jnp.einsum("df,td->ft", w_qkv, normed, preferred_element_type=F32)
    shift = jnp.concatenate([biases[1], jnp.zeros_like(biases[1]), biases[2]])
    mixed = (mixed + shift[:, None]).astype(BF16)
    mixed = mixed.reshape(3, HEADS, HEAD_DIM, TOK).transpose(1, 0, 2, 3).reshape(HEADS, 3 * HEAD_DIM, TOK)
    mixed = jnp.einsum("hft,htu->hfu", mixed, order, preferred_element_type=F32).astype(BF16)
    heads = trade(mixed)
    merged, merged_low, summary = attn_fwd(heads, docs)
    attended = trade(merged_low)
    attended = jnp.einsum("hdu,htu->hdt", attended, order, preferred_element_type=F32).astype(BF16)
    attended = attended.reshape(D, TOK)
    middle = hidden + jnp.einsum("ft,fd->td", attended, w_out, preferred_element_type=F32) + biases[3]
    unit_two, scale_two, normed_two = layer_norm(middle, gains[1], biases[4])
    upward = jnp.dot(normed_two, w_up, preferred_element_type=F32) + up_bias
    activated, slope = gelu_parts(upward)
    result = middle + jnp.dot(activated, w_down, preferred_element_type=F32) + biases[5]
    kept = (unit_one, scale_one, normed, heads, merged, summary, attended, unit_two, scale_two, normed_two, slope, activated)
    return result.astype(BF16), kept


def cube_backward(incoming_low, kept, params, order, docs, trade):
    w_qkv, w_out, w_up, w_down, gains, biases, up_bias = params
    unit_one, scale_one, normed, heads, merged, summary, attended, unit_two, scale_two, normed_two, slope, activated = kept
    incoming = incoming_low.astype(F32)
    grad_down = inner_rows(activated, incoming_low)
    act_grad = jnp.einsum("tb,ab->ta", incoming_low, w_down, preferred_element_type=F32)
    up_grad = (act_grad * slope).astype(BF16)
    grad_up = inner_rows(normed_two, up_grad)
    norm_two_grad = jnp.einsum("tb,ab->ta", up_grad, w_up, preferred_element_type=F32)
    middle_grad = incoming + layer_norm_back(norm_two_grad, unit_two, scale_two, gains[1])
    branch_grad = middle_grad.astype(BF16)
    grad_out = jnp.einsum("ft,td->fd", attended, branch_grad, preferred_element_type=F32)
    merged_grad = jnp.einsum("fd,td->ft", w_out, branch_grad, preferred_element_type=F32).astype(BF16)
    merged_grad = merged_grad.reshape(HEADS, HEAD_DIM, TOK)
    merged_grad = jnp.einsum("hdt,htu->hdu", merged_grad, order, preferred_element_type=F32).astype(BF16)
    back_heads = attn_bwd(heads, trade(merged_grad), docs, merged, summary)
    mixed_grad = trade(back_heads)
    mixed_grad = jnp.einsum("hfu,htu->hft", mixed_grad, order, preferred_element_type=F32).astype(BF16)
    mixed_grad = mixed_grad.reshape(HEADS, 3, HEAD_DIM, TOK).transpose(1, 0, 2, 3).reshape(3 * D, TOK)
    grad_qkv = jnp.einsum("td,ft->df", normed, mixed_grad, preferred_element_type=F32)
    grad_shift = jnp.sum(mixed_grad.astype(F32), axis=1)
    normed_grad = jnp.einsum("ft,df->td", mixed_grad, w_qkv, preferred_element_type=F32)
    start_grad = middle_grad + layer_norm_back(normed_grad, unit_one, scale_one, gains[0])
    small = jnp.stack([
        jnp.sum(normed_grad * unit_one, axis=0),
        jnp.sum(norm_two_grad * unit_two, axis=0),
        jnp.sum(normed_grad, axis=0),
        grad_shift[:D],
        grad_shift[2 * D:],
        jnp.sum(branch_grad.astype(F32), axis=0),
        jnp.sum(norm_two_grad, axis=0),
        jnp.sum(incoming, axis=0),
    ])
    grad_up_bias = jnp.sum(up_grad.astype(F32), axis=0)
    return start_grad, (grad_qkv, grad_out, grad_up, grad_down, small, grad_up_bias)


def cube_body(inputs, cotangent, documents, w_qkv, w_out, w_up, w_down, norm_gains, biases, up_bias):
    section_id = lax.axis_index("section")
    place = lax.axis_index("seq")
    count = lax.axis_size("seq")
    half = count // 2
    micro_id = place // half
    member = section_id * half + place % half
    teams = [[s * count + k * half + j for s in range(2) for j in range(half)] for k in range(2)]
    axes = ("section", "seq")

    def trade(value):
        return lax.all_to_all(value, axes, 0, 0, axis_index_groups=teams, tiled=True)

    def across(value, pairs):
        return lax.ppermute(value, axes, pairs)

    def own_rows(pair):
        mine = jnp.where(micro_id == 0, pair[0], pair[1])
        other = jnp.where(micro_id == 0, pair[1], pair[0])
        swap = across(other, [(count + j, count + (j ^ half)) for j in range(count)])
        return jnp.where(section_id == 0, mine, swap)

    table = jnp.asarray(head_order())
    order = (table[:, None, :] == jnp.arange(TOK)[None, :, None]).astype(BF16)
    docs = jnp.where(micro_id == 0, documents[0], documents[1]).reshape(count, TOK)
    docs = jnp.where(micro_id == 0, docs, jnp.roll(docs, half, axis=0))
    own_order = lax.dynamic_index_in_dim(order, member, 0, keepdims=False)
    docs = jnp.dot(docs.astype(BF16), own_order, preferred_element_type=F32).reshape(count, 1, TOK)

    def whole(shard):
        got = lax.all_gather(shard.astype(BF16), axes, axis=0, tiled=True)
        return got.reshape((2, got.shape[0] // 2) + got.shape[1:])

    hidden = own_rows(inputs)
    small = jnp.concatenate([norm_gains[0], biases[0]]).astype(BF16)
    small = jnp.concatenate([small.reshape(-1), up_bias[0].astype(BF16)])
    small = lax.all_gather(small, axes, axis=0).astype(F32).reshape(2, count, -1)
    wide = D // count
    rows = small[:, :, : 8 * wide].reshape(2, count, 8, wide).transpose(0, 2, 1, 3).reshape(2, 8, D)
    lifts = small[:, :, 8 * wide:].reshape(2, -1)
    weights = [whole(w[0]) for w in (w_qkv, w_out, w_up, w_down)]
    params = [tuple(w[l] for w in weights) + (rows[l, :2], rows[l, 2:], lifts[l]) for l in range(2)]

    first, kept_first = cube_forward(hidden.astype(F32), params[0], order, docs, trade)
    final, kept_final = cube_forward(first.astype(F32), params[1], order, docs, trade)
    grad_final, terms_final = cube_backward(own_rows(cotangent), kept_final, params[1], order, docs, trade)
    sent = grad_final.astype(BF16)
    grad_first, terms_first = cube_backward(sent, kept_first, params[0], order, docs, trade)

    def shared_out(value_first, value_final):
        far = across(value_first, [(count + j, j ^ half) for j in range(count)])
        near = across(value_final, [(j, count + j) for j in range(count)])
        beside = across(value_final, [(count + j, count + (j ^ half)) for j in range(count)])
        return jnp.where(section_id == 0, far, beside), near

    def placed(mine, other):
        return jnp.where(micro_id == 0, jnp.stack([mine, other]), jnp.stack([other, mine]))[None]

    other, near = shared_out(first, final)
    layer_outputs = placed(jnp.where(section_id == 0, first, near), other)
    other, near = shared_out(grad_first.astype(BF16), sent)
    input_grads = placed(jnp.where(section_id == 0, grad_first, near.astype(F32)), other.astype(F32))

    def summed(first_term, final_term, axis):
        parts = [
            lax.psum_scatter(t, "seq", scatter_dimension=axis, tiled=True)
            for t in (first_term, final_term)
        ]
        away = jnp.where(section_id == 0, parts[1], parts[0])
        mine = jnp.where(section_id == 0, parts[0], parts[1])
        return (mine.astype(F32) + lax.ppermute(away, "section", [(0, 1), (1, 0)]).astype(F32))[None]

    grads = [summed(a.astype(BF16), b.astype(BF16), 0) for a, b in zip(terms_first[:4], terms_final[:4])]
    small = summed(terms_first[4], terms_final[4], 1)
    lift = summed(terms_first[5], terms_final[5], 0)
    return (layer_outputs, input_grads, *grads, small[:, :2], small[:, 2:], lift)


def solution(mesh):
    cube = mesh.shape["seq"] == 16
    return jax.shard_map(
        cube_body if cube else body,
        mesh=mesh,
        in_specs=(
            P(None, "seq", None),
            P(None, "seq", None),
            P(),
            P("section", "seq", None),
            P("section", "seq", None),
            P("section", "seq", None),
            P("section", "seq", None),
            P("section", None, "seq"),
            P("section", None, "seq"),
            P("section", "seq"),
        ),
        out_specs=(
            P("section", None, "seq", None),
            P("section", None, "seq", None),
            P("section", "seq", None),
            P("section", "seq", None),
            P("section", "seq", None),
            P("section", "seq", None),
            P("section", None, "seq"),
            P("section", None, "seq"),
            P("section", "seq"),
        ),
        check_vma=False,
    )
```

```python
import functools
import math

import jax
import jax.numpy as jnp
import numpy as np
from jax import lax
from jax.experimental import pallas as pl
from jax.experimental.pallas import tpu as pltpu
from jax.sharding import PartitionSpec as P

D = 768
HEADS = 16
HEAD_DIM = 48
SEG0 = 1024
BRANCHES = 5


epsilon = 1e-05
masked_score = -1e30
highest = lax.Precision.HIGHEST


def swapped(value, axis, apart):
    mask = 2**apart
    pairs = [(source, source ^ mask) for source in range(lax.axis_size(axis))]
    return lax.ppermute(value, axis, pairs)


def for_sending(array):
    return jax.tree.map(lambda a: a.astype(jnp.bfloat16) if a.dtype == jnp.float32 else a, array)


def passed_along(array, axis, by):
    peers = lax.axis_size(axis)
    pairs = [(i, i + by) for i in range(peers) if 0 <= i + by < peers]
    return lax.ppermute(array, axis, pairs)


def layer_norm_parts(values, gain_row, shift_row):
    center = values - jnp.mean(values, axis=-1, keepdims=True)
    spread = jnp.mean(center * center, axis=-1, keepdims=True)
    return center * lax.rsqrt(spread + epsilon) * gain_row + shift_row


def exact_gelu(values):
    return jax.nn.gelu(values, approximate=False)


def inner_rows(left, right):
    return jnp.einsum("ta,tb->ab", left, right, preferred_element_type=jnp.float32)


def geometry(tokens_dev, devices):
    groups = [
        min(SEG0 * 2**level_id, tokens_dev * devices) // tokens_dev for level_id in range(BRANCHES)
    ]
    return (groups, max(groups).bit_length() - 1)


def first_level(groups, step_id):
    return min((level_id for level_id in range(BRANCHES) if groups[level_id] > 2**step_id))


def pick_grid(level_id, dtype):
    dilation = 2**level_id
    return (jnp.arange(dilation)[:, None] == (jnp.arange(HEADS) % dilation)[None, :]).astype(dtype)


def select_rows(tensor, level_id):
    dilation = 2**level_id
    shaped = tensor.reshape((tensor.shape[0] // dilation, dilation) + tensor.shape[1:])
    if tensor.dtype == jnp.bfloat16:
        chosen = jnp.einsum(
            "jrh...,rh->jh...",
            shaped,
            pick_grid(level_id, jnp.bfloat16),
            preferred_element_type=jnp.float32,
        )
        return chosen.astype(jnp.bfloat16)
    return jnp.einsum(
        "jrh...,rh->jh...", shaped, pick_grid(level_id, jnp.float32), precision=highest
    )


def spread_rows(tensor, level_id):
    dilation = 2**level_id
    spread = jnp.einsum(
        "jh...,rh->jrh...", tensor, pick_grid(level_id, jnp.float32), precision=highest
    )
    return spread.reshape((tensor.shape[0] * dilation,) + tensor.shape[1:])


def spread_sums(tensor, level_id):
    dilation = 2**level_id
    grid = pick_grid(level_id, jnp.float32)
    spread = jnp.where(grid[None] > 0, tensor[:, None, :], masked_score)
    return spread.reshape(tensor.shape[0] * dilation, HEADS)


def doc_tables(documents_now, level_id, group, tokens_dev, seq_place):
    dilation = 2**level_id
    offsets = np.arange(HEADS) % dilation
    own_docs = lax.dynamic_slice_in_dim(documents_now, seq_place * tokens_dev, tokens_dev)
    own_docs = own_docs.reshape(tokens_dev // dilation, dilation)[:, offsets]
    seg_start = seq_place // group * group * tokens_dev
    seg_docs = lax.dynamic_slice_in_dim(documents_now, seg_start, group * tokens_dev)
    seg_docs = seg_docs.reshape(group * tokens_dev // dilation, dilation)[:, offsets]
    return (own_docs, seg_docs)


def head_bits(level_id):
    return jnp.arange(HEADS) >> level_id & 1


def halve(buffer, level_id):
    pairs = buffer.reshape(buffer.shape[0], buffer.shape[1] // 2, 2, HEADS, HEAD_DIM)
    chosen = head_bits(level_id)[None, None, :, None] == 1
    return jnp.where(chosen, pairs[:, :, 1], pairs[:, :, 0])


def widen(buffer, level_id):
    chosen = head_bits(level_id)[None, None, :, None] == 1
    empty = jnp.zeros_like(buffer)
    upper_part = jnp.where(chosen, buffer, empty)
    lower_part = jnp.where(chosen, empty, buffer)
    stacked = jnp.stack([lower_part, upper_part], axis=2)
    return stacked.reshape(buffer.shape[0], buffer.shape[1] * 2, HEADS, HEAD_DIM)


def thin_to(buffer, low_level, high_level):
    for level_id in range(low_level, high_level):
        buffer = halve(buffer, level_id)
    return buffer


def widen_to(buffer, low_level, high_level):
    for level_id in reversed(range(low_level, high_level)):
        buffer = widen(buffer, level_id)
    return buffer


def gather_keys(own_rows, groups, step_count, seq_place):
    results = [None] * BRANCHES
    current = own_rows
    level_now = 0
    for level_id in range(BRANCHES):
        pass
    for step_id in range(step_count):
        target = first_level(groups, step_id)
        current = thin_to(current, level_now, target)
        level_now = target
        row_count = current.shape[1]
        flat_rows = current.reshape(2, row_count, HEADS * HEAD_DIM)
        incoming = swapped(flat_rows, "seq", step_id).reshape(current.shape)
        upper_half = seq_place >> step_id & 1 == 1
        current = jnp.where(
            upper_half,
            jnp.concatenate([incoming, current], axis=1),
            jnp.concatenate([current, incoming], axis=1),
        )
        for level_id in range(BRANCHES):
            if groups[level_id] == 2 ** (step_id + 1):
                results[level_id] = thin_to(current, level_now, level_id)
    return results


def scatter_keys(key_grads, groups, step_count, seq_place):
    carried = None
    for step_id in reversed(range(step_count)):
        level_now = first_level(groups, step_id)
        total_grad = None
        if carried is not None:
            total_grad = widen_to(carried, level_now, first_level(groups, step_id + 1))
        for level_id in range(BRANCHES):
            if groups[level_id] == 2 ** (step_id + 1):
                branch_term = widen_to(key_grads[level_id], level_now, level_id)
                total_grad = branch_term if total_grad is None else total_grad + branch_term
        half_rows = total_grad.shape[1] // 2
        upper_half = seq_place >> step_id & 1 == 1
        own_half = jnp.where(upper_half, total_grad[:, half_rows:], total_grad[:, :half_rows])
        theirs = jnp.where(upper_half, total_grad[:, :half_rows], total_grad[:, half_rows:])
        flat_rows = theirs.reshape(2, half_rows, HEADS * HEAD_DIM)
        incoming = (
            swapped(for_sending(flat_rows), "seq", step_id)
            .astype(flat_rows.dtype)
            .reshape(own_half.shape)
        )
        carried = own_half + incoming
    own_grad = widen_to(carried, 0, first_level(groups, 0))
    for level_id in range(BRANCHES):
        pass
    return own_grad


def head_blocks(level_id):
    block_size = min(HEADS, 4 * 2**level_id)
    return (HEADS // block_size, block_size)


def to_blocks(tensor, block_count, block_size):
    moved = jnp.moveaxis(tensor, 1, 0)
    return moved.reshape((block_count, block_size) + moved.shape[1:])


def from_blocks(tensor):
    joined = tensor.reshape((tensor.shape[0] * tensor.shape[1],) + tensor.shape[2:])
    return jnp.moveaxis(joined, 0, 1)


def score_block(query_block, key_block, query_doc, key_doc):
    scores = jnp.einsum(
        "hqd,hkd->hqk", query_block, key_block, preferred_element_type=jnp.float32
    ) * HEAD_DIM ** (-0.5)
    return jnp.where(query_doc[:, :, None] == key_doc[:, None, :], scores, masked_score)


def forward_block(pieces):
    query_block, key_block, value_block, query_doc, key_doc = pieces
    scores = score_block(query_block, key_block, query_doc, key_doc)
    row_max = jnp.max(scores, axis=-1, keepdims=True)
    weights = jnp.exp(scores - row_max)
    row_total = jnp.sum(weights, axis=-1, keepdims=True)
    prob_rows = (weights / row_total).astype(jnp.bfloat16)
    result = jnp.einsum("hqk,hkd->hqd", prob_rows, value_block, preferred_element_type=jnp.float32)
    return (result, (row_max + jnp.log(row_total))[:, :, 0])


def backward_block(pieces):
    query_block, key_block, value_block, query_doc, key_doc, summary, out_grad, summary_grad = (
        pieces
    )
    scores = score_block(query_block, key_block, query_doc, key_doc)
    prob_rows = jnp.exp(scores - summary[:, :, None])
    prob_grad = jnp.einsum(
        "hqd,hkd->hqk", out_grad, value_block, preferred_element_type=jnp.float32
    )
    score_grad = prob_rows * (
        prob_grad
        - jnp.sum(prob_rows * prob_grad, axis=-1, keepdims=True)
        + summary_grad[:, :, None]
    )
    score_grad = score_grad.astype(jnp.bfloat16)
    score_scale = HEAD_DIM ** (-0.5)
    query_grad = (
        jnp.einsum("hqk,hkd->hqd", score_grad, key_block, preferred_element_type=jnp.float32)
        * score_scale
    )
    key_grad = (
        jnp.einsum("hqk,hqd->hkd", score_grad, query_block, preferred_element_type=jnp.float32)
        * score_scale
    )
    value_grad = jnp.einsum(
        "hqk,hqd->hkd", prob_rows.astype(jnp.bfloat16), out_grad, preferred_element_type=jnp.float32
    )
    return (query_grad, key_grad, value_grad)


def branch_forward(query_sel, key_value, query_docs, key_docs, level_id):
    block_count, block_size = head_blocks(level_id)
    pieces = (
        to_blocks(query_sel, block_count, block_size),
        to_blocks(key_value[0], block_count, block_size),
        to_blocks(key_value[1], block_count, block_size),
        to_blocks(query_docs, block_count, block_size),
        to_blocks(key_docs, block_count, block_size),
    )
    results, summaries = lax.map(forward_block, pieces)
    return (from_blocks(results), from_blocks(summaries))


def branch_backward(
    query_sel, key_value, query_docs, key_docs, summary, out_grad, summary_grad, level_id
):
    block_count, block_size = head_blocks(level_id)
    pieces = (
        to_blocks(query_sel, block_count, block_size),
        to_blocks(key_value[0], block_count, block_size),
        to_blocks(key_value[1], block_count, block_size),
        to_blocks(query_docs, block_count, block_size),
        to_blocks(key_docs, block_count, block_size),
        to_blocks(summary, block_count, block_size),
        to_blocks(out_grad, block_count, block_size),
        to_blocks(summary_grad, block_count, block_size),
    )
    query_grad, key_grad, value_grad = lax.map(backward_block, pieces)
    return (from_blocks(query_grad), jnp.stack([from_blocks(key_grad), from_blocks(value_grad)]))


def layer_forward(hidden, params, documents_now, groups, step_count, seq_place):
    w_qkv, w_out, w_up, w_down, gains, biases, up_bias = params
    gains = gains.astype(jnp.float32)
    biases = biases.astype(jnp.float32)
    tokens_dev = hidden.shape[0]
    normed = layer_norm_parts(hidden, gains[0], biases[0]).astype(jnp.bfloat16)
    mixed_rows = jnp.dot(normed, w_qkv, preferred_element_type=jnp.float32)
    queries = (mixed_rows[:, :D] + biases[1]).astype(jnp.bfloat16)
    key_part = mixed_rows[:, D : 2 * D].astype(jnp.bfloat16)
    values = (mixed_rows[:, 2 * D :] + biases[2]).astype(jnp.bfloat16)
    own_rows = jnp.stack([key_part, values]).reshape(2, tokens_dev, HEADS, HEAD_DIM)
    gathered = gather_keys(own_rows, groups, step_count, seq_place)
    query_heads = queries.reshape(tokens_dev, HEADS, HEAD_DIM)
    picked, branch_outs, branch_sums = ([], [], [])
    for level_id in range(BRANCHES):
        query_sel = select_rows(query_heads, level_id)
        query_docs, key_docs = doc_tables(
            documents_now, level_id, groups[level_id], tokens_dev, seq_place
        )
        result, summary = branch_forward(
            query_sel, gathered[level_id], query_docs, key_docs, level_id
        )
        picked.append(query_sel)
        branch_outs.append(result)
        branch_sums.append(summary)
    full_sums = jnp.stack(
        [spread_sums(branch_sums[level_id], level_id) for level_id in range(BRANCHES)]
    )
    row_max = jnp.max(full_sums, axis=0)
    shares = jnp.exp(full_sums - row_max)
    shares = shares / jnp.sum(shares, axis=0)
    merged = sum(
        (
            shares[level_id][:, :, None] * spread_rows(branch_outs[level_id], level_id)
            for level_id in range(BRANCHES)
        )
    )
    attended = merged.reshape(tokens_dev, D).astype(jnp.bfloat16)
    middle = hidden + jnp.dot(attended, w_out, preferred_element_type=jnp.float32) + biases[3]
    normed_two = layer_norm_parts(middle, gains[1], biases[4]).astype(jnp.bfloat16)
    upward = jnp.dot(normed_two, w_up, preferred_element_type=jnp.float32) + up_bias.astype(
        jnp.float32
    )
    activated = exact_gelu(upward).astype(jnp.bfloat16)
    result = middle + jnp.dot(activated, w_down, preferred_element_type=jnp.float32) + biases[5]
    kept_values = (
        hidden,
        normed,
        picked,
        gathered,
        branch_sums,
        branch_outs,
        shares,
        merged,
        attended,
        middle,
        normed_two,
        upward,
        activated,
    )
    return (result, kept_values)


def layer_backward(incoming, kept_values, params, documents_now, groups, step_count, seq_place):
    w_qkv, w_out, w_up, w_down, gains, biases, up_bias = params
    gains = gains.astype(jnp.float32)
    biases = biases.astype(jnp.float32)
    (
        hidden,
        normed,
        picked,
        gathered,
        branch_sums,
        branch_outs,
        shares,
        merged,
        attended,
        middle,
        normed_two,
        upward,
        activated,
    ) = kept_values
    tokens_dev = hidden.shape[0]
    down_grad = incoming.astype(jnp.bfloat16)
    grad_down = inner_rows(activated, down_grad)
    grad_bias_down = jnp.sum(down_grad.astype(jnp.float32), axis=0)
    act_grad = jnp.einsum("tb,ab->ta", down_grad, w_down, preferred_element_type=jnp.float32)
    gelu_pulled = jax.vjp(exact_gelu, upward)
    up_grad = gelu_pulled[1](act_grad)[0].astype(jnp.bfloat16)
    grad_up = inner_rows(normed_two, up_grad)
    grad_up_bias = jnp.sum(up_grad.astype(jnp.float32), axis=0)
    norm_two_grad = jnp.einsum("tb,ab->ta", up_grad, w_up, preferred_element_type=jnp.float32)
    norm_pulled = jax.vjp(layer_norm_parts, middle, gains[1], biases[4])
    middle_part, grad_gain_two, grad_shift_two = norm_pulled[1](norm_two_grad)
    middle_grad = incoming + middle_part
    branch_grad = middle_grad.astype(jnp.bfloat16)
    grad_out = inner_rows(attended, branch_grad)
    grad_bias_out = jnp.sum(branch_grad.astype(jnp.float32), axis=0)
    merged_grad = jnp.einsum("tb,ab->ta", branch_grad, w_out, preferred_element_type=jnp.float32)
    merged_grad = merged_grad.reshape(tokens_dev, HEADS, HEAD_DIM)
    query_grad = jnp.zeros((tokens_dev, HEADS, HEAD_DIM), jnp.float32)
    key_grads = []
    for level_id in range(BRANCHES):
        share_sel = select_rows(shares[level_id], level_id)
        merged_sel = select_rows(merged, level_id)
        grad_sel = select_rows(merged_grad, level_id)
        out_grad = (share_sel[:, :, None] * grad_sel).astype(jnp.bfloat16)
        summary_grad = share_sel * (
            jnp.sum(grad_sel * branch_outs[level_id], axis=-1)
            - jnp.sum(grad_sel * merged_sel, axis=-1)
        )
        query_docs, key_docs = doc_tables(
            documents_now, level_id, groups[level_id], tokens_dev, seq_place
        )
        query_part, key_value_grad = branch_backward(
            picked[level_id],
            gathered[level_id],
            query_docs,
            key_docs,
            branch_sums[level_id],
            out_grad,
            summary_grad,
            level_id,
        )
        query_grad = query_grad + spread_rows(query_part, level_id)
        key_grads.append(key_value_grad)
    own_grad = scatter_keys(key_grads, groups, step_count, seq_place)
    mixed_grad = jnp.concatenate(
        [
            query_grad.reshape(tokens_dev, D),
            own_grad[0].reshape(tokens_dev, D),
            own_grad[1].reshape(tokens_dev, D),
        ],
        axis=1,
    ).astype(jnp.bfloat16)
    grad_qkv = inner_rows(normed, mixed_grad)
    grad_bias_query = jnp.sum(mixed_grad[:, :D].astype(jnp.float32), axis=0)
    grad_bias_value = jnp.sum(mixed_grad[:, 2 * D :].astype(jnp.float32), axis=0)
    normed_grad = jnp.einsum("tb,ab->ta", mixed_grad, w_qkv, preferred_element_type=jnp.float32)
    norm_pulled = jax.vjp(layer_norm_parts, hidden, gains[0], biases[0])
    hidden_part, grad_gain_one, grad_shift_one = norm_pulled[1](normed_grad)
    start_grad = middle_grad + hidden_part
    gradients = (
        grad_qkv,
        grad_out,
        grad_up,
        grad_down,
        jnp.stack([grad_gain_one, grad_gain_two]),
        jnp.stack(
            [
                grad_shift_one,
                grad_bias_query,
                grad_bias_value,
                grad_bias_out,
                grad_shift_two,
                grad_bias_down,
            ]
        ),
        grad_up_bias,
    )
    return (start_grad, gradients)


def body(inputs, cotangent, documents, w_qkv, w_out, w_up, w_down, norm_gains, biases, up_bias):
    section_id = lax.axis_index("section")
    seq_place = lax.axis_index("seq")
    devices = lax.axis_size("seq")
    micro = inputs.shape[0]
    tokens_dev = inputs.shape[1]
    groups, step_count = geometry(tokens_dev, devices)
    params = (
        lax.all_gather(w_qkv[0].astype(jnp.bfloat16), "seq", axis=0, tiled=True),
        lax.all_gather(w_out[0].astype(jnp.bfloat16), "seq", axis=0, tiled=True),
        lax.all_gather(w_up[0].astype(jnp.bfloat16), "seq", axis=0, tiled=True),
        lax.all_gather(w_down[0].astype(jnp.bfloat16), "seq", axis=0, tiled=True),
        lax.all_gather(norm_gains[0].astype(jnp.bfloat16), "seq", axis=1, tiled=True),
        lax.all_gather(biases[0].astype(jnp.bfloat16), "seq", axis=1, tiled=True),
        lax.all_gather(up_bias[0].astype(jnp.bfloat16), "seq", axis=0, tiled=True),
    )
    empty_rows = jnp.zeros((tokens_dev, D), jnp.bfloat16)
    received = empty_rows
    saved = []
    produced = []
    for tick_id in range(micro + 1):
        batch_index = jnp.clip(tick_id - section_id, 0, micro - 1)
        documents_now = lax.dynamic_index_in_dim(documents, batch_index, 0, keepdims=False)
        fresh_rows = inputs[tick_id] if tick_id < micro else empty_rows
        start_rows = jnp.where(section_id == 0, fresh_rows, received).astype(jnp.float32)
        result, kept_values = layer_forward(
            start_rows, params, documents_now, groups, step_count, seq_place
        )
        sent_rows = result.astype(jnp.bfloat16)
        produced.append(sent_rows)
        saved.append((kept_values, documents_now))
        if tick_id < micro:
            received = passed_along(sent_rows, "section", 1)
    back_received = empty_rows
    start_grads = []
    sent_grads = []
    totals = None
    shards = None
    for tick_id in range(micro + 1):
        earlier_save = saved[max(tick_id - 1, 0)]
        later_save = saved[min(tick_id + 1, micro)]
        kept_values, documents_now = jax.tree.map(
            lambda earlier, latter: jnp.where(section_id == 0, earlier, latter),
            earlier_save,
            later_save,
        )
        fresh_rows = cotangent[tick_id] if tick_id < micro else empty_rows
        incoming = jnp.where(section_id == 1, fresh_rows, back_received).astype(jnp.float32)
        start_grad, gradients = layer_backward(
            incoming, kept_values, params, documents_now, groups, step_count, seq_place
        )
        sent_rows = start_grad.astype(jnp.bfloat16)
        start_grads.append(start_grad)
        sent_grads.append(sent_rows.astype(jnp.float32))
        if tick_id < micro:
            back_received = passed_along(sent_rows, "section", -1)
        totals = (
            list(gradients)
            if totals is None
            else [earlier + latter for earlier, latter in zip(totals, gradients)]
        )
    shards = (
        lax.psum_scatter(totals[0], "seq", scatter_dimension=0, tiled=True),
        lax.psum_scatter(totals[1], "seq", scatter_dimension=0, tiled=True),
        lax.psum_scatter(totals[2], "seq", scatter_dimension=0, tiled=True),
        lax.psum_scatter(totals[3], "seq", scatter_dimension=0, tiled=True),
        lax.psum_scatter(totals[4], "seq", scatter_dimension=1, tiled=True),
        lax.psum_scatter(totals[5], "seq", scatter_dimension=1, tiled=True),
        lax.psum_scatter(totals[6], "seq", scatter_dimension=0, tiled=True),
    )
    layer_outputs = jnp.stack(
        [
            jnp.where(section_id == 0, produced[batch_id], produced[batch_id + 1])
            for batch_id in range(micro)
        ]
    )[None]
    input_grads = jnp.stack(
        [
            jnp.where(section_id == 0, start_grads[batch_id + 1], sent_grads[batch_id])
            for batch_id in range(micro)
        ]
    )[None]
    return (
        layer_outputs,
        input_grads,
        shards[0][None],
        shards[1][None],
        shards[2][None],
        shards[3][None],
        shards[4][None],
        shards[5][None],
        shards[6][None],
    )


HD = 48
AUG = 128
IDS = 32
SRC = 16
TOK = 256
ROOT = HD ** -0.5
C2 = ROOT * math.log2(math.e)
AWAY = -(2.0 ** 100)
BLOCKS = (16, 8, 4, 2, 1)
FIRST = (0, 16, 24, 28, 30)
F32, BF16 = jnp.float32, jnp.bfloat16

def nt(a, b):
    return lax.dot_general(a, b, (((1,), (1,)), ((), ())), preferred_element_type=F32)

def nn(a, b):
    return jnp.dot(a, b, preferred_element_type=F32)

def eye(n):
    return (lax.broadcasted_iota(jnp.int32, (n, n), 0) == lax.broadcasted_iota(jnp.int32, (n, n), 1)).astype(BF16)

def pack_grid(c):
    col = lax.broadcasted_iota(jnp.int32, (256, 128), 1)
    row = lax.broadcasted_iota(jnp.int32, (256, 128), 0)
    return (row == (col // c) * (2 * c) + col % c).astype(BF16)

def spread_grid(c):
    row = lax.broadcasted_iota(jnp.int32, (128, 256), 0)
    col = lax.broadcasted_iota(jnp.int32, (128, 256), 1)
    return (col == (row // c) * (2 * c) + row % c).astype(BF16)

def split3(v):
    hi = v.astype(BF16)
    r = v - hi.astype(F32)
    mid = r.astype(BF16)
    lo = (r - mid.astype(F32)).astype(BF16)
    return hi, mid, lo

def spread(v, grid):
    hi, mid, lo = split3(v)
    return nn(hi, grid) + nn(mid, grid) + nn(lo, grid)

def pack_levels(stack):
    for level in range(1, 5):
        c = TOK >> level
        def step(g, _, level=level, c=c):
            a = stack[FIRST[level - 1] + 2 * g]
            b = stack[FIRST[level - 1] + 2 * g + 1]
            if level == 1:
                pa, pb = a[:, :128], b[:, :128]
            else:
                grid = pack_grid(c)
                pa, pb = nn(a, grid).astype(BF16), nn(b, grid).astype(BF16)
            stack[FIRST[level] + g] = jnp.concatenate([pa, pb], axis=1)
            return 0
        lax.fori_loop(0, BLOCKS[level], step, 0)

def marks(doc_row, away):
    ids = lax.broadcasted_iota(jnp.int32, (IDS, TOK), 0).astype(F32)
    same = ids == doc_row
    return (jnp.where(same, 0.0, AWAY) if away else jnp.where(same, 1.0, 0.0)).astype(BF16)

def fwd_kernel(x_ref, docs_ref, o_ref, ob_ref, lse_ref, fm, ktm, part, *, kc):
    pad = jnp.zeros((AUG - HD - IDS, TOK), BF16)
    def load(s, _):
        x = x_ref[s]
        d = docs_ref[s]
        fm[s] = jnp.concatenate([x[0:HD], marks(d, False), pad, x[HD:2 * HD], marks(d, True), pad, x[2 * HD:]], axis=0)
        return 0
    lax.fori_loop(0, SRC, load, 0)
    pack_levels(fm)
    iden = eye(TOK)
    def turn(i, _):
        ktm[i] = nt(iden, fm[i, AUG:2 * AUG, :]).astype(BF16)
        return 0
    lax.fori_loop(0, 31, turn, 0)

    def block(i, kfirst, count):
        q = fm[i, 0:AUG, :]
        scores = []
        for t in range(count):
            scores.append(nn(ktm[kfirst + t], q))
        top = functools.reduce(jnp.maximum, [jnp.max(s, axis=0, keepdims=True) for s in scores])
        total = jnp.zeros((1, TOK), F32)
        out = jnp.zeros((HD, TOK), F32)
        for t in range(count):
            p = jnp.exp2((scores[t] - top) * C2)
            total = total + jnp.sum(p, axis=0, keepdims=True)
            out = out + nn(fm[kfirst + t, 2 * AUG:2 * AUG + HD, :], p.astype(BF16))
        part[i, 0:HD] = out
        part[i, HD:HD + 8] = jnp.broadcast_to(total, (8, TOK))
        part[i, HD + 8:HD + 16] = jnp.broadcast_to(top * C2, (8, TOK))
    def main(i, _):
        block(i, (i // 4) * 4, 4)
        return 0
    lax.fori_loop(0, 28, main, 0)
    block(28, 28, 2)
    block(29, 28, 2)
    block(30, 30, 1)

    for level in range(4, 0, -1):
        c = TOK >> level
        def join(g, _, level=level, c=c):
            child = FIRST[level] + g
            grid = spread_grid(c) if level > 1 else None
            for half in range(2):
                mine = FIRST[level - 1] + 2 * g + half
                got = part[child, :, half * 128:half * 128 + 128]
                if level > 1:
                    got = spread(got, grid)
                else:
                    got = jnp.concatenate([got, jnp.zeros_like(got)], axis=1)
                own = part[mine]
                cl, cm = got[HD:HD + 1], got[HD + 8:HD + 9]
                cm = jnp.where(cl > 0, cm, AWAY)
                ol, om = own[HD:HD + 1], own[HD + 8:HD + 9]
                top = jnp.maximum(cm, om)
                wc, wo = jnp.exp2(cm - top), jnp.exp2(om - top)
                part[mine, 0:HD] = got[0:HD] * wc + own[0:HD] * wo
                part[mine, HD:HD + 8] = jnp.broadcast_to(cl * wc + ol * wo, (8, TOK))
                part[mine, HD + 8:HD + 16] = jnp.broadcast_to(top, (8, TOK))
            return 0
        lax.fori_loop(0, BLOCKS[level], join, 0)
    def finish(s, _):
        own = part[s]
        l, m = own[HD:HD + 1], own[HD + 8:HD + 9]
        out = own[0:HD] / l
        o_ref[s] = out
        ob_ref[s] = out.astype(BF16)
        lse_ref[s] = m + jnp.log2(l)
        return 0
    lax.fori_loop(0, SRC, finish, 0)

def attn_fwd(x, docs):
    return pl.pallas_call(
        functools.partial(fwd_kernel, kc=256),
        out_shape=(jax.ShapeDtypeStruct((SRC, HD, TOK), F32), jax.ShapeDtypeStruct((SRC, HD, TOK), BF16), jax.ShapeDtypeStruct((SRC, 1, TOK), F32)),
        in_specs=[pl.BlockSpec(memory_space=pltpu.VMEM)] * 2,
        out_specs=[pl.BlockSpec(memory_space=pltpu.VMEM)] * 3,
        scratch_shapes=[
            pltpu.VMEM((31, 2 * AUG + HD, TOK), BF16),
            pltpu.VMEM((31, TOK, AUG), BF16),
            pltpu.VMEM((31, HD + 16, TOK), F32),
        ],
        compiler_params=pltpu.CompilerParams(vmem_limit_bytes=50 * 2**20),
        cost_estimate=pl.CostEstimate(flops=35 * 10**9, bytes_accessed=3 * 2**20, transcendentals=0),
        name="attend",
    )(x, docs)

def bwd_kernel(x_ref, g_ref, docs_ref, o_ref, lse_ref, e_ref, fm, tm, eq, ek, ev):
    pad = jnp.zeros((AUG - HD - IDS - 16, TOK), BF16)
    pad2 = jnp.zeros((AUG - HD - 16, TOK), BF16)
    row16 = lax.broadcasted_iota(jnp.int32, (16, TOK), 0)
    ones = jnp.where(row16 < 3, 1.0, 0.0).astype(BF16)
    def three(v):
        hi, mid, lo = split3(v)
        hi, mid, lo = hi.astype(F32), mid.astype(F32), lo.astype(F32)
        return jnp.where(row16 == 0, hi, jnp.where(row16 == 1, mid, jnp.where(row16 == 2, lo, 0.0))).astype(BF16)
    def load(s, _):
        x = x_ref[s]
        d = docs_ref[s]
        g = g_ref[s]
        dot = jnp.sum(g.astype(F32) * o_ref[s], axis=0, keepdims=True)
        low = three(lse_ref[s] * (-1.0 / C2))
        off = three(-dot)
        fm[s] = jnp.concatenate([
            x[0:HD], marks(d, False), low, pad,
            g, off, pad2,
            x[HD:2 * HD], marks(d, True), ones, pad,
            x[2 * HD:], ones, pad2], axis=0)
        return 0
    lax.fori_loop(0, SRC, load, 0)
    pack_levels(fm)
    iden = eye(TOK)
    def turn(i, _):
        tm[i] = nt(iden, fm[i]).astype(BF16)
        return 0
    lax.fori_loop(0, 31, turn, 0)
    def zero(i, _):
        ek[i] = jnp.zeros((TOK, AUG), F32)
        ev[i] = jnp.zeros((TOK, AUG), F32)
        return 0
    lax.fori_loop(0, 31, zero, 0)

    def block(i, kfirst, count):
        q = fm[i, 0:AUG, :]
        g = fm[i, AUG:2 * AUG, :]
        qt = tm[i, :, 0:AUG]
        gt = tm[i, :, AUG:2 * AUG]
        acc = jnp.zeros((HD, TOK), F32)
        for t in range(count):
            k = kfirst + t
            p = jnp.exp2(nn(tm[k, :, 2 * AUG:3 * AUG], q) * C2)
            es = (p * nn(tm[k, :, 3 * AUG:], g)).astype(BF16)
            ev[k] += nn(p.astype(BF16), gt)
            ek[k] += nn(es, qt)
            acc = acc + nn(fm[k, 2 * AUG:2 * AUG + HD, :], es)
        eq[i] = acc
    def main(i, _):
        block(i, (i // 4) * 4, 4)
        return 0
    lax.fori_loop(0, 28, main, 0)
    block(28, 28, 2)
    block(29, 28, 2)
    block(30, 30, 1)

    for level in range(4, 0, -1):
        c = TOK >> level
        def join(g, _, level=level, c=c):
            child = FIRST[level] + g
            grid = spread_grid(c) if level > 1 else None
            for half in range(2):
                mine = FIRST[level - 1] + 2 * g + half
                got = eq[child, :, half * 128:half * 128 + 128]
                if level > 1:
                    eq[mine] += spread(got, grid)
                else:
                    eq[mine, :, 0:128] += got
                for s in range(128 // c):
                    ek[mine, 2 * c * s:2 * c * s + c, :] += ek[child, half * 128 + c * s:half * 128 + c * s + c, :]
                    ev[mine, 2 * c * s:2 * c * s + c, :] += ev[child, half * 128 + c * s:half * 128 + c * s + c, :]
            return 0
        lax.fori_loop(0, BLOCKS[level], join, 0)
    small = (lax.broadcasted_iota(jnp.int32, (HD, AUG), 0) == lax.broadcasted_iota(jnp.int32, (HD, AUG), 1)).astype(BF16)
    def finish(s, _):
        a = (eq[s] * ROOT).astype(BF16)
        b = nt(small, (ek[s] * ROOT).astype(BF16)).astype(BF16)
        v = nt(small, ev[s].astype(BF16)).astype(BF16)
        e_ref[s] = jnp.concatenate([a, b, v], axis=0)
        return 0
    lax.fori_loop(0, SRC, finish, 0)

def attn_bwd(x, g, docs, o, lse):
    return pl.pallas_call(
        bwd_kernel,
        out_shape=jax.ShapeDtypeStruct((SRC, 3 * HD, TOK), BF16),
        in_specs=[pl.BlockSpec(memory_space=pltpu.VMEM)] * 5,
        out_specs=pl.BlockSpec(memory_space=pltpu.VMEM),
        scratch_shapes=[
            pltpu.VMEM((31, 4 * AUG, TOK), BF16),
            pltpu.VMEM((31, TOK, 4 * AUG), BF16),
            pltpu.VMEM((31, HD, TOK), F32),
            pltpu.VMEM((31, TOK, AUG), F32),
            pltpu.VMEM((31, TOK, AUG), F32),
        ],
        compiler_params=pltpu.CompilerParams(vmem_limit_bytes=56 * 2**20),
        cost_estimate=pl.CostEstimate(flops=50 * 10**9, bytes_accessed=6 * 2**20, transcendentals=0),
        name="attend_back",
    )(x, g, docs, o, lse)


def layer_norm(values, gain_row, shift_row):
    center = values - jnp.mean(values, axis=-1, keepdims=True)
    scale = lax.rsqrt(jnp.mean(center * center, axis=-1, keepdims=True) + epsilon)
    unit = center * scale
    return unit, scale, (unit * gain_row + shift_row).astype(BF16)


def layer_norm_back(grad, unit, scale, gain_row):
    pulled = grad * gain_row
    return (
        pulled
        - jnp.mean(pulled, axis=-1, keepdims=True)
        - unit * jnp.mean(pulled * unit, axis=-1, keepdims=True)
    ) * scale


def gelu_parts(values):
    share = 0.5 * (1.0 + lax.erf(values * math.sqrt(0.5)))
    slope = share + values * jnp.exp(-0.5 * values * values) * (1.0 / math.sqrt(2 * math.pi))
    return (values * share).astype(BF16), slope


def head_order():
    block = np.array([int(f"{k:04b}"[::-1], 2) for k in range(16)])
    heads = np.arange(HEADS)[:, None, None]
    residue = (heads + block[None, :, None]) % 16
    return (np.arange(16)[None, None, :] * 16 + residue).reshape(HEADS, TOK)


def cube_forward(hidden, w_qkv, more, w_mlp, lines, order, docs, trade):
    gains, biases, up_bias = lines
    unit_one, scale_one, normed = layer_norm(hidden, gains[0], biases[0])
    mixed = jnp.einsum("df,td->ft", w_qkv, normed, preferred_element_type=F32)
    shift = jnp.concatenate([biases[1], jnp.zeros_like(biases[1]), biases[2]])
    mixed = (mixed + shift[:, None]).astype(BF16)
    mixed = mixed.reshape(3, HEADS, HEAD_DIM, TOK).transpose(1, 0, 2, 3).reshape(HEADS, 3 * HEAD_DIM, TOK)
    mixed = jnp.einsum("hft,htu->hfu", mixed, order, preferred_element_type=F32).astype(BF16)
    w_out, w_later, mixed = more(mixed)
    heads = trade(mixed)
    merged, merged_low, summary = attn_fwd(heads, docs)
    attended = trade(merged_low)
    attended = jnp.einsum("hdu,htu->hdt", attended, order, preferred_element_type=F32).astype(BF16)
    attended = attended.reshape(D, TOK)
    middle = hidden + jnp.einsum("ft,fd->td", attended, w_out, preferred_element_type=F32) + biases[3]
    unit_two, scale_two, normed_two = layer_norm(middle, gains[1], biases[4])
    ff = up_bias.shape[0]
    upward = jnp.dot(normed_two, w_mlp[:, :ff], preferred_element_type=F32) + up_bias
    activated, slope = gelu_parts(upward)
    result = middle + biases[5]
    for at in range(0, ff, D):
        result = result + jnp.dot(activated[:, at : at + D], w_mlp[:, ff + at : ff + at + D], preferred_element_type=F32)
    kept = (unit_one, scale_one, normed, heads, merged, summary, attended, unit_two, scale_two, normed_two, slope, activated)
    return result.astype(BF16), kept, w_out, w_later


def cube_backward(incoming_low, kept, params, order, docs, trade):
    w_qkv, w_out, w_mlp, gains, biases, up_bias = params
    unit_one, scale_one, normed, heads, merged, summary, attended, unit_two, scale_two, normed_two, slope, activated = kept
    ff = up_bias.shape[0]
    incoming = incoming_low.astype(F32)
    act_grad = jnp.concatenate([
        jnp.einsum("tb,ab->ta", incoming_low, w_mlp[:, ff + at : ff + at + D], preferred_element_type=F32)
        for at in range(0, ff, D)
    ], axis=1)
    up_grad = (act_grad * slope).astype(BF16)
    norm_two_grad = jnp.einsum("tb,ab->ta", up_grad, w_mlp[:, :ff], preferred_element_type=F32)
    middle_grad = incoming + layer_norm_back(norm_two_grad, unit_two, scale_two, gains[1])
    branch_grad = middle_grad.astype(BF16)
    merged_grad = jnp.einsum("fd,td->ft", w_out, branch_grad, preferred_element_type=F32).astype(BF16)
    merged_grad = merged_grad.reshape(HEADS, HEAD_DIM, TOK)
    merged_grad = jnp.einsum("hdt,htu->hdu", merged_grad, order, preferred_element_type=F32).astype(BF16)
    grad_rest = jnp.concatenate(
        [inner_rows(normed_two, up_grad).astype(BF16)]
        + [inner_rows(activated[:, at : at + D], incoming_low).astype(BF16) for at in range(0, ff, D)]
        + [jnp.einsum("ft,td->fd", attended, branch_grad, preferred_element_type=F32).astype(BF16)],
        axis=1,
    )
    merged_grad = trade(merged_grad)
    merged_grad, grad_rest = lax.optimization_barrier((merged_grad, grad_rest))
    back_heads = attn_bwd(heads, merged_grad, docs, merged, summary)
    mixed_grad = trade(back_heads)
    mixed_grad = jnp.einsum("hfu,htu->hft", mixed_grad, order, preferred_element_type=F32).astype(BF16)
    mixed_grad = mixed_grad.reshape(HEADS, 3, HEAD_DIM, TOK).transpose(1, 0, 2, 3).reshape(3 * D, TOK)
    grad_qkv = jnp.einsum("td,ft->df", normed, mixed_grad, preferred_element_type=F32).astype(BF16)
    grad_shift = jnp.sum(mixed_grad.astype(F32), axis=1)
    normed_grad = jnp.einsum("ft,df->td", mixed_grad, w_qkv, preferred_element_type=F32)
    start_grad = middle_grad + layer_norm_back(normed_grad, unit_one, scale_one, gains[0])
    small = jnp.stack([
        jnp.sum(normed_grad * unit_one, axis=0),
        jnp.sum(norm_two_grad * unit_two, axis=0),
        jnp.sum(normed_grad, axis=0),
        grad_shift[:D],
        grad_shift[2 * D:],
        jnp.sum(branch_grad.astype(F32), axis=0),
        jnp.sum(norm_two_grad, axis=0),
        jnp.sum(incoming, axis=0),
    ])
    grad_up_bias = jnp.sum(up_grad.astype(F32), axis=0)
    return start_grad, (grad_qkv, grad_rest, small, grad_up_bias)


def half_pairs(source, count):
    return [(source * count + j, (1 - source) * count + j) for j in range(count)]


def core_swap(value, bit):
    return lax.ppermute(value, "seq", [(j, j ^ (1 << bit)) for j in range(16)])


def section_swap(value):
    return lax.ppermute(value, "section", [(0, 1), (1, 0)])


def place_bit(bit):
    return (lax.axis_index("seq") >> bit) & 1


def two_of(own, got, bit, axis):
    return jnp.where(bit == 1, jnp.stack([got, own], axis), jnp.stack([own, got], axis))


def two_wide(own, got, bit):
    return jnp.where(bit == 1, jnp.concatenate([got, own], -1), jnp.concatenate([own, got], -1))


def collect(piece, order):
    rows = piece.shape[0]
    now = two_of(piece, core_swap(piece, 2), place_bit(2), 0)
    now = two_of(now, core_swap(now, 3), place_bit(3), 0).reshape(4, rows, -1)
    for axis in order:
        if axis == "y":
            now = two_of(now, core_swap(now, 1), place_bit(1), 1).reshape(8, rows, -1)
        else:
            now = two_wide(now, section_swap(now), lax.axis_index("section"))
    now = two_of(now, core_swap(now, 0), place_bit(0), 1)
    return now.reshape(16 * rows, -1)


def plus(own, got, dtype=BF16):
    return (own.astype(F32) + got.astype(F32)).astype(dtype)


def fold(value, bit, axis, dtype=BF16):
    mine = place_bit(bit)
    away = lax.dynamic_index_in_dim(value, 1 - mine, axis, keepdims=False)
    kept = lax.dynamic_index_in_dim(value, mine, axis, keepdims=False)
    return plus(kept, core_swap(away, bit), dtype)


def fold_wide(value):
    half = value.shape[-1] // 2
    lower = lax.axis_index("section") == 0
    away = jnp.where(lower, value[..., half:], value[..., :half])
    kept = jnp.where(lower, value[..., :half], value[..., half:])
    return plus(kept, section_swap(away))


def reduce_rows(partial, order):
    rows = partial.shape[0] // 16
    now = fold(partial.reshape(8, 2, rows, -1), 0, 1)
    for axis in order:
        if axis == "y":
            now = fold(now.reshape(4, 2, rows, -1), 1, 1)
        else:
            now = fold_wide(now)
    now = fold(now.reshape(2, 2, rows, -1), 3, 0)
    return fold(now, 2, 0, F32)


def cube_body(inputs, cotangent, documents, w_qkv, w_out, w_up, w_down, norm_gains, biases, up_bias):
    section_id = lax.axis_index("section")
    place = lax.axis_index("seq")
    count = lax.axis_size("seq")
    half = count // 2
    micro_id = place // half
    member = section_id * half + place % half
    teams = [[s * count + k * half + j for s in range(2) for j in range(half)] for k in range(2)]
    axes = ("section", "seq")
    lower = section_id == 0

    def trade(value):
        return lax.all_to_all(value, axes, 0, 0, axis_index_groups=teams, tiled=True)

    def across(value, pairs):
        return lax.ppermute(value, axes, pairs)

    def own_rows(pair):
        mine = jnp.where(micro_id == 0, pair[0], pair[1])
        other = jnp.where(micro_id == 0, pair[1], pair[0])
        swap = across(other, [(count + j, count + (j ^ half)) for j in range(count)])
        return jnp.where(lower, mine, swap)

    table = jnp.asarray(head_order())
    order = (table[:, None, :] == jnp.arange(TOK)[None, :, None]).astype(BF16)
    docs = jnp.where(micro_id == 0, documents[0], documents[1]).reshape(count, TOK)
    docs = jnp.where(micro_id == 0, docs, jnp.roll(docs, half, axis=0))
    own_order = lax.dynamic_index_in_dim(order, member, 0, keepdims=False)
    docs = jnp.dot(docs.astype(BF16), own_order, preferred_element_type=F32).reshape(count, 1, TOK)

    hidden = own_rows(inputs)
    wide = D // count
    lift = up_bias[0].reshape(-1, wide)
    small = jnp.concatenate([norm_gains[0], biases[0], lift]).T.astype(BF16)
    small = jnp.pad(small, ((0, 0), (0, 128 - small.shape[1])))

    def column_halves(shard, source):
        columns = shard.shape[1] // 2
        got = across(shard[:, columns:] if source == 0 else shard[:, :columns], half_pairs(source, count))
        if source == 0:
            return jnp.where(lower, shard[:, :columns], got)
        return jnp.where(lower, got, shard[:, columns:])

    def row_halves(shard, source):
        rows = shard.shape[0] // 2
        got = across(shard[rows:] if source == 0 else shard[:rows], half_pairs(source, count))
        if source == 0:
            return jnp.where(lower, shard[:rows], got)
        return jnp.where(lower, got, shard[rows:])

    ff = w_up.shape[2]
    low_qkv, low_out = w_qkv[0].astype(BF16), w_out[0].astype(BF16)
    piece = column_halves(low_qkv, 0)
    part_a = collect(piece[:, :640], "yx")
    part_b = collect(jnp.concatenate([piece[:, 640:], small], axis=1), "xy")
    qkv_first = jnp.concatenate([part_a[:, :640], part_b[:, :512], part_a[:, 640:], part_b[:, 640:1152]], axis=1)

    up_shard = w_up[0].astype(BF16).reshape(wide, count, 4, wide).transpose(0, 2, 1, 3).reshape(wide, ff)
    down_shard = w_down[0].astype(BF16).reshape(4, wide, D).transpose(1, 0, 2).reshape(wide, 4 * D)
    shard = jnp.concatenate([up_shard, down_shard, low_out], axis=1)
    mlp_first = lax.all_gather(row_halves(shard[:, : 2 * ff], 0), ("seq", "section"), axis=0, tiled=True)
    rest_final = lax.all_gather(row_halves(shard, 1), ("seq", "section"), axis=0, tiled=True)
    piece = jnp.concatenate([column_halves(low_qkv, 1), column_halves(low_out, 0)], axis=1)

    def lines(columns):
        values = columns[:, :12].astype(F32).T
        return values[:2], values[2:8], values[8:].reshape(ff)

    def second_weights(after):
        later, after = lax.optimization_barrier((piece, after))
        part_a = collect(later[:, :768], "yx")
        part_b = collect(later[:, 768:], "xy")
        qkv = jnp.concatenate([part_a[:, :768], part_b[:, :384], part_a[:, 768:], part_b[:, 768:1152]], axis=1)
        return jnp.concatenate([part_b[:, 384:768], part_b[:, 1152:]], axis=1), qkv, after

    lines_first, lines_final = lines(part_b[:, 512:640]), lines(part_b[:, 1152:])
    first, kept_first, out_first, qkv_final = cube_forward(
        hidden.astype(F32), qkv_first, second_weights, mlp_first, lines_first, order, docs, trade
    )
    out_final = rest_final[:, 2 * ff :]
    final, kept_final, _, _ = cube_forward(
        first.astype(F32), qkv_final, lambda after: (out_final, None, after), rest_final, lines_final, order, docs, trade
    )
    params_final = (qkv_final, out_final, rest_final) + lines_final
    grad_final, terms_final = cube_backward(own_rows(cotangent), kept_final, params_final, order, docs, trade)

    def scattered(partial):
        return lax.psum_scatter(partial, "seq", scatter_dimension=0, tiled=True)

    sent, qkv_term = lax.optimization_barrier((grad_final.astype(BF16), terms_final[0]))
    rest_final = scattered(terms_final[1])
    params_first = (qkv_first, out_first, mlp_first) + lines_first
    grad_first, terms_first = cube_backward(sent, kept_first, params_first, order, docs, trade)
    rest_first = scattered(terms_first[1])

    def shared_out(value_first, value_final):
        far = across(value_first, [(count + j, j ^ half) for j in range(count)])
        near = across(value_final, half_pairs(0, count))
        beside = across(value_final, [(count + j, count + (j ^ half)) for j in range(count)])
        return far, near, beside

    def placed(mine, other):
        return jnp.where(micro_id == 0, jnp.stack([mine, other]), jnp.stack([other, mine]))[None]

    outs = shared_out(first, final)
    backs = shared_out(grad_first.astype(BF16), sent)
    qkv_first = reduce_rows(terms_first[0], "xy")
    qkv_final = reduce_rows(qkv_term, "yx")

    def upright(rows, wide_row):
        return jnp.concatenate([rows, wide_row.reshape(4, D)]).T

    smalls = jnp.concatenate([upright(*terms_first[2:]), upright(*terms_final[2:])], axis=1)
    smalls = fold(smalls.reshape(8, 2, wide, 24), 0, 1, F32)
    smalls = fold(smalls.reshape(4, 2, wide, 24), 1, 1, F32)
    smalls = fold(smalls.reshape(2, 2, wide, 24), 3, 0, F32)
    smalls = fold(smalls, 2, 0, F32)
    smalls = smalls + section_swap(smalls)
    smalls = jnp.where(lower, smalls[:, :12], smalls[:, 12:]).T

    grad_first, outs, rest_first, rest_final = lax.optimization_barrier((grad_first, outs, rest_first, rest_final))
    far, near, beside = outs
    layer_outputs = placed(jnp.where(lower, first, near), jnp.where(lower, far, beside))
    far, near, beside = backs
    input_grads = placed(
        jnp.where(lower, grad_first, near.astype(F32)), jnp.where(lower, far, beside).astype(F32)
    )

    def finished(part_first, part_final):
        got_final = across(part_final, half_pairs(0, count))
        got_first = across(part_first, half_pairs(1, count))
        return jnp.where(
            lower,
            part_first.astype(F32) + got_first.astype(F32),
            part_final.astype(F32) + got_final.astype(F32),
        )

    rest = finished(rest_first, rest_final)
    away = section_swap(jnp.where(lower, qkv_final, qkv_first).astype(BF16)).astype(F32)
    qkv = jnp.where(
        lower, jnp.concatenate([qkv_first, away], axis=1), jnp.concatenate([away, qkv_final], axis=1)
    )
    up = rest[:, :ff].reshape(wide, 4, count, wide).transpose(0, 2, 1, 3).reshape(wide, ff)
    down = rest[:, ff : 2 * ff].reshape(wide, 4, D).transpose(1, 0, 2).reshape(4 * wide, D)
    return (
        layer_outputs,
        input_grads,
        qkv[None],
        rest[None, :, 2 * ff :],
        up[None],
        down[None],
        smalls[None, :2],
        smalls[None, 2:8],
        smalls[8:].reshape(1, -1),
    )


def solution(mesh):
    cube = mesh.shape["seq"] == 16
    return jax.shard_map(
        cube_body if cube else body,
        mesh=mesh,
        in_specs=(
            P(None, "seq", None),
            P(None, "seq", None),
            P(),
            P("section", "seq", None),
            P("section", "seq", None),
            P("section", "seq", None),
            P("section", "seq", None),
            P("section", None, "seq"),
            P("section", None, "seq"),
            P("section", "seq"),
        ),
        out_specs=(
            P("section", None, "seq", None),
            P("section", None, "seq", None),
            P("section", "seq", None),
            P("section", "seq", None),
            P("section", "seq", None),
            P("section", "seq", None),
            P("section", None, "seq"),
            P("section", None, "seq"),
            P("section", "seq"),
        ),
        check_vma=False,
    )
```

```python
import functools
import math

import jax
import jax.numpy as jnp
import numpy as np
from jax import lax
from jax.experimental import pallas as pl
from jax.experimental.pallas import tpu as pltpu
from jax.sharding import PartitionSpec as P

D = 768
HEADS = 16
HEAD_DIM = 48
SEG0 = 1024
BRANCHES = 5


epsilon = 1e-05
masked_score = -1e30
highest = lax.Precision.HIGHEST


def swapped(value, axis, apart):
    mask = 2**apart
    pairs = [(source, source ^ mask) for source in range(lax.axis_size(axis))]
    return lax.ppermute(value, axis, pairs)


def for_sending(array):
    return jax.tree.map(lambda a: a.astype(jnp.bfloat16) if a.dtype == jnp.float32 else a, array)


def passed_along(array, axis, by):
    peers = lax.axis_size(axis)
    pairs = [(i, i + by) for i in range(peers) if 0 <= i + by < peers]
    return lax.ppermute(array, axis, pairs)


def layer_norm_parts(values, gain_row, shift_row):
    center = values - jnp.mean(values, axis=-1, keepdims=True)
    spread = jnp.mean(center * center, axis=-1, keepdims=True)
    return center * lax.rsqrt(spread + epsilon) * gain_row + shift_row


def exact_gelu(values):
    return jax.nn.gelu(values, approximate=False)


def inner_rows(left, right):
    return jnp.einsum("ta,tb->ab", left, right, preferred_element_type=jnp.float32)


def geometry(tokens_dev, devices):
    groups = [
        min(SEG0 * 2**level_id, tokens_dev * devices) // tokens_dev for level_id in range(BRANCHES)
    ]
    return (groups, max(groups).bit_length() - 1)


def first_level(groups, step_id):
    return min((level_id for level_id in range(BRANCHES) if groups[level_id] > 2**step_id))


def pick_grid(level_id, dtype):
    dilation = 2**level_id
    return (jnp.arange(dilation)[:, None] == (jnp.arange(HEADS) % dilation)[None, :]).astype(dtype)


def select_rows(tensor, level_id):
    dilation = 2**level_id
    shaped = tensor.reshape((tensor.shape[0] // dilation, dilation) + tensor.shape[1:])
    if tensor.dtype == jnp.bfloat16:
        chosen = jnp.einsum(
            "jrh...,rh->jh...",
            shaped,
            pick_grid(level_id, jnp.bfloat16),
            preferred_element_type=jnp.float32,
        )
        return chosen.astype(jnp.bfloat16)
    return jnp.einsum(
        "jrh...,rh->jh...", shaped, pick_grid(level_id, jnp.float32), precision=highest
    )


def spread_rows(tensor, level_id):
    dilation = 2**level_id
    spread = jnp.einsum(
        "jh...,rh->jrh...", tensor, pick_grid(level_id, jnp.float32), precision=highest
    )
    return spread.reshape((tensor.shape[0] * dilation,) + tensor.shape[1:])


def spread_sums(tensor, level_id):
    dilation = 2**level_id
    grid = pick_grid(level_id, jnp.float32)
    spread = jnp.where(grid[None] > 0, tensor[:, None, :], masked_score)
    return spread.reshape(tensor.shape[0] * dilation, HEADS)


def doc_tables(documents_now, level_id, group, tokens_dev, seq_place):
    dilation = 2**level_id
    offsets = np.arange(HEADS) % dilation
    own_docs = lax.dynamic_slice_in_dim(documents_now, seq_place * tokens_dev, tokens_dev)
    own_docs = own_docs.reshape(tokens_dev // dilation, dilation)[:, offsets]
    seg_start = seq_place // group * group * tokens_dev
    seg_docs = lax.dynamic_slice_in_dim(documents_now, seg_start, group * tokens_dev)
    seg_docs = seg_docs.reshape(group * tokens_dev // dilation, dilation)[:, offsets]
    return (own_docs, seg_docs)


def head_bits(level_id):
    return jnp.arange(HEADS) >> level_id & 1


def halve(buffer, level_id):
    pairs = buffer.reshape(buffer.shape[0], buffer.shape[1] // 2, 2, HEADS, HEAD_DIM)
    chosen = head_bits(level_id)[None, None, :, None] == 1
    return jnp.where(chosen, pairs[:, :, 1], pairs[:, :, 0])


def widen(buffer, level_id):
    chosen = head_bits(level_id)[None, None, :, None] == 1
    empty = jnp.zeros_like(buffer)
    upper_part = jnp.where(chosen, buffer, empty)
    lower_part = jnp.where(chosen, empty, buffer)
    stacked = jnp.stack([lower_part, upper_part], axis=2)
    return stacked.reshape(buffer.shape[0], buffer.shape[1] * 2, HEADS, HEAD_DIM)


def thin_to(buffer, low_level, high_level):
    for level_id in range(low_level, high_level):
        buffer = halve(buffer, level_id)
    return buffer


def widen_to(buffer, low_level, high_level):
    for level_id in reversed(range(low_level, high_level)):
        buffer = widen(buffer, level_id)
    return buffer


def gather_keys(own_rows, groups, step_count, seq_place):
    results = [None] * BRANCHES
    current = own_rows
    level_now = 0
    for level_id in range(BRANCHES):
        pass
    for step_id in range(step_count):
        target = first_level(groups, step_id)
        current = thin_to(current, level_now, target)
        level_now = target
        row_count = current.shape[1]
        flat_rows = current.reshape(2, row_count, HEADS * HEAD_DIM)
        incoming = swapped(flat_rows, "seq", step_id).reshape(current.shape)
        upper_half = seq_place >> step_id & 1 == 1
        current = jnp.where(
            upper_half,
            jnp.concatenate([incoming, current], axis=1),
            jnp.concatenate([current, incoming], axis=1),
        )
        for level_id in range(BRANCHES):
            if groups[level_id] == 2 ** (step_id + 1):
                results[level_id] = thin_to(current, level_now, level_id)
    return results


def scatter_keys(key_grads, groups, step_count, seq_place):
    carried = None
    for step_id in reversed(range(step_count)):
        level_now = first_level(groups, step_id)
        total_grad = None
        if carried is not None:
            total_grad = widen_to(carried, level_now, first_level(groups, step_id + 1))
        for level_id in range(BRANCHES):
            if groups[level_id] == 2 ** (step_id + 1):
                branch_term = widen_to(key_grads[level_id], level_now, level_id)
                total_grad = branch_term if total_grad is None else total_grad + branch_term
        half_rows = total_grad.shape[1] // 2
        upper_half = seq_place >> step_id & 1 == 1
        own_half = jnp.where(upper_half, total_grad[:, half_rows:], total_grad[:, :half_rows])
        theirs = jnp.where(upper_half, total_grad[:, :half_rows], total_grad[:, half_rows:])
        flat_rows = theirs.reshape(2, half_rows, HEADS * HEAD_DIM)
        incoming = (
            swapped(for_sending(flat_rows), "seq", step_id)
            .astype(flat_rows.dtype)
            .reshape(own_half.shape)
        )
        carried = own_half + incoming
    own_grad = widen_to(carried, 0, first_level(groups, 0))
    for level_id in range(BRANCHES):
        pass
    return own_grad


def head_blocks(level_id):
    block_size = min(HEADS, 4 * 2**level_id)
    return (HEADS // block_size, block_size)


def to_blocks(tensor, block_count, block_size):
    moved = jnp.moveaxis(tensor, 1, 0)
    return moved.reshape((block_count, block_size) + moved.shape[1:])


def from_blocks(tensor):
    joined = tensor.reshape((tensor.shape[0] * tensor.shape[1],) + tensor.shape[2:])
    return jnp.moveaxis(joined, 0, 1)


def score_block(query_block, key_block, query_doc, key_doc):
    scores = jnp.einsum(
        "hqd,hkd->hqk", query_block, key_block, preferred_element_type=jnp.float32
    ) * HEAD_DIM ** (-0.5)
    return jnp.where(query_doc[:, :, None] == key_doc[:, None, :], scores, masked_score)


def forward_block(pieces):
    query_block, key_block, value_block, query_doc, key_doc = pieces
    scores = score_block(query_block, key_block, query_doc, key_doc)
    row_max = jnp.max(scores, axis=-1, keepdims=True)
    weights = jnp.exp(scores - row_max)
    row_total = jnp.sum(weights, axis=-1, keepdims=True)
    prob_rows = (weights / row_total).astype(jnp.bfloat16)
    result = jnp.einsum("hqk,hkd->hqd", prob_rows, value_block, preferred_element_type=jnp.float32)
    return (result, (row_max + jnp.log(row_total))[:, :, 0])


def backward_block(pieces):
    query_block, key_block, value_block, query_doc, key_doc, summary, out_grad, summary_grad = (
        pieces
    )
    scores = score_block(query_block, key_block, query_doc, key_doc)
    prob_rows = jnp.exp(scores - summary[:, :, None])
    prob_grad = jnp.einsum(
        "hqd,hkd->hqk", out_grad, value_block, preferred_element_type=jnp.float32
    )
    score_grad = prob_rows * (
        prob_grad
        - jnp.sum(prob_rows * prob_grad, axis=-1, keepdims=True)
        + summary_grad[:, :, None]
    )
    score_grad = score_grad.astype(jnp.bfloat16)
    score_scale = HEAD_DIM ** (-0.5)
    query_grad = (
        jnp.einsum("hqk,hkd->hqd", score_grad, key_block, preferred_element_type=jnp.float32)
        * score_scale
    )
    key_grad = (
        jnp.einsum("hqk,hqd->hkd", score_grad, query_block, preferred_element_type=jnp.float32)
        * score_scale
    )
    value_grad = jnp.einsum(
        "hqk,hqd->hkd", prob_rows.astype(jnp.bfloat16), out_grad, preferred_element_type=jnp.float32
    )
    return (query_grad, key_grad, value_grad)


def branch_forward(query_sel, key_value, query_docs, key_docs, level_id):
    block_count, block_size = head_blocks(level_id)
    pieces = (
        to_blocks(query_sel, block_count, block_size),
        to_blocks(key_value[0], block_count, block_size),
        to_blocks(key_value[1], block_count, block_size),
        to_blocks(query_docs, block_count, block_size),
        to_blocks(key_docs, block_count, block_size),
    )
    results, summaries = lax.map(forward_block, pieces)
    return (from_blocks(results), from_blocks(summaries))


def branch_backward(
    query_sel, key_value, query_docs, key_docs, summary, out_grad, summary_grad, level_id
):
    block_count, block_size = head_blocks(level_id)
    pieces = (
        to_blocks(query_sel, block_count, block_size),
        to_blocks(key_value[0], block_count, block_size),
        to_blocks(key_value[1], block_count, block_size),
        to_blocks(query_docs, block_count, block_size),
        to_blocks(key_docs, block_count, block_size),
        to_blocks(summary, block_count, block_size),
        to_blocks(out_grad, block_count, block_size),
        to_blocks(summary_grad, block_count, block_size),
    )
    query_grad, key_grad, value_grad = lax.map(backward_block, pieces)
    return (from_blocks(query_grad), jnp.stack([from_blocks(key_grad), from_blocks(value_grad)]))


def layer_forward(hidden, params, documents_now, groups, step_count, seq_place):
    w_qkv, w_out, w_up, w_down, gains, biases, up_bias = params
    gains = gains.astype(jnp.float32)
    biases = biases.astype(jnp.float32)
    tokens_dev = hidden.shape[0]
    normed = layer_norm_parts(hidden, gains[0], biases[0]).astype(jnp.bfloat16)
    mixed_rows = jnp.dot(normed, w_qkv, preferred_element_type=jnp.float32)
    queries = (mixed_rows[:, :D] + biases[1]).astype(jnp.bfloat16)
    key_part = mixed_rows[:, D : 2 * D].astype(jnp.bfloat16)
    values = (mixed_rows[:, 2 * D :] + biases[2]).astype(jnp.bfloat16)
    own_rows = jnp.stack([key_part, values]).reshape(2, tokens_dev, HEADS, HEAD_DIM)
    gathered = gather_keys(own_rows, groups, step_count, seq_place)
    query_heads = queries.reshape(tokens_dev, HEADS, HEAD_DIM)
    picked, branch_outs, branch_sums = ([], [], [])
    for level_id in range(BRANCHES):
        query_sel = select_rows(query_heads, level_id)
        query_docs, key_docs = doc_tables(
            documents_now, level_id, groups[level_id], tokens_dev, seq_place
        )
        result, summary = branch_forward(
            query_sel, gathered[level_id], query_docs, key_docs, level_id
        )
        picked.append(query_sel)
        branch_outs.append(result)
        branch_sums.append(summary)
    full_sums = jnp.stack(
        [spread_sums(branch_sums[level_id], level_id) for level_id in range(BRANCHES)]
    )
    row_max = jnp.max(full_sums, axis=0)
    shares = jnp.exp(full_sums - row_max)
    shares = shares / jnp.sum(shares, axis=0)
    merged = sum(
        (
            shares[level_id][:, :, None] * spread_rows(branch_outs[level_id], level_id)
            for level_id in range(BRANCHES)
        )
    )
    attended = merged.reshape(tokens_dev, D).astype(jnp.bfloat16)
    middle = hidden + jnp.dot(attended, w_out, preferred_element_type=jnp.float32) + biases[3]
    normed_two = layer_norm_parts(middle, gains[1], biases[4]).astype(jnp.bfloat16)
    upward = jnp.dot(normed_two, w_up, preferred_element_type=jnp.float32) + up_bias.astype(
        jnp.float32
    )
    activated = exact_gelu(upward).astype(jnp.bfloat16)
    result = middle + jnp.dot(activated, w_down, preferred_element_type=jnp.float32) + biases[5]
    kept_values = (
        hidden,
        normed,
        picked,
        gathered,
        branch_sums,
        branch_outs,
        shares,
        merged,
        attended,
        middle,
        normed_two,
        upward,
        activated,
    )
    return (result, kept_values)


def layer_backward(incoming, kept_values, params, documents_now, groups, step_count, seq_place):
    w_qkv, w_out, w_up, w_down, gains, biases, up_bias = params
    gains = gains.astype(jnp.float32)
    biases = biases.astype(jnp.float32)
    (
        hidden,
        normed,
        picked,
        gathered,
        branch_sums,
        branch_outs,
        shares,
        merged,
        attended,
        middle,
        normed_two,
        upward,
        activated,
    ) = kept_values
    tokens_dev = hidden.shape[0]
    down_grad = incoming.astype(jnp.bfloat16)
    grad_down = inner_rows(activated, down_grad)
    grad_bias_down = jnp.sum(down_grad.astype(jnp.float32), axis=0)
    act_grad = jnp.einsum("tb,ab->ta", down_grad, w_down, preferred_element_type=jnp.float32)
    gelu_pulled = jax.vjp(exact_gelu, upward)
    up_grad = gelu_pulled[1](act_grad)[0].astype(jnp.bfloat16)
    grad_up = inner_rows(normed_two, up_grad)
    grad_up_bias = jnp.sum(up_grad.astype(jnp.float32), axis=0)
    norm_two_grad = jnp.einsum("tb,ab->ta", up_grad, w_up, preferred_element_type=jnp.float32)
    norm_pulled = jax.vjp(layer_norm_parts, middle, gains[1], biases[4])
    middle_part, grad_gain_two, grad_shift_two = norm_pulled[1](norm_two_grad)
    middle_grad = incoming + middle_part
    branch_grad = middle_grad.astype(jnp.bfloat16)
    grad_out = inner_rows(attended, branch_grad)
    grad_bias_out = jnp.sum(branch_grad.astype(jnp.float32), axis=0)
    merged_grad = jnp.einsum("tb,ab->ta", branch_grad, w_out, preferred_element_type=jnp.float32)
    merged_grad = merged_grad.reshape(tokens_dev, HEADS, HEAD_DIM)
    query_grad = jnp.zeros((tokens_dev, HEADS, HEAD_DIM), jnp.float32)
    key_grads = []
    for level_id in range(BRANCHES):
        share_sel = select_rows(shares[level_id], level_id)
        merged_sel = select_rows(merged, level_id)
        grad_sel = select_rows(merged_grad, level_id)
        out_grad = (share_sel[:, :, None] * grad_sel).astype(jnp.bfloat16)
        summary_grad = share_sel * (
            jnp.sum(grad_sel * branch_outs[level_id], axis=-1)
            - jnp.sum(grad_sel * merged_sel, axis=-1)
        )
        query_docs, key_docs = doc_tables(
            documents_now, level_id, groups[level_id], tokens_dev, seq_place
        )
        query_part, key_value_grad = branch_backward(
            picked[level_id],
            gathered[level_id],
            query_docs,
            key_docs,
            branch_sums[level_id],
            out_grad,
            summary_grad,
            level_id,
        )
        query_grad = query_grad + spread_rows(query_part, level_id)
        key_grads.append(key_value_grad)
    own_grad = scatter_keys(key_grads, groups, step_count, seq_place)
    mixed_grad = jnp.concatenate(
        [
            query_grad.reshape(tokens_dev, D),
            own_grad[0].reshape(tokens_dev, D),
            own_grad[1].reshape(tokens_dev, D),
        ],
        axis=1,
    ).astype(jnp.bfloat16)
    grad_qkv = inner_rows(normed, mixed_grad)
    grad_bias_query = jnp.sum(mixed_grad[:, :D].astype(jnp.float32), axis=0)
    grad_bias_value = jnp.sum(mixed_grad[:, 2 * D :].astype(jnp.float32), axis=0)
    normed_grad = jnp.einsum("tb,ab->ta", mixed_grad, w_qkv, preferred_element_type=jnp.float32)
    norm_pulled = jax.vjp(layer_norm_parts, hidden, gains[0], biases[0])
    hidden_part, grad_gain_one, grad_shift_one = norm_pulled[1](normed_grad)
    start_grad = middle_grad + hidden_part
    gradients = (
        grad_qkv,
        grad_out,
        grad_up,
        grad_down,
        jnp.stack([grad_gain_one, grad_gain_two]),
        jnp.stack(
            [
                grad_shift_one,
                grad_bias_query,
                grad_bias_value,
                grad_bias_out,
                grad_shift_two,
                grad_bias_down,
            ]
        ),
        grad_up_bias,
    )
    return (start_grad, gradients)


def body(inputs, cotangent, documents, w_qkv, w_out, w_up, w_down, norm_gains, biases, up_bias):
    section_id = lax.axis_index("section")
    seq_place = lax.axis_index("seq")
    devices = lax.axis_size("seq")
    micro = inputs.shape[0]
    tokens_dev = inputs.shape[1]
    groups, step_count = geometry(tokens_dev, devices)
    params = (
        lax.all_gather(w_qkv[0].astype(jnp.bfloat16), "seq", axis=0, tiled=True),
        lax.all_gather(w_out[0].astype(jnp.bfloat16), "seq", axis=0, tiled=True),
        lax.all_gather(w_up[0].astype(jnp.bfloat16), "seq", axis=0, tiled=True),
        lax.all_gather(w_down[0].astype(jnp.bfloat16), "seq", axis=0, tiled=True),
        lax.all_gather(norm_gains[0].astype(jnp.bfloat16), "seq", axis=1, tiled=True),
        lax.all_gather(biases[0].astype(jnp.bfloat16), "seq", axis=1, tiled=True),
        lax.all_gather(up_bias[0].astype(jnp.bfloat16), "seq", axis=0, tiled=True),
    )
    empty_rows = jnp.zeros((tokens_dev, D), jnp.bfloat16)
    received = empty_rows
    saved = []
    produced = []
    for tick_id in range(micro + 1):
        batch_index = jnp.clip(tick_id - section_id, 0, micro - 1)
        documents_now = lax.dynamic_index_in_dim(documents, batch_index, 0, keepdims=False)
        fresh_rows = inputs[tick_id] if tick_id < micro else empty_rows
        start_rows = jnp.where(section_id == 0, fresh_rows, received).astype(jnp.float32)
        result, kept_values = layer_forward(
            start_rows, params, documents_now, groups, step_count, seq_place
        )
        sent_rows = result.astype(jnp.bfloat16)
        produced.append(sent_rows)
        saved.append((kept_values, documents_now))
        if tick_id < micro:
            received = passed_along(sent_rows, "section", 1)
    back_received = empty_rows
    start_grads = []
    sent_grads = []
    totals = None
    shards = None
    for tick_id in range(micro + 1):
        earlier_save = saved[max(tick_id - 1, 0)]
        later_save = saved[min(tick_id + 1, micro)]
        kept_values, documents_now = jax.tree.map(
            lambda earlier, latter: jnp.where(section_id == 0, earlier, latter),
            earlier_save,
            later_save,
        )
        fresh_rows = cotangent[tick_id] if tick_id < micro else empty_rows
        incoming = jnp.where(section_id == 1, fresh_rows, back_received).astype(jnp.float32)
        start_grad, gradients = layer_backward(
            incoming, kept_values, params, documents_now, groups, step_count, seq_place
        )
        sent_rows = start_grad.astype(jnp.bfloat16)
        start_grads.append(start_grad)
        sent_grads.append(sent_rows.astype(jnp.float32))
        if tick_id < micro:
            back_received = passed_along(sent_rows, "section", -1)
        totals = (
            list(gradients)
            if totals is None
            else [earlier + latter for earlier, latter in zip(totals, gradients)]
        )
    shards = (
        lax.psum_scatter(totals[0], "seq", scatter_dimension=0, tiled=True),
        lax.psum_scatter(totals[1], "seq", scatter_dimension=0, tiled=True),
        lax.psum_scatter(totals[2], "seq", scatter_dimension=0, tiled=True),
        lax.psum_scatter(totals[3], "seq", scatter_dimension=0, tiled=True),
        lax.psum_scatter(totals[4], "seq", scatter_dimension=1, tiled=True),
        lax.psum_scatter(totals[5], "seq", scatter_dimension=1, tiled=True),
        lax.psum_scatter(totals[6], "seq", scatter_dimension=0, tiled=True),
    )
    layer_outputs = jnp.stack(
        [
            jnp.where(section_id == 0, produced[batch_id], produced[batch_id + 1])
            for batch_id in range(micro)
        ]
    )[None]
    input_grads = jnp.stack(
        [
            jnp.where(section_id == 0, start_grads[batch_id + 1], sent_grads[batch_id])
            for batch_id in range(micro)
        ]
    )[None]
    return (
        layer_outputs,
        input_grads,
        shards[0][None],
        shards[1][None],
        shards[2][None],
        shards[3][None],
        shards[4][None],
        shards[5][None],
        shards[6][None],
    )


HD = 48
AUG = 128
IDS = 32
SRC = 16
TOK = 256
ROOT = HD ** -0.5
C2 = ROOT * math.log2(math.e)
AWAY = -(2.0 ** 100)
BLOCKS = (16, 8, 4, 2, 1)
FIRST = (0, 16, 24, 28, 30)
F32, BF16 = jnp.float32, jnp.bfloat16

UN = 16
MAIN = 1
QW = 4
TWO = False

def loop(n, f, u=None):
    u = min(u or UN, n)
    while n % u:
        u -= 1
    def many(i, _):
        for j in range(u):
            f(i * u + j, 0)
        return 0
    lax.fori_loop(0, n // u, many, 0)

def nt(a, b):
    return lax.dot_general(a, b, (((1,), (1,)), ((), ())), preferred_element_type=F32)

def nn(a, b):
    return jnp.dot(a, b, preferred_element_type=F32)

def eye(n):
    return (lax.broadcasted_iota(jnp.int32, (n, n), 0) == lax.broadcasted_iota(jnp.int32, (n, n), 1)).astype(BF16)

def pack_grid(c):
    col = lax.broadcasted_iota(jnp.int32, (256, 128), 1)
    row = lax.broadcasted_iota(jnp.int32, (256, 128), 0)
    return (row == (col // c) * (2 * c) + col % c).astype(BF16)

def spread_grid(c):
    row = lax.broadcasted_iota(jnp.int32, (128, 256), 0)
    col = lax.broadcasted_iota(jnp.int32, (128, 256), 1)
    return (col == (row // c) * (2 * c) + row % c).astype(BF16)

def split3(v):
    hi = v.astype(BF16)
    r = v - hi.astype(F32)
    mid = r.astype(BF16)
    lo = (r - mid.astype(F32)).astype(BF16)
    return hi, mid, lo

def spread(v, grid):
    hi, mid, lo = split3(v)
    return nn(hi, grid) + nn(mid, grid) + nn(lo, grid)

def pack_levels(stack):
    for level in range(1, 5):
        c = TOK >> level
        def step(g, _, level=level, c=c):
            a = stack[FIRST[level - 1] + 2 * g]
            b = stack[FIRST[level - 1] + 2 * g + 1]
            if level == 1:
                pa, pb = a[:, :128], b[:, :128]
            else:
                grid = pack_grid(c)
                pa, pb = nn(a, grid).astype(BF16), nn(b, grid).astype(BF16)
            stack[FIRST[level] + g] = jnp.concatenate([pa, pb], axis=1)
            return 0
        loop(BLOCKS[level], step)

def marks(doc_row, away):
    ids = lax.broadcasted_iota(jnp.int32, (IDS, TOK), 0).astype(F32)
    same = ids == doc_row
    return (jnp.where(same, 0.0, AWAY) if away else jnp.where(same, 1.0, 0.0)).astype(BF16)

def fwd_kernel(x_ref, docs_ref, o_ref, ob_ref, lse_ref, fm, ktm, part, *, kc):
    pad = jnp.zeros((AUG - HD - IDS, TOK), BF16)
    def load(s, _):
        x = x_ref[s]
        d = docs_ref[s]
        fm[s] = jnp.concatenate([x[0:HD], marks(d, False), pad, x[HD:2 * HD], marks(d, True), pad, x[2 * HD:]], axis=0)
        return 0
    loop(SRC, load)
    pack_levels(fm)
    iden = eye(TOK)
    def turn(i, _):
        ktm[i] = nt(iden, fm[i, AUG:2 * AUG, :]).astype(BF16)
        return 0
    loop(30, turn); turn(30, 0)

    def segment(first, count):
        for at in range(0, count, QW):
            n = min(QW, count - at)
            q = jnp.concatenate([fm[first + at + b, 0:AUG, :] for b in range(n)], axis=1)
            scores = [nn(ktm[first + t], q) for t in range(count)]
            top = functools.reduce(jnp.maximum, [jnp.max(x, axis=0, keepdims=True) for x in scores])
            ps = [jnp.exp2((x - top) * C2) for x in scores]
            total = functools.reduce(jnp.add, [jnp.sum(p, axis=0, keepdims=True) for p in ps])
            p = jnp.concatenate([p.astype(BF16) for p in ps], axis=0)
            v = jnp.concatenate([fm[first + t, 2 * AUG:2 * AUG + HD, :] for t in range(count)], axis=1)
            out = nn(v, p)
            for b in range(n):
                part[first + at + b, 0:HD] = out[:, b * TOK:(b + 1) * TOK]
                part[first + at + b, HD:HD + 8] = jnp.broadcast_to(total[:, b * TOK:(b + 1) * TOK], (8, TOK))
                part[first + at + b, HD + 8:HD + 16] = jnp.broadcast_to(top[:, b * TOK:(b + 1) * TOK] * C2, (8, TOK))
    loop(7, lambda i, _: segment(i * 4, 4), MAIN)
    segment(28, 2)
    segment(30, 1)

    for level in range(4, 0, -1):
        c = TOK >> level
        def join(g, _, level=level, c=c):
            child = FIRST[level] + g
            grid = spread_grid(c) if level > 1 else None
            for half in range(2):
                mine = FIRST[level - 1] + 2 * g + half
                got = part[child, :, half * 128:half * 128 + 128]
                if level > 1:
                    got = spread(got, grid)
                else:
                    got = jnp.concatenate([got, jnp.zeros_like(got)], axis=1)
                own = part[mine]
                cl, cm = got[HD:HD + 1], got[HD + 8:HD + 9]
                cm = jnp.where(cl > 0, cm, AWAY)
                ol, om = own[HD:HD + 1], own[HD + 8:HD + 9]
                top = jnp.maximum(cm, om)
                wc, wo = jnp.exp2(cm - top), jnp.exp2(om - top)
                part[mine, 0:HD] = got[0:HD] * wc + own[0:HD] * wo
                part[mine, HD:HD + 8] = jnp.broadcast_to(cl * wc + ol * wo, (8, TOK))
                part[mine, HD + 8:HD + 16] = jnp.broadcast_to(top, (8, TOK))
            return 0
        loop(BLOCKS[level], join)
    def finish(s, _):
        own = part[s]
        l, m = own[HD:HD + 1], own[HD + 8:HD + 9]
        out = own[0:HD] / l
        o_ref[s] = out
        ob_ref[s] = out.astype(BF16)
        lse_ref[s] = m + jnp.log2(l)
        return 0
    loop(SRC, finish)

def attn_fwd(x, docs):
    return pl.pallas_call(
        functools.partial(fwd_kernel, kc=256),
        out_shape=(jax.ShapeDtypeStruct((SRC, HD, TOK), F32), jax.ShapeDtypeStruct((SRC, HD, TOK), BF16), jax.ShapeDtypeStruct((SRC, 1, TOK), F32)),
        in_specs=[pl.BlockSpec(memory_space=pltpu.VMEM)] * 2,
        out_specs=[pl.BlockSpec(memory_space=pltpu.VMEM)] * 3,
        scratch_shapes=[
            pltpu.VMEM((31, 2 * AUG + HD, TOK), BF16),
            pltpu.VMEM((31, TOK, AUG), BF16),
            pltpu.VMEM((31, HD + 16, TOK), F32),
        ],
        compiler_params=pltpu.CompilerParams(vmem_limit_bytes=50 * 2**20),
        cost_estimate=pl.CostEstimate(flops=18 * 10**9, bytes_accessed=3 * 2**20, transcendentals=0),
        name="attend",
    )(x, docs)

def bwd_kernel(x_ref, g_ref, docs_ref, o_ref, lse_ref, e_ref, fm, tm, eq, ek, ev):
    pad = jnp.zeros((AUG - HD - IDS - 16, TOK), BF16)
    pad2 = jnp.zeros((AUG - HD - 16, TOK), BF16)
    row16 = lax.broadcasted_iota(jnp.int32, (16, TOK), 0)
    ones = jnp.where(row16 < 3, 1.0, 0.0).astype(BF16)
    def three(v):
        hi, mid, lo = split3(v)
        hi, mid, lo = hi.astype(F32), mid.astype(F32), lo.astype(F32)
        return jnp.where(row16 == 0, hi, jnp.where(row16 == 1, mid, jnp.where(row16 == 2, lo, 0.0))).astype(BF16)
    def load(s, _):
        x = x_ref[s]
        d = docs_ref[s]
        g = g_ref[s]
        dot = jnp.sum(g.astype(F32) * o_ref[s], axis=0, keepdims=True)
        low = three(lse_ref[s] * (-1.0 / C2))
        off = three(-dot)
        fm[s] = jnp.concatenate([
            x[0:HD], marks(d, False), low, pad,
            g, off, pad2,
            x[HD:2 * HD], marks(d, True), ones, pad,
            x[2 * HD:], ones, pad2], axis=0)
        return 0
    loop(SRC, load)
    pack_levels(fm)
    iden = eye(TOK)
    def turn(i, _):
        tm[i] = nt(iden, fm[i]).astype(BF16)
        return 0
    loop(30, turn); turn(30, 0)
    def segment(first, count):
        q = jnp.concatenate([fm[first + b, 0:AUG, :] for b in range(count)], axis=1)
        g = jnp.concatenate([fm[first + b, AUG:2 * AUG, :] for b in range(count)], axis=1)
        rows = pl.ds(first, count)
        qt = tm[rows, :, 0:AUG].reshape(count * TOK, AUG)
        gt = tm[rows, :, AUG:2 * AUG].reshape(count * TOK, AUG)
        parts = []
        for t in range(count):
            k = first + t
            p = jnp.exp2(nn(tm[k, :, 2 * AUG:3 * AUG], q) * C2)
            es = (p * nn(tm[k, :, 3 * AUG:], g)).astype(BF16)
            ev[k] = nn(p.astype(BF16), gt)
            ek[k] = nn(es, qt)
            parts.append(es)
        k = jnp.concatenate([fm[first + t, 2 * AUG:2 * AUG + HD, :] for t in range(count)], axis=1)
        out = nn(k, jnp.concatenate(parts, axis=0))
        for b in range(count):
            eq[first + b] = out[:, b * TOK:(b + 1) * TOK]
    loop(7, lambda i, _: segment(i * 4, 4), MAIN)
    segment(28, 2)
    segment(30, 1)

    for level in range(4, 0, -1):
        c = TOK >> level
        def join(g, _, level=level, c=c):
            child = FIRST[level] + g
            grid = spread_grid(c) if level > 1 else None
            for half in range(2):
                mine = FIRST[level - 1] + 2 * g + half
                got = eq[child, :, half * 128:half * 128 + 128]
                if level > 1:
                    eq[mine] += spread(got, grid)
                else:
                    eq[mine, :, 0:128] += got
                for s in range(128 // c):
                    ek[mine, 2 * c * s:2 * c * s + c, :] += ek[child, half * 128 + c * s:half * 128 + c * s + c, :]
                    ev[mine, 2 * c * s:2 * c * s + c, :] += ev[child, half * 128 + c * s:half * 128 + c * s + c, :]
            return 0
        loop(BLOCKS[level], join)
    small = (lax.broadcasted_iota(jnp.int32, (HD, AUG), 0) == lax.broadcasted_iota(jnp.int32, (HD, AUG), 1)).astype(BF16)
    def finish(s, _):
        a = (eq[s] * ROOT).astype(BF16)
        b = nt(small, (ek[s] * ROOT).astype(BF16)).astype(BF16)
        v = nt(small, ev[s].astype(BF16)).astype(BF16)
        e_ref[s] = jnp.concatenate([a, b, v], axis=0)
        return 0
    loop(SRC, finish)

def attn_bwd(x, g, docs, o, lse):
    return pl.pallas_call(
        bwd_kernel,
        out_shape=jax.ShapeDtypeStruct((SRC, 3 * HD, TOK), BF16),
        in_specs=[pl.BlockSpec(memory_space=pltpu.VMEM)] * 5,
        out_specs=pl.BlockSpec(memory_space=pltpu.VMEM),
        scratch_shapes=[
            pltpu.VMEM((31, 4 * AUG, TOK), BF16),
            pltpu.VMEM((31, TOK, 4 * AUG), BF16),
            pltpu.VMEM((31, HD, TOK), F32),
            pltpu.VMEM((31, TOK, AUG), F32),
            pltpu.VMEM((31, TOK, AUG), F32),
        ],
        compiler_params=pltpu.CompilerParams(vmem_limit_bytes=56 * 2**20),
        cost_estimate=pl.CostEstimate(flops=28 * 10**9, bytes_accessed=6 * 2**20, transcendentals=0),
        name="attend_back",
    )(x, g, docs, o, lse)


def layer_norm(values, gain_row, shift_row):
    center = values - jnp.mean(values, axis=-1, keepdims=True)
    scale = lax.rsqrt(jnp.mean(center * center, axis=-1, keepdims=True) + epsilon)
    unit = center * scale
    return unit, scale, (unit * gain_row + shift_row).astype(BF16)


def layer_norm_back(grad, unit, scale, gain_row):
    pulled = grad * gain_row
    return (
        pulled
        - jnp.mean(pulled, axis=-1, keepdims=True)
        - unit * jnp.mean(pulled * unit, axis=-1, keepdims=True)
    ) * scale


def gelu_parts(values):
    share = 0.5 * (1.0 + lax.erf(values * math.sqrt(0.5)))
    slope = share + values * jnp.exp(-0.5 * values * values) * (1.0 / math.sqrt(2 * math.pi))
    return (values * share).astype(BF16), slope


def head_order():
    block = np.array([int(f"{k:04b}"[::-1], 2) for k in range(16)])
    heads = np.arange(HEADS)[:, None, None]
    residue = (heads + block[None, :, None]) % 16
    return (np.arange(16)[None, None, :] * 16 + residue).reshape(HEADS, TOK)


def cube_forward(hidden, params, order, docs, trade):
    w_qkv, w_out, w_mlp, gains, biases, up_bias = params
    unit_one, scale_one, normed = layer_norm(hidden, gains[0], biases[0])
    mixed = jnp.einsum("df,td->ft", w_qkv, normed, preferred_element_type=F32)
    shift = jnp.concatenate([biases[1], jnp.zeros_like(biases[1]), biases[2]])
    mixed = (mixed + shift[:, None]).astype(BF16)
    mixed = mixed.reshape(3, HEADS, HEAD_DIM, TOK).transpose(1, 0, 2, 3).reshape(HEADS, 3 * HEAD_DIM, TOK)
    mixed = jnp.einsum("hft,htu->hfu", mixed, order, preferred_element_type=F32).astype(BF16)
    heads = trade(mixed)
    merged, merged_low, summary = attn_fwd(heads, docs)
    attended = trade(merged_low)
    attended = jnp.einsum("hdu,htu->hdt", attended, order, preferred_element_type=F32).astype(BF16)
    attended = attended.reshape(D, TOK)
    middle = hidden + jnp.einsum("ft,fd->td", attended, w_out, preferred_element_type=F32) + biases[3]
    unit_two, scale_two, normed_two = layer_norm(middle, gains[1], biases[4])
    ff = up_bias.shape[0]
    upward = jnp.dot(normed_two, w_mlp[:, :ff], preferred_element_type=F32) + up_bias
    activated, slope = gelu_parts(upward)
    result = middle + biases[5]
    for at in range(0, ff, D):
        result = result + jnp.dot(activated[:, at : at + D], w_mlp[:, ff + at : ff + at + D], preferred_element_type=F32)
    kept = (unit_one, scale_one, normed, heads, merged, summary, attended, unit_two, scale_two, normed_two, slope, activated)
    return result.astype(BF16), kept


def cube_backward(incoming_low, kept, params, order, docs, trade, before, between, along, send_rest):
    w_qkv, w_out, w_mlp, gains, biases, up_bias = params
    unit_one, scale_one, normed, heads, merged, summary, attended, unit_two, scale_two, normed_two, slope, activated = kept
    ff = up_bias.shape[0]
    incoming = incoming_low.astype(F32)
    act_grad = jnp.concatenate([
        jnp.einsum("tb,ab->ta", incoming_low, w_mlp[:, ff + at : ff + at + D], preferred_element_type=F32)
        for at in range(0, ff, D)
    ], axis=1)
    up_grad = (act_grad * slope).astype(BF16)
    norm_two_grad = jnp.einsum("tb,ab->ta", up_grad, w_mlp[:, :ff], preferred_element_type=F32)
    middle_grad = incoming + layer_norm_back(norm_two_grad, unit_two, scale_two, gains[1])
    branch_grad = middle_grad.astype(BF16)
    merged_grad = jnp.einsum("fd,td->ft", w_out, branch_grad, preferred_element_type=F32).astype(BF16)
    merged_grad = merged_grad.reshape(HEADS, HEAD_DIM, TOK)
    merged_grad = jnp.einsum("hdt,htu->hdu", merged_grad, order, preferred_element_type=F32).astype(BF16)
    grad_rest = jnp.concatenate(
        [inner_rows(normed_two, up_grad).astype(BF16)]
        + [inner_rows(activated[:, at : at + D], incoming_low).astype(BF16) for at in range(0, ff, D)]
        + [jnp.einsum("ft,td->fd", attended, branch_grad, preferred_element_type=F32).astype(BF16)],
        axis=1,
    )
    merged_grad = trade(merged_grad)
    merged_grad, grad_rest, before = lax.optimization_barrier((merged_grad, grad_rest, before))
    sums_rest = send_rest(grad_rest)
    back_heads = attn_bwd(heads, merged_grad, docs, merged, summary)
    mixed_grad = trade(back_heads)
    mixed_grad, before, along = lax.optimization_barrier((mixed_grad, between(before), along))
    mixed_grad = jnp.einsum("hfu,htu->hft", mixed_grad, order, preferred_element_type=F32).astype(BF16)
    mixed_grad = mixed_grad.reshape(HEADS, 3, HEAD_DIM, TOK).transpose(1, 0, 2, 3).reshape(3 * D, TOK)
    grad_qkv = jnp.einsum("td,ft->df", normed, mixed_grad, preferred_element_type=F32).astype(BF16)
    grad_shift = jnp.sum(mixed_grad.astype(F32), axis=1)
    normed_grad = jnp.einsum("ft,df->td", mixed_grad, w_qkv, preferred_element_type=F32)
    start_grad = middle_grad + layer_norm_back(normed_grad, unit_one, scale_one, gains[0])
    small = jnp.stack([
        jnp.sum(normed_grad * unit_one, axis=0),
        jnp.sum(norm_two_grad * unit_two, axis=0),
        jnp.sum(normed_grad, axis=0),
        grad_shift[:D],
        grad_shift[2 * D:],
        jnp.sum(branch_grad.astype(F32), axis=0),
        jnp.sum(norm_two_grad, axis=0),
        jnp.sum(incoming, axis=0),
    ])
    grad_up_bias = jnp.sum(up_grad.astype(F32), axis=0)
    return start_grad, (grad_qkv, sums_rest, small, grad_up_bias), before, along


def half_pairs(source, count):
    return [(source * count + j, (1 - source) * count + j) for j in range(count)]


def core_swap(value, bit):
    return lax.ppermute(value, "seq", [(j, j ^ (1 << bit)) for j in range(16)])


def section_swap(value):
    return lax.ppermute(value, "section", [(0, 1), (1, 0)])


def place_bit(bit):
    return (lax.axis_index("seq") >> bit) & 1


def team(kind):
    def device(x, z, y, c):
        return x * 16 + z * 4 + y * 2 + c
    two, four = range(2), range(4)
    if kind == "plane":
        return [[device(x, z, y, c) for x in two for y in two] for z in four for c in two]
    return [[device(x, z, y, c) for z in four] for x in two for y in two for c in two]


def team_trade(value, kind):
    return lax.all_to_all(value, ("section", "seq"), 0, 0, axis_index_groups=team(kind), tiled=True)


def collect_line(piece):
    return team_trade(jnp.broadcast_to(piece[None], (4,) + piece.shape), "line")


def collect_plane(now):
    rows, columns = now.shape[1:]
    now = team_trade(jnp.broadcast_to(now[None], (4,) + now.shape), "plane")
    now = now.reshape(2, 2, 4, rows, columns)
    got = core_swap(now, 0)
    upper = place_bit(0) == 1
    halves = []
    for x in range(2):
        a, b = now[x].transpose(1, 0, 2, 3), got[x].transpose(1, 0, 2, 3)
        both = jnp.stack([jnp.where(upper, b, a), jnp.where(upper, a, b)], axis=2)
        halves.append(both.reshape(16 * rows, columns))
    return halves


def plus(own, got, dtype=BF16):
    return (own.astype(F32) + got.astype(F32)).astype(dtype)


def fold(value, bit, axis, dtype=BF16):
    mine = place_bit(bit)
    away = lax.dynamic_index_in_dim(value, 1 - mine, axis, keepdims=False)
    kept = lax.dynamic_index_in_dim(value, mine, axis, keepdims=False)
    return plus(kept, core_swap(away, bit), dtype)


def reduce_core(partial):
    rows, half = partial.shape[0] // 16, partial.shape[1] // 2
    now = fold(partial.reshape(8, 2, rows, 2 * half), 0, 1).reshape(4, 2, rows, 2 * half)
    return jnp.stack([now[:, y, :, x * half : x * half + half] for x in range(2) for y in range(2)])


def reduce_plane(now):
    return jnp.sum(team_trade(now, "plane").astype(F32), axis=0).astype(BF16)


def reduce_line(now):
    return jnp.sum(team_trade(now, "line").astype(F32), axis=0)


def cube_body(inputs, cotangent, documents, w_qkv, w_out, w_up, w_down, norm_gains, biases, up_bias):
    section_id = lax.axis_index("section")
    place = lax.axis_index("seq")
    count = lax.axis_size("seq")
    half = count // 2
    micro_id = place // half
    member = section_id * half + place % half
    teams = [[s * count + k * half + j for s in range(2) for j in range(half)] for k in range(2)]
    axes = ("section", "seq")
    lower = section_id == 0

    def trade(value):
        return lax.all_to_all(value, axes, 0, 0, axis_index_groups=teams, tiled=True)

    def across(value, pairs):
        return lax.ppermute(value, axes, pairs)

    def own_rows(pair):
        mine = jnp.where(micro_id == 0, pair[0], pair[1])
        other = jnp.where(micro_id == 0, pair[1], pair[0])
        swap = across(other, [(count + j, count + (j ^ half)) for j in range(count)])
        return jnp.where(lower, mine, swap)

    table = jnp.asarray(head_order())
    order = (table[:, None, :] == jnp.arange(TOK)[None, :, None]).astype(BF16)
    docs = jnp.where(micro_id == 0, documents[0], documents[1]).reshape(count, TOK)
    docs = jnp.where(micro_id == 0, docs, jnp.roll(docs, half, axis=0))
    own_order = lax.dynamic_index_in_dim(order, member, 0, keepdims=False)
    docs = jnp.dot(docs.astype(BF16), own_order, preferred_element_type=F32).reshape(count, 1, TOK)

    hidden = own_rows(inputs)
    wide = D // count
    lift = up_bias[0].reshape(-1, wide)
    small = jnp.concatenate([norm_gains[0], biases[0], lift]).T.astype(BF16)
    small = jnp.pad(small, ((0, 0), (0, 128 - small.shape[1])))

    ff = w_up.shape[2]
    low_qkv = w_qkv[0].astype(BF16)
    columns = low_qkv.shape[1] // 2
    got = across(low_qkv[:, columns:], half_pairs(0, count))
    piece = jnp.where(lower, low_qkv[:, :columns], got)
    line = collect_line(jnp.concatenate([piece, small], axis=1))
    parts = collect_plane(line)
    qkv_first = jnp.concatenate([part[:, :columns] for part in parts], axis=1)

    piece, w_up, w_down = lax.optimization_barrier((piece, w_up, w_down))
    up_shard = w_up[0].astype(BF16).reshape(wide, count, 4, wide).transpose(0, 2, 1, 3).reshape(wide, ff)
    down_shard = w_down[0].astype(BF16).reshape(4, wide, D).transpose(1, 0, 2).reshape(wide, 4 * D)
    shard = jnp.concatenate([up_shard, down_shard, w_out[0].astype(BF16), low_qkv], axis=1)
    rows, rest = wide // 2, 2 * ff + D
    got = section_swap(jnp.where(lower, shard[rows:], shard[:rows]))
    near = jnp.concatenate([jnp.where(lower, shard[:rows, :rest], got[:, :rest]), jnp.where(lower, got, shard[rows:])[:, rest:]], axis=1)
    far = jnp.where(lower, got[:, :rest], shard[rows:, :rest])
    near, far, line = lax.optimization_barrier((near, far, line))
    near = lax.all_gather(near, ("seq", "section"), axis=0, tiled=True)
    rest_final = lax.all_gather(far, ("seq", "section"), axis=0, tiled=True)
    rest_first, qkv_final = near[:, :rest], near[:, rest:]

    def lines(columns):
        values = columns[:, :12].astype(F32).T
        return values[:2], values[2:8], values[8:].reshape(ff)

    lines_first, lines_final = lines(parts[0][:, columns:]), lines(parts[1][:, columns:])
    params_first = (qkv_first, rest_first[:, 2 * ff :], rest_first) + lines_first
    params_final = (qkv_final, rest_final[:, 2 * ff :], rest_final) + lines_final
    first, kept_first = cube_forward(hidden.astype(F32), params_first, order, docs, trade)
    final, kept_final = cube_forward(first.astype(F32), params_final, order, docs, trade)
    def shared_out(value_first, value_final):
        far = across(value_first, [(count + j, j ^ half) for j in range(count)])
        near = across(value_final, half_pairs(0, count))
        beside = across(value_final, [(count + j, count + (j ^ half)) for j in range(count)])
        return far, near, beside

    def placed(mine, other):
        return jnp.where(micro_id == 0, jnp.stack([mine, other]), jnp.stack([other, mine]))[None]

    def scattered(partial):
        return lax.psum_scatter(partial, ("seq", "section"), scatter_dimension=0, tiled=True)

    start_back, merged = lax.optimization_barrier((own_rows(cotangent), kept_final[4]))
    kept_final = kept_final[:4] + (merged,) + kept_final[5:]
    grad_final, terms_final, _, _ = cube_backward(
        start_back, kept_final, params_final, order, docs, trade, None, lambda now: now, None, scattered
    )
    rest_final = terms_final[1]
    sent, qkv_final = lax.optimization_barrier((grad_final.astype(BF16), terms_final[0]))
    near = across(sent, half_pairs(0, count))
    beside = across(sent, [(count + j, count + (j ^ half)) for j in range(count)])
    grad_first, terms_first, qkv_final, along = cube_backward(
        sent, kept_first, params_first, order, docs, trade,
        reduce_core(qkv_final), reduce_plane, (rest_final, shared_out(first, final), near, beside), scattered,
    )
    rest_final, outs, near, beside = along

    def upright(rows, wide_row):
        return jnp.concatenate([rows, wide_row.reshape(4, D)]).T

    smalls = jnp.concatenate([upright(*terms_first[2:]), upright(*terms_final[2:])], axis=1)
    smalls = fold(smalls.reshape(8, 2, wide, 24), 0, 1).reshape(4, 2, wide, 24)
    smalls = jnp.stack([smalls[:, 0], smalls[:, 1]] * 2)
    smalls = jnp.pad(smalls, ((0, 0), (0, 0), (0, 0), (0, 128 - 24)))
    now = jnp.concatenate([reduce_core(terms_first[0]), smalls], axis=3)
    now = reduce_line(reduce_plane(now))
    qkv_first, smalls = now[:, :-128], now[:, -128:-104]
    smalls = jnp.where(lower, smalls[:, :12], smalls[:, 12:]).T
    qkv_final = reduce_line(qkv_final)
    rest_first = terms_first[1]
    backs = across(grad_first.astype(BF16), [(count + j, j ^ half) for j in range(count)]), near, beside
    far, near, beside = outs
    layer_outputs = placed(jnp.where(lower, first, near), jnp.where(lower, far, beside))
    far, near, beside = backs
    input_grads = placed(
        jnp.where(lower, grad_first, near.astype(F32)), jnp.where(lower, far, beside).astype(F32)
    )

    away = section_swap(jnp.where(lower, rest_final, rest_first))
    rest = jnp.where(
        lower, jnp.concatenate([rest_first, away]), jnp.concatenate([away, rest_final])
    ).astype(F32)
    away = section_swap(jnp.where(lower, qkv_final, qkv_first).astype(BF16)).astype(F32)
    qkv = jnp.where(
        lower, jnp.concatenate([qkv_first, away], axis=1), jnp.concatenate([away, qkv_final], axis=1)
    )
    up = rest[:, :ff].reshape(wide, 4, count, wide).transpose(0, 2, 1, 3).reshape(wide, ff)
    down = rest[:, ff : 2 * ff].reshape(wide, 4, D).transpose(1, 0, 2).reshape(4 * wide, D)
    return (
        layer_outputs,
        input_grads,
        qkv[None],
        rest[None, :, 2 * ff :],
        up[None],
        down[None],
        smalls[None, :2],
        smalls[None, 2:8],
        smalls[8:].reshape(1, -1),
    )


def solution(mesh):
    cube = mesh.shape["seq"] == 16
    return jax.shard_map(
        cube_body if cube else body,
        mesh=mesh,
        in_specs=(
            P(None, "seq", None),
            P(None, "seq", None),
            P(),
            P("section", "seq", None),
            P("section", "seq", None),
            P("section", "seq", None),
            P("section", "seq", None),
            P("section", None, "seq"),
            P("section", None, "seq"),
            P("section", "seq"),
        ),
        out_specs=(
            P("section", None, "seq", None),
            P("section", None, "seq", None),
            P("section", "seq", None),
            P("section", "seq", None),
            P("section", "seq", None),
            P("section", "seq", None),
            P("section", None, "seq"),
            P("section", None, "seq"),
            P("section", "seq"),
        ),
        check_vma=False,
    )
```

```python
import functools
import math

import jax
import jax.numpy as jnp
import numpy as np
from jax import lax
from jax.experimental import pallas as pl
from jax.experimental.pallas import tpu as pltpu
from jax.sharding import PartitionSpec as P

D = 768
HEADS = 16
HEAD_DIM = 48
SEG0 = 1024
BRANCHES = 5


epsilon = 1e-05
masked_score = -1e30
highest = lax.Precision.HIGHEST


def swapped(value, axis, apart):
    mask = 2**apart
    pairs = [(source, source ^ mask) for source in range(lax.axis_size(axis))]
    return lax.ppermute(value, axis, pairs)


def for_sending(array):
    return jax.tree.map(lambda a: a.astype(jnp.bfloat16) if a.dtype == jnp.float32 else a, array)


def passed_along(array, axis, by):
    peers = lax.axis_size(axis)
    pairs = [(i, i + by) for i in range(peers) if 0 <= i + by < peers]
    return lax.ppermute(array, axis, pairs)


def layer_norm_parts(values, gain_row, shift_row):
    center = values - jnp.mean(values, axis=-1, keepdims=True)
    spread = jnp.mean(center * center, axis=-1, keepdims=True)
    return center * lax.rsqrt(spread + epsilon) * gain_row + shift_row


def exact_gelu(values):
    return jax.nn.gelu(values, approximate=False)


def inner_rows(left, right):
    return jnp.einsum("ta,tb->ab", left, right, preferred_element_type=jnp.float32)


def geometry(tokens_dev, devices):
    groups = [
        min(SEG0 * 2**level_id, tokens_dev * devices) // tokens_dev for level_id in range(BRANCHES)
    ]
    return (groups, max(groups).bit_length() - 1)


def first_level(groups, step_id):
    return min((level_id for level_id in range(BRANCHES) if groups[level_id] > 2**step_id))


def pick_grid(level_id, dtype):
    dilation = 2**level_id
    return (jnp.arange(dilation)[:, None] == (jnp.arange(HEADS) % dilation)[None, :]).astype(dtype)


def select_rows(tensor, level_id):
    dilation = 2**level_id
    shaped = tensor.reshape((tensor.shape[0] // dilation, dilation) + tensor.shape[1:])
    if tensor.dtype == jnp.bfloat16:
        chosen = jnp.einsum(
            "jrh...,rh->jh...",
            shaped,
            pick_grid(level_id, jnp.bfloat16),
            preferred_element_type=jnp.float32,
        )
        return chosen.astype(jnp.bfloat16)
    return jnp.einsum(
        "jrh...,rh->jh...", shaped, pick_grid(level_id, jnp.float32), precision=highest
    )


def spread_rows(tensor, level_id):
    dilation = 2**level_id
    spread = jnp.einsum(
        "jh...,rh->jrh...", tensor, pick_grid(level_id, jnp.float32), precision=highest
    )
    return spread.reshape((tensor.shape[0] * dilation,) + tensor.shape[1:])


def spread_sums(tensor, level_id):
    dilation = 2**level_id
    grid = pick_grid(level_id, jnp.float32)
    spread = jnp.where(grid[None] > 0, tensor[:, None, :], masked_score)
    return spread.reshape(tensor.shape[0] * dilation, HEADS)


def doc_tables(documents_now, level_id, group, tokens_dev, seq_place):
    dilation = 2**level_id
    offsets = np.arange(HEADS) % dilation
    own_docs = lax.dynamic_slice_in_dim(documents_now, seq_place * tokens_dev, tokens_dev)
    own_docs = own_docs.reshape(tokens_dev // dilation, dilation)[:, offsets]
    seg_start = seq_place // group * group * tokens_dev
    seg_docs = lax.dynamic_slice_in_dim(documents_now, seg_start, group * tokens_dev)
    seg_docs = seg_docs.reshape(group * tokens_dev // dilation, dilation)[:, offsets]
    return (own_docs, seg_docs)


def head_bits(level_id):
    return jnp.arange(HEADS) >> level_id & 1


def halve(buffer, level_id):
    pairs = buffer.reshape(buffer.shape[0], buffer.shape[1] // 2, 2, HEADS, HEAD_DIM)
    chosen = head_bits(level_id)[None, None, :, None] == 1
    return jnp.where(chosen, pairs[:, :, 1], pairs[:, :, 0])


def widen(buffer, level_id):
    chosen = head_bits(level_id)[None, None, :, None] == 1
    empty = jnp.zeros_like(buffer)
    upper_part = jnp.where(chosen, buffer, empty)
    lower_part = jnp.where(chosen, empty, buffer)
    stacked = jnp.stack([lower_part, upper_part], axis=2)
    return stacked.reshape(buffer.shape[0], buffer.shape[1] * 2, HEADS, HEAD_DIM)


def thin_to(buffer, low_level, high_level):
    for level_id in range(low_level, high_level):
        buffer = halve(buffer, level_id)
    return buffer


def widen_to(buffer, low_level, high_level):
    for level_id in reversed(range(low_level, high_level)):
        buffer = widen(buffer, level_id)
    return buffer


def gather_keys(own_rows, groups, step_count, seq_place):
    results = [None] * BRANCHES
    current = own_rows
    level_now = 0
    for level_id in range(BRANCHES):
        pass
    for step_id in range(step_count):
        target = first_level(groups, step_id)
        current = thin_to(current, level_now, target)
        level_now = target
        row_count = current.shape[1]
        flat_rows = current.reshape(2, row_count, HEADS * HEAD_DIM)
        incoming = swapped(flat_rows, "seq", step_id).reshape(current.shape)
        upper_half = seq_place >> step_id & 1 == 1
        current = jnp.where(
            upper_half,
            jnp.concatenate([incoming, current], axis=1),
            jnp.concatenate([current, incoming], axis=1),
        )
        for level_id in range(BRANCHES):
            if groups[level_id] == 2 ** (step_id + 1):
                results[level_id] = thin_to(current, level_now, level_id)
    return results


def scatter_keys(key_grads, groups, step_count, seq_place):
    carried = None
    for step_id in reversed(range(step_count)):
        level_now = first_level(groups, step_id)
        total_grad = None
        if carried is not None:
            total_grad = widen_to(carried, level_now, first_level(groups, step_id + 1))
        for level_id in range(BRANCHES):
            if groups[level_id] == 2 ** (step_id + 1):
                branch_term = widen_to(key_grads[level_id], level_now, level_id)
                total_grad = branch_term if total_grad is None else total_grad + branch_term
        half_rows = total_grad.shape[1] // 2
        upper_half = seq_place >> step_id & 1 == 1
        own_half = jnp.where(upper_half, total_grad[:, half_rows:], total_grad[:, :half_rows])
        theirs = jnp.where(upper_half, total_grad[:, :half_rows], total_grad[:, half_rows:])
        flat_rows = theirs.reshape(2, half_rows, HEADS * HEAD_DIM)
        incoming = (
            swapped(for_sending(flat_rows), "seq", step_id)
            .astype(flat_rows.dtype)
            .reshape(own_half.shape)
        )
        carried = own_half + incoming
    own_grad = widen_to(carried, 0, first_level(groups, 0))
    for level_id in range(BRANCHES):
        pass
    return own_grad


def head_blocks(level_id):
    block_size = min(HEADS, 4 * 2**level_id)
    return (HEADS // block_size, block_size)


def to_blocks(tensor, block_count, block_size):
    moved = jnp.moveaxis(tensor, 1, 0)
    return moved.reshape((block_count, block_size) + moved.shape[1:])


def from_blocks(tensor):
    joined = tensor.reshape((tensor.shape[0] * tensor.shape[1],) + tensor.shape[2:])
    return jnp.moveaxis(joined, 0, 1)


def score_block(query_block, key_block, query_doc, key_doc):
    scores = jnp.einsum(
        "hqd,hkd->hqk", query_block, key_block, preferred_element_type=jnp.float32
    ) * HEAD_DIM ** (-0.5)
    return jnp.where(query_doc[:, :, None] == key_doc[:, None, :], scores, masked_score)


def forward_block(pieces):
    query_block, key_block, value_block, query_doc, key_doc = pieces
    scores = score_block(query_block, key_block, query_doc, key_doc)
    row_max = jnp.max(scores, axis=-1, keepdims=True)
    weights = jnp.exp(scores - row_max)
    row_total = jnp.sum(weights, axis=-1, keepdims=True)
    prob_rows = (weights / row_total).astype(jnp.bfloat16)
    result = jnp.einsum("hqk,hkd->hqd", prob_rows, value_block, preferred_element_type=jnp.float32)
    return (result, (row_max + jnp.log(row_total))[:, :, 0])


def backward_block(pieces):
    query_block, key_block, value_block, query_doc, key_doc, summary, out_grad, summary_grad = (
        pieces
    )
    scores = score_block(query_block, key_block, query_doc, key_doc)
    prob_rows = jnp.exp(scores - summary[:, :, None])
    prob_grad = jnp.einsum(
        "hqd,hkd->hqk", out_grad, value_block, preferred_element_type=jnp.float32
    )
    score_grad = prob_rows * (
        prob_grad
        - jnp.sum(prob_rows * prob_grad, axis=-1, keepdims=True)
        + summary_grad[:, :, None]
    )
    score_grad = score_grad.astype(jnp.bfloat16)
    score_scale = HEAD_DIM ** (-0.5)
    query_grad = (
        jnp.einsum("hqk,hkd->hqd", score_grad, key_block, preferred_element_type=jnp.float32)
        * score_scale
    )
    key_grad = (
        jnp.einsum("hqk,hqd->hkd", score_grad, query_block, preferred_element_type=jnp.float32)
        * score_scale
    )
    value_grad = jnp.einsum(
        "hqk,hqd->hkd", prob_rows.astype(jnp.bfloat16), out_grad, preferred_element_type=jnp.float32
    )
    return (query_grad, key_grad, value_grad)


def branch_forward(query_sel, key_value, query_docs, key_docs, level_id):
    block_count, block_size = head_blocks(level_id)
    pieces = (
        to_blocks(query_sel, block_count, block_size),
        to_blocks(key_value[0], block_count, block_size),
        to_blocks(key_value[1], block_count, block_size),
        to_blocks(query_docs, block_count, block_size),
        to_blocks(key_docs, block_count, block_size),
    )
    results, summaries = lax.map(forward_block, pieces)
    return (from_blocks(results), from_blocks(summaries))


def branch_backward(
    query_sel, key_value, query_docs, key_docs, summary, out_grad, summary_grad, level_id
):
    block_count, block_size = head_blocks(level_id)
    pieces = (
        to_blocks(query_sel, block_count, block_size),
        to_blocks(key_value[0], block_count, block_size),
        to_blocks(key_value[1], block_count, block_size),
        to_blocks(query_docs, block_count, block_size),
        to_blocks(key_docs, block_count, block_size),
        to_blocks(summary, block_count, block_size),
        to_blocks(out_grad, block_count, block_size),
        to_blocks(summary_grad, block_count, block_size),
    )
    query_grad, key_grad, value_grad = lax.map(backward_block, pieces)
    return (from_blocks(query_grad), jnp.stack([from_blocks(key_grad), from_blocks(value_grad)]))


def layer_forward(hidden, params, documents_now, groups, step_count, seq_place):
    w_qkv, w_out, w_up, w_down, gains, biases, up_bias = params
    gains = gains.astype(jnp.float32)
    biases = biases.astype(jnp.float32)
    tokens_dev = hidden.shape[0]
    normed = layer_norm_parts(hidden, gains[0], biases[0]).astype(jnp.bfloat16)
    mixed_rows = jnp.dot(normed, w_qkv, preferred_element_type=jnp.float32)
    queries = (mixed_rows[:, :D] + biases[1]).astype(jnp.bfloat16)
    key_part = mixed_rows[:, D : 2 * D].astype(jnp.bfloat16)
    values = (mixed_rows[:, 2 * D :] + biases[2]).astype(jnp.bfloat16)
    own_rows = jnp.stack([key_part, values]).reshape(2, tokens_dev, HEADS, HEAD_DIM)
    gathered = gather_keys(own_rows, groups, step_count, seq_place)
    query_heads = queries.reshape(tokens_dev, HEADS, HEAD_DIM)
    picked, branch_outs, branch_sums = ([], [], [])
    for level_id in range(BRANCHES):
        query_sel = select_rows(query_heads, level_id)
        query_docs, key_docs = doc_tables(
            documents_now, level_id, groups[level_id], tokens_dev, seq_place
        )
        result, summary = branch_forward(
            query_sel, gathered[level_id], query_docs, key_docs, level_id
        )
        picked.append(query_sel)
        branch_outs.append(result)
        branch_sums.append(summary)
    full_sums = jnp.stack(
        [spread_sums(branch_sums[level_id], level_id) for level_id in range(BRANCHES)]
    )
    row_max = jnp.max(full_sums, axis=0)
    shares = jnp.exp(full_sums - row_max)
    shares = shares / jnp.sum(shares, axis=0)
    merged = sum(
        (
            shares[level_id][:, :, None] * spread_rows(branch_outs[level_id], level_id)
            for level_id in range(BRANCHES)
        )
    )
    attended = merged.reshape(tokens_dev, D).astype(jnp.bfloat16)
    middle = hidden + jnp.dot(attended, w_out, preferred_element_type=jnp.float32) + biases[3]
    normed_two = layer_norm_parts(middle, gains[1], biases[4]).astype(jnp.bfloat16)
    upward = jnp.dot(normed_two, w_up, preferred_element_type=jnp.float32) + up_bias.astype(
        jnp.float32
    )
    activated = exact_gelu(upward).astype(jnp.bfloat16)
    result = middle + jnp.dot(activated, w_down, preferred_element_type=jnp.float32) + biases[5]
    kept_values = (
        hidden,
        normed,
        picked,
        gathered,
        branch_sums,
        branch_outs,
        shares,
        merged,
        attended,
        middle,
        normed_two,
        upward,
        activated,
    )
    return (result, kept_values)


def layer_backward(incoming, kept_values, params, documents_now, groups, step_count, seq_place):
    w_qkv, w_out, w_up, w_down, gains, biases, up_bias = params
    gains = gains.astype(jnp.float32)
    biases = biases.astype(jnp.float32)
    (
        hidden,
        normed,
        picked,
        gathered,
        branch_sums,
        branch_outs,
        shares,
        merged,
        attended,
        middle,
        normed_two,
        upward,
        activated,
    ) = kept_values
    tokens_dev = hidden.shape[0]
    down_grad = incoming.astype(jnp.bfloat16)
    grad_down = inner_rows(activated, down_grad)
    grad_bias_down = jnp.sum(down_grad.astype(jnp.float32), axis=0)
    act_grad = jnp.einsum("tb,ab->ta", down_grad, w_down, preferred_element_type=jnp.float32)
    gelu_pulled = jax.vjp(exact_gelu, upward)
    up_grad = gelu_pulled[1](act_grad)[0].astype(jnp.bfloat16)
    grad_up = inner_rows(normed_two, up_grad)
    grad_up_bias = jnp.sum(up_grad.astype(jnp.float32), axis=0)
    norm_two_grad = jnp.einsum("tb,ab->ta", up_grad, w_up, preferred_element_type=jnp.float32)
    norm_pulled = jax.vjp(layer_norm_parts, middle, gains[1], biases[4])
    middle_part, grad_gain_two, grad_shift_two = norm_pulled[1](norm_two_grad)
    middle_grad = incoming + middle_part
    branch_grad = middle_grad.astype(jnp.bfloat16)
    grad_out = inner_rows(attended, branch_grad)
    grad_bias_out = jnp.sum(branch_grad.astype(jnp.float32), axis=0)
    merged_grad = jnp.einsum("tb,ab->ta", branch_grad, w_out, preferred_element_type=jnp.float32)
    merged_grad = merged_grad.reshape(tokens_dev, HEADS, HEAD_DIM)
    query_grad = jnp.zeros((tokens_dev, HEADS, HEAD_DIM), jnp.float32)
    key_grads = []
    for level_id in range(BRANCHES):
        share_sel = select_rows(shares[level_id], level_id)
        merged_sel = select_rows(merged, level_id)
        grad_sel = select_rows(merged_grad, level_id)
        out_grad = (share_sel[:, :, None] * grad_sel).astype(jnp.bfloat16)
        summary_grad = share_sel * (
            jnp.sum(grad_sel * branch_outs[level_id], axis=-1)
            - jnp.sum(grad_sel * merged_sel, axis=-1)
        )
        query_docs, key_docs = doc_tables(
            documents_now, level_id, groups[level_id], tokens_dev, seq_place
        )
        query_part, key_value_grad = branch_backward(
            picked[level_id],
            gathered[level_id],
            query_docs,
            key_docs,
            branch_sums[level_id],
            out_grad,
            summary_grad,
            level_id,
        )
        query_grad = query_grad + spread_rows(query_part, level_id)
        key_grads.append(key_value_grad)
    own_grad = scatter_keys(key_grads, groups, step_count, seq_place)
    mixed_grad = jnp.concatenate(
        [
            query_grad.reshape(tokens_dev, D),
            own_grad[0].reshape(tokens_dev, D),
            own_grad[1].reshape(tokens_dev, D),
        ],
        axis=1,
    ).astype(jnp.bfloat16)
    grad_qkv = inner_rows(normed, mixed_grad)
    grad_bias_query = jnp.sum(mixed_grad[:, :D].astype(jnp.float32), axis=0)
    grad_bias_value = jnp.sum(mixed_grad[:, 2 * D :].astype(jnp.float32), axis=0)
    normed_grad = jnp.einsum("tb,ab->ta", mixed_grad, w_qkv, preferred_element_type=jnp.float32)
    norm_pulled = jax.vjp(layer_norm_parts, hidden, gains[0], biases[0])
    hidden_part, grad_gain_one, grad_shift_one = norm_pulled[1](normed_grad)
    start_grad = middle_grad + hidden_part
    gradients = (
        grad_qkv,
        grad_out,
        grad_up,
        grad_down,
        jnp.stack([grad_gain_one, grad_gain_two]),
        jnp.stack(
            [
                grad_shift_one,
                grad_bias_query,
                grad_bias_value,
                grad_bias_out,
                grad_shift_two,
                grad_bias_down,
            ]
        ),
        grad_up_bias,
    )
    return (start_grad, gradients)


def body(inputs, cotangent, documents, w_qkv, w_out, w_up, w_down, norm_gains, biases, up_bias):
    section_id = lax.axis_index("section")
    seq_place = lax.axis_index("seq")
    devices = lax.axis_size("seq")
    micro = inputs.shape[0]
    tokens_dev = inputs.shape[1]
    groups, step_count = geometry(tokens_dev, devices)
    params = (
        lax.all_gather(w_qkv[0].astype(jnp.bfloat16), "seq", axis=0, tiled=True),
        lax.all_gather(w_out[0].astype(jnp.bfloat16), "seq", axis=0, tiled=True),
        lax.all_gather(w_up[0].astype(jnp.bfloat16), "seq", axis=0, tiled=True),
        lax.all_gather(w_down[0].astype(jnp.bfloat16), "seq", axis=0, tiled=True),
        lax.all_gather(norm_gains[0].astype(jnp.bfloat16), "seq", axis=1, tiled=True),
        lax.all_gather(biases[0].astype(jnp.bfloat16), "seq", axis=1, tiled=True),
        lax.all_gather(up_bias[0].astype(jnp.bfloat16), "seq", axis=0, tiled=True),
    )
    empty_rows = jnp.zeros((tokens_dev, D), jnp.bfloat16)
    received = empty_rows
    saved = []
    produced = []
    for tick_id in range(micro + 1):
        batch_index = jnp.clip(tick_id - section_id, 0, micro - 1)
        documents_now = lax.dynamic_index_in_dim(documents, batch_index, 0, keepdims=False)
        fresh_rows = inputs[tick_id] if tick_id < micro else empty_rows
        start_rows = jnp.where(section_id == 0, fresh_rows, received).astype(jnp.float32)
        result, kept_values = layer_forward(
            start_rows, params, documents_now, groups, step_count, seq_place
        )
        sent_rows = result.astype(jnp.bfloat16)
        produced.append(sent_rows)
        saved.append((kept_values, documents_now))
        if tick_id < micro:
            received = passed_along(sent_rows, "section", 1)
    back_received = empty_rows
    start_grads = []
    sent_grads = []
    totals = None
    shards = None
    for tick_id in range(micro + 1):
        earlier_save = saved[max(tick_id - 1, 0)]
        later_save = saved[min(tick_id + 1, micro)]
        kept_values, documents_now = jax.tree.map(
            lambda earlier, latter: jnp.where(section_id == 0, earlier, latter),
            earlier_save,
            later_save,
        )
        fresh_rows = cotangent[tick_id] if tick_id < micro else empty_rows
        incoming = jnp.where(section_id == 1, fresh_rows, back_received).astype(jnp.float32)
        start_grad, gradients = layer_backward(
            incoming, kept_values, params, documents_now, groups, step_count, seq_place
        )
        sent_rows = start_grad.astype(jnp.bfloat16)
        start_grads.append(start_grad)
        sent_grads.append(sent_rows.astype(jnp.float32))
        if tick_id < micro:
            back_received = passed_along(sent_rows, "section", -1)
        totals = (
            list(gradients)
            if totals is None
            else [earlier + latter for earlier, latter in zip(totals, gradients)]
        )
    shards = (
        lax.psum_scatter(totals[0], "seq", scatter_dimension=0, tiled=True),
        lax.psum_scatter(totals[1], "seq", scatter_dimension=0, tiled=True),
        lax.psum_scatter(totals[2], "seq", scatter_dimension=0, tiled=True),
        lax.psum_scatter(totals[3], "seq", scatter_dimension=0, tiled=True),
        lax.psum_scatter(totals[4], "seq", scatter_dimension=1, tiled=True),
        lax.psum_scatter(totals[5], "seq", scatter_dimension=1, tiled=True),
        lax.psum_scatter(totals[6], "seq", scatter_dimension=0, tiled=True),
    )
    layer_outputs = jnp.stack(
        [
            jnp.where(section_id == 0, produced[batch_id], produced[batch_id + 1])
            for batch_id in range(micro)
        ]
    )[None]
    input_grads = jnp.stack(
        [
            jnp.where(section_id == 0, start_grads[batch_id + 1], sent_grads[batch_id])
            for batch_id in range(micro)
        ]
    )[None]
    return (
        layer_outputs,
        input_grads,
        shards[0][None],
        shards[1][None],
        shards[2][None],
        shards[3][None],
        shards[4][None],
        shards[5][None],
        shards[6][None],
    )


HD = 48
AUG = 128
IDS = 32
SRC = 16
TOK = 256
ROOT = HD ** -0.5
C2 = ROOT * math.log2(math.e)
AWAY = -(2.0 ** 100)
BLOCKS = (16, 8, 4, 2, 1)
FIRST = (0, 16, 24, 28, 30)
F32, BF16 = jnp.float32, jnp.bfloat16

UN = 16
MAIN = 1
QW = 4
TWO = False

def loop(n, f, u=None):
    u = min(u or UN, n)
    while n % u:
        u -= 1
    def many(i, _):
        for j in range(u):
            f(i * u + j, 0)
        return 0
    lax.fori_loop(0, n // u, many, 0)

def nt(a, b):
    return lax.dot_general(a, b, (((1,), (1,)), ((), ())), preferred_element_type=F32)

def nn(a, b):
    return jnp.dot(a, b, preferred_element_type=F32)

def eye(n):
    return (lax.broadcasted_iota(jnp.int32, (n, n), 0) == lax.broadcasted_iota(jnp.int32, (n, n), 1)).astype(BF16)

def pack_grid(c):
    col = lax.broadcasted_iota(jnp.int32, (256, 128), 1)
    row = lax.broadcasted_iota(jnp.int32, (256, 128), 0)
    return (row == (col // c) * (2 * c) + col % c).astype(BF16)

def spread_grid(c):
    row = lax.broadcasted_iota(jnp.int32, (128, 256), 0)
    col = lax.broadcasted_iota(jnp.int32, (128, 256), 1)
    return (col == (row // c) * (2 * c) + row % c).astype(BF16)

def split3(v):
    hi = v.astype(BF16)
    r = v - hi.astype(F32)
    mid = r.astype(BF16)
    lo = (r - mid.astype(F32)).astype(BF16)
    return hi, mid, lo

def spread(v, grid):
    hi, mid, lo = split3(v)
    return nn(hi, grid) + nn(mid, grid) + nn(lo, grid)

def pack_levels(stack):
    for level in range(1, 5):
        c = TOK >> level
        def step(g, _, level=level, c=c):
            a = stack[FIRST[level - 1] + 2 * g]
            b = stack[FIRST[level - 1] + 2 * g + 1]
            if level == 1:
                pa, pb = a[:, :128], b[:, :128]
            else:
                grid = pack_grid(c)
                pa, pb = nn(a, grid).astype(BF16), nn(b, grid).astype(BF16)
            stack[FIRST[level] + g] = jnp.concatenate([pa, pb], axis=1)
            return 0
        loop(BLOCKS[level], step)

def marks(doc_row, away):
    ids = lax.broadcasted_iota(jnp.int32, (IDS, TOK), 0).astype(F32)
    same = ids == doc_row
    return (jnp.where(same, 0.0, AWAY) if away else jnp.where(same, 1.0, 0.0)).astype(BF16)

def fwd_kernel(x_ref, docs_ref, o_ref, ob_ref, lse_ref, fm, ktm, part, *, kc):
    pad = jnp.zeros((AUG - HD - IDS, TOK), BF16)
    def load(s, _):
        x = x_ref[s]
        d = docs_ref[s]
        fm[s] = jnp.concatenate([x[0:HD], marks(d, False), pad, x[HD:2 * HD], marks(d, True), pad, x[2 * HD:]], axis=0)
        return 0
    loop(SRC, load)
    pack_levels(fm)
    iden = eye(TOK)
    def turn(i, _):
        ktm[i] = nt(iden, fm[i, AUG:2 * AUG, :]).astype(BF16)
        return 0
    loop(30, turn); turn(30, 0)

    def segment(first, count):
        for at in range(0, count, QW):
            n = min(QW, count - at)
            q = jnp.concatenate([fm[first + at + b, 0:AUG, :] for b in range(n)], axis=1)
            scores = [nn(ktm[first + t], q) for t in range(count)]
            top = functools.reduce(jnp.maximum, [jnp.max(x, axis=0, keepdims=True) for x in scores])
            ps = [jnp.exp2((x - top) * C2) for x in scores]
            total = functools.reduce(jnp.add, [jnp.sum(p, axis=0, keepdims=True) for p in ps])
            p = jnp.concatenate([p.astype(BF16) for p in ps], axis=0)
            v = jnp.concatenate([fm[first + t, 2 * AUG:2 * AUG + HD, :] for t in range(count)], axis=1)
            out = nn(v, p)
            for b in range(n):
                part[first + at + b, 0:HD] = out[:, b * TOK:(b + 1) * TOK]
                part[first + at + b, HD:HD + 8] = jnp.broadcast_to(total[:, b * TOK:(b + 1) * TOK], (8, TOK))
                part[first + at + b, HD + 8:HD + 16] = jnp.broadcast_to(top[:, b * TOK:(b + 1) * TOK] * C2, (8, TOK))
    loop(7, lambda i, _: segment(i * 4, 4), MAIN)
    segment(28, 2)
    segment(30, 1)

    for level in range(4, 0, -1):
        c = TOK >> level
        def join(g, _, level=level, c=c):
            child = FIRST[level] + g
            grid = spread_grid(c) if level > 1 else None
            for half in range(2):
                mine = FIRST[level - 1] + 2 * g + half
                got = part[child, :, half * 128:half * 128 + 128]
                if level > 1:
                    got = spread(got, grid)
                else:
                    got = jnp.concatenate([got, jnp.zeros_like(got)], axis=1)
                own = part[mine]
                cl, cm = got[HD:HD + 1], got[HD + 8:HD + 9]
                cm = jnp.where(cl > 0, cm, AWAY)
                ol, om = own[HD:HD + 1], own[HD + 8:HD + 9]
                top = jnp.maximum(cm, om)
                wc, wo = jnp.exp2(cm - top), jnp.exp2(om - top)
                part[mine, 0:HD] = got[0:HD] * wc + own[0:HD] * wo
                part[mine, HD:HD + 8] = jnp.broadcast_to(cl * wc + ol * wo, (8, TOK))
                part[mine, HD + 8:HD + 16] = jnp.broadcast_to(top, (8, TOK))
            return 0
        loop(BLOCKS[level], join)
    def finish(s, _):
        own = part[s]
        l, m = own[HD:HD + 1], own[HD + 8:HD + 9]
        out = own[0:HD] / l
        o_ref[s] = out
        ob_ref[s] = out.astype(BF16)
        lse_ref[s] = m + jnp.log2(l)
        return 0
    loop(SRC, finish)

def attn_fwd(x, docs):
    return pl.pallas_call(
        functools.partial(fwd_kernel, kc=256),
        out_shape=(jax.ShapeDtypeStruct((SRC, HD, TOK), F32), jax.ShapeDtypeStruct((SRC, HD, TOK), BF16), jax.ShapeDtypeStruct((SRC, 1, TOK), F32)),
        in_specs=[pl.BlockSpec(memory_space=pltpu.VMEM)] * 2,
        out_specs=[pl.BlockSpec(memory_space=pltpu.VMEM)] * 3,
        scratch_shapes=[
            pltpu.VMEM((31, 2 * AUG + HD, TOK), BF16),
            pltpu.VMEM((31, TOK, AUG), BF16),
            pltpu.VMEM((31, HD + 16, TOK), F32),
        ],
        compiler_params=pltpu.CompilerParams(vmem_limit_bytes=50 * 2**20),
        cost_estimate=pl.CostEstimate(flops=18 * 10**9, bytes_accessed=3 * 2**20, transcendentals=0),
        name="attend",
    )(x, docs)

def bwd_kernel(x_ref, g_ref, docs_ref, o_ref, lse_ref, e_ref, fm, tm, eq, ek, ev):
    pad = jnp.zeros((AUG - HD - IDS - 16, TOK), BF16)
    pad2 = jnp.zeros((AUG - HD - 16, TOK), BF16)
    row16 = lax.broadcasted_iota(jnp.int32, (16, TOK), 0)
    ones = jnp.where(row16 < 3, 1.0, 0.0).astype(BF16)
    def three(v):
        hi, mid, lo = split3(v)
        hi, mid, lo = hi.astype(F32), mid.astype(F32), lo.astype(F32)
        return jnp.where(row16 == 0, hi, jnp.where(row16 == 1, mid, jnp.where(row16 == 2, lo, 0.0))).astype(BF16)
    def load(s, _):
        x = x_ref[s]
        d = docs_ref[s]
        g = g_ref[s]
        dot = jnp.sum(g.astype(F32) * o_ref[s], axis=0, keepdims=True)
        low = three(lse_ref[s] * (-1.0 / C2))
        off = three(-dot)
        fm[s] = jnp.concatenate([
            x[0:HD], marks(d, False), low, pad,
            g, off, pad2,
            x[HD:2 * HD], marks(d, True), ones, pad,
            x[2 * HD:], ones, pad2], axis=0)
        return 0
    loop(SRC, load)
    pack_levels(fm)
    iden = eye(TOK)
    def turn(i, _):
        tm[i] = nt(iden, fm[i]).astype(BF16)
        return 0
    loop(30, turn); turn(30, 0)
    def segment(first, count):
        q = jnp.concatenate([fm[first + b, 0:AUG, :] for b in range(count)], axis=1)
        g = jnp.concatenate([fm[first + b, AUG:2 * AUG, :] for b in range(count)], axis=1)
        rows = pl.ds(first, count)
        qt = tm[rows, :, 0:AUG].reshape(count * TOK, AUG)
        gt = tm[rows, :, AUG:2 * AUG].reshape(count * TOK, AUG)
        parts = []
        for t in range(count):
            k = first + t
            p = jnp.exp2(nn(tm[k, :, 2 * AUG:3 * AUG], q) * C2)
            es = (p * nn(tm[k, :, 3 * AUG:], g)).astype(BF16)
            ev[k] = nn(p.astype(BF16), gt)
            ek[k] = nn(es, qt)
            parts.append(es)
        k = jnp.concatenate([fm[first + t, 2 * AUG:2 * AUG + HD, :] for t in range(count)], axis=1)
        out = nn(k, jnp.concatenate(parts, axis=0))
        for b in range(count):
            eq[first + b] = out[:, b * TOK:(b + 1) * TOK]
    loop(7, lambda i, _: segment(i * 4, 4), MAIN)
    segment(28, 2)
    segment(30, 1)

    for level in range(4, 0, -1):
        c = TOK >> level
        def join(g, _, level=level, c=c):
            child = FIRST[level] + g
            grid = spread_grid(c) if level > 1 else None
            for half in range(2):
                mine = FIRST[level - 1] + 2 * g + half
                got = eq[child, :, half * 128:half * 128 + 128]
                if level > 1:
                    eq[mine] += spread(got, grid)
                else:
                    eq[mine, :, 0:128] += got
                for s in range(128 // c):
                    ek[mine, 2 * c * s:2 * c * s + c, :] += ek[child, half * 128 + c * s:half * 128 + c * s + c, :]
                    ev[mine, 2 * c * s:2 * c * s + c, :] += ev[child, half * 128 + c * s:half * 128 + c * s + c, :]
            return 0
        loop(BLOCKS[level], join)
    small = (lax.broadcasted_iota(jnp.int32, (HD, AUG), 0) == lax.broadcasted_iota(jnp.int32, (HD, AUG), 1)).astype(BF16)
    def finish(s, _):
        a = (eq[s] * ROOT).astype(BF16)
        b = nt(small, (ek[s] * ROOT).astype(BF16)).astype(BF16)
        v = nt(small, ev[s].astype(BF16)).astype(BF16)
        e_ref[s] = jnp.concatenate([a, b, v], axis=0)
        return 0
    loop(SRC, finish)

def attn_bwd(x, g, docs, o, lse):
    return pl.pallas_call(
        bwd_kernel,
        out_shape=jax.ShapeDtypeStruct((SRC, 3 * HD, TOK), BF16),
        in_specs=[pl.BlockSpec(memory_space=pltpu.VMEM)] * 5,
        out_specs=pl.BlockSpec(memory_space=pltpu.VMEM),
        scratch_shapes=[
            pltpu.VMEM((31, 4 * AUG, TOK), BF16),
            pltpu.VMEM((31, TOK, 4 * AUG), BF16),
            pltpu.VMEM((31, HD, TOK), F32),
            pltpu.VMEM((31, TOK, AUG), F32),
            pltpu.VMEM((31, TOK, AUG), F32),
        ],
        compiler_params=pltpu.CompilerParams(vmem_limit_bytes=56 * 2**20),
        cost_estimate=pl.CostEstimate(flops=28 * 10**9, bytes_accessed=6 * 2**20, transcendentals=0),
        name="attend_back",
    )(x, g, docs, o, lse)


def layer_norm(values, gain_row, shift_row):
    center = values - jnp.mean(values, axis=-1, keepdims=True)
    scale = lax.rsqrt(jnp.mean(center * center, axis=-1, keepdims=True) + epsilon)
    unit = center * scale
    return unit, scale, (unit * gain_row + shift_row).astype(BF16)


def layer_norm_back(grad, unit, scale, gain_row):
    pulled = grad * gain_row
    return (
        pulled
        - jnp.mean(pulled, axis=-1, keepdims=True)
        - unit * jnp.mean(pulled * unit, axis=-1, keepdims=True)
    ) * scale


def gelu_parts(values):
    share = 0.5 * (1.0 + lax.erf(values * math.sqrt(0.5)))
    slope = share + values * jnp.exp(-0.5 * values * values) * (1.0 / math.sqrt(2 * math.pi))
    return (values * share).astype(BF16), slope


def head_order():
    block = np.array([int(f"{k:04b}"[::-1], 2) for k in range(16)])
    heads = np.arange(HEADS)[:, None, None]
    residue = (heads + block[None, :, None]) % 16
    return (np.arange(16)[None, None, :] * 16 + residue).reshape(HEADS, TOK)


def cube_forward(hidden, params, order, docs, trade, window):
    w_qkv, w_out, w_mlp, gains, biases, up_bias = params
    unit_one, scale_one, normed = layer_norm(hidden, gains[0], biases[0])
    mixed = jnp.einsum("df,td->ft", w_qkv, normed, preferred_element_type=F32)
    shift = jnp.concatenate([biases[1], jnp.zeros_like(biases[1]), biases[2]])
    mixed = (mixed + shift[:, None]).astype(BF16)
    mixed = mixed.reshape(3, HEADS, HEAD_DIM, TOK).transpose(1, 0, 2, 3).reshape(HEADS, 3 * HEAD_DIM, TOK)
    mixed = jnp.einsum("hft,htu->hfu", mixed, order, preferred_element_type=F32).astype(BF16)
    heads = trade(mixed)
    merged, merged_low, summary = attn_fwd(heads, docs)
    merged_low, window = lax.optimization_barrier((merged_low, window))
    attended = trade(merged_low)
    attended = jnp.einsum("hdu,htu->hdt", attended, order, preferred_element_type=F32).astype(BF16)
    attended = attended.reshape(D, TOK)
    middle = hidden + jnp.einsum("ft,fd->td", attended, w_out, preferred_element_type=F32) + biases[3]
    unit_two, scale_two, normed_two = layer_norm(middle, gains[1], biases[4])
    ff = up_bias.shape[0]
    upward = jnp.dot(normed_two, w_mlp[:, :ff], preferred_element_type=F32) + up_bias
    activated, slope = gelu_parts(upward)
    result = middle + biases[5]
    for at in range(0, ff, D):
        result = result + jnp.dot(activated[:, at : at + D], w_mlp[:, ff + at : ff + at + D], preferred_element_type=F32)
    kept = (unit_one, scale_one, normed, heads, merged, summary, attended, unit_two, scale_two, normed_two, slope, activated)
    return result.astype(BF16), kept, window


def columns_of(values, at, number, over=0):
    place = (jnp.arange(128)[None, :] == at + number).astype(values.dtype)
    place = jnp.broadcast_to(place, (values.shape[over], 128))
    precision = highest if values.dtype == F32 else None
    return lax.dot_general(values, place, (((over,), (0,)), ((), ())), precision=precision, preferred_element_type=F32)


def cube_backward(incoming_low, kept, params, order, docs, trade, before, between, window, send_rest, at):
    w_qkv, w_out, w_mlp, gains, biases, up_bias = params
    unit_one, scale_one, normed, heads, merged, summary, attended, unit_two, scale_two, normed_two, slope, activated = kept
    ff = up_bias.shape[0]
    incoming = incoming_low.astype(F32)
    act_grad = jnp.concatenate([
        jnp.einsum("tb,ab->ta", incoming_low, w_mlp[:, ff + at : ff + at + D], preferred_element_type=F32)
        for at in range(0, ff, D)
    ], axis=1)
    up_grad = (act_grad * slope).astype(BF16)
    norm_two_grad = jnp.einsum("tb,ab->ta", up_grad, w_mlp[:, :ff], preferred_element_type=F32)
    middle_grad = incoming + layer_norm_back(norm_two_grad, unit_two, scale_two, gains[1])
    branch_grad = middle_grad.astype(BF16)
    merged_grad = jnp.einsum("fd,td->ft", w_out, branch_grad, preferred_element_type=F32).astype(BF16)
    merged_grad = merged_grad.reshape(HEADS, HEAD_DIM, TOK)
    merged_grad = jnp.einsum("hdt,htu->hdu", merged_grad, order, preferred_element_type=F32).astype(BF16)
    grad_rest = jnp.concatenate(
        [inner_rows(normed_two, up_grad).astype(BF16)]
        + [inner_rows(activated[:, at : at + D], incoming_low).astype(BF16) for at in range(0, ff, D)]
        + [jnp.einsum("ft,td->fd", attended, branch_grad, preferred_element_type=F32).astype(BF16)],
        axis=1,
    )
    merged_grad = trade(merged_grad)
    small = (
        columns_of(norm_two_grad * unit_two, at, 1)
        + columns_of(branch_grad, at, 5)
        + columns_of(norm_two_grad, at, 6)
        + columns_of(incoming_low, at, 7)
        + sum(columns_of(up_grad[:, k * D : (k + 1) * D], at, 8 + k) for k in range(4))
    )
    merged_grad, grad_rest, before = lax.optimization_barrier((merged_grad, grad_rest, before))
    sums_rest = send_rest(grad_rest)
    back_heads = attn_bwd(heads, merged_grad, docs, merged, summary)
    back_heads, window = lax.optimization_barrier((back_heads, window))
    mixed_grad = trade(back_heads)
    mixed_grad, before, small = lax.optimization_barrier((mixed_grad, between(before), small))
    mixed_grad = jnp.einsum("hfu,htu->hft", mixed_grad, order, preferred_element_type=F32).astype(BF16)
    mixed_grad = mixed_grad.reshape(HEADS, 3, HEAD_DIM, TOK).transpose(1, 0, 2, 3).reshape(3 * D, TOK)
    grad_qkv = jnp.einsum("td,ft->df", normed, mixed_grad, preferred_element_type=F32).astype(BF16)
    normed_grad = jnp.einsum("ft,df->td", mixed_grad, w_qkv, preferred_element_type=F32)
    start_grad = middle_grad + layer_norm_back(normed_grad, unit_one, scale_one, gains[0])
    late = (
        columns_of(normed_grad * unit_one, at, 0)
        + columns_of(normed_grad, at, 2)
        + columns_of(mixed_grad[:D], at, 3, 1)
        + columns_of(mixed_grad[2 * D :], at, 4, 1)
    )
    return start_grad, (grad_qkv, sums_rest, small + late), before, window


def half_pairs(source, count):
    return [(source * count + j, (1 - source) * count + j) for j in range(count)]


def core_swap(value, bit):
    return lax.ppermute(value, "seq", [(j, j ^ (1 << bit)) for j in range(16)])


def section_swap(value):
    return lax.ppermute(value, "section", [(0, 1), (1, 0)])


def place_bit(bit):
    return (lax.axis_index("seq") >> bit) & 1


def team(kind):
    def device(x, z, y, c):
        return x * 16 + z * 4 + y * 2 + c
    two, four = range(2), range(4)
    if kind == "plane":
        return [[device(x, z, y, c) for x in two for y in two] for z in four for c in two]
    return [[device(x, z, y, c) for z in four] for x in two for y in two for c in two]


def team_trade(value, kind):
    return lax.all_to_all(value, ("section", "seq"), 0, 0, axis_index_groups=team(kind), tiled=True)


def collect_line(piece):
    return team_trade(jnp.broadcast_to(piece[None], (4,) + piece.shape), "line")


def collect_plane(now):
    rows, columns = now.shape[1:]
    now = team_trade(jnp.broadcast_to(now[None], (4,) + now.shape), "plane")
    now = now.reshape(2, 2, 4, rows, columns)
    got = core_swap(now, 0)
    upper = place_bit(0) == 1
    halves = []
    for x in range(2):
        a, b = now[x].transpose(1, 0, 2, 3), got[x].transpose(1, 0, 2, 3)
        both = jnp.stack([jnp.where(upper, b, a), jnp.where(upper, a, b)], axis=2)
        halves.append(both.reshape(16 * rows, columns))
    return halves


def plus(own, got, dtype=BF16):
    return (own.astype(F32) + got.astype(F32)).astype(dtype)


def fold(value, bit, axis, dtype=BF16):
    mine = place_bit(bit)
    away = lax.dynamic_index_in_dim(value, 1 - mine, axis, keepdims=False)
    kept = lax.dynamic_index_in_dim(value, mine, axis, keepdims=False)
    return plus(kept, core_swap(away, bit), dtype)


def reduce_core(partial):
    rows, half = partial.shape[0] // 16, partial.shape[1] // 2
    now = fold(partial.reshape(8, 2, rows, 2 * half), 0, 1).reshape(4, 2, rows, 2 * half)
    return jnp.stack([now[:, y, :, x * half : x * half + half] for x in range(2) for y in range(2)])


def reduce_plane(now):
    return jnp.sum(team_trade(now, "plane").astype(F32), axis=0).astype(BF16)


def reduce_line(now):
    return jnp.sum(team_trade(now, "line").astype(F32), axis=0)


def cube_body(inputs, cotangent, documents, w_qkv, w_out, w_up, w_down, norm_gains, biases, up_bias):
    section_id = lax.axis_index("section")
    place = lax.axis_index("seq")
    count = lax.axis_size("seq")
    half = count // 2
    micro_id = place // half
    member = section_id * half + place % half
    teams = [[s * count + k * half + j for s in range(2) for j in range(half)] for k in range(2)]
    axes = ("section", "seq")
    lower = section_id == 0

    def trade(value):
        return lax.all_to_all(value, axes, 0, 0, axis_index_groups=teams, tiled=True)

    def across(value, pairs):
        return lax.ppermute(value, axes, pairs)

    def own_rows(pair):
        mine = jnp.where(micro_id == 0, pair[0], pair[1])
        other = jnp.where(micro_id == 0, pair[1], pair[0])
        swap = across(other, [(count + j, count + (j ^ half)) for j in range(count)])
        return jnp.where(lower, mine, swap)

    table = jnp.asarray(head_order())
    order = (table[:, None, :] == jnp.arange(TOK)[None, :, None]).astype(BF16)
    docs = jnp.where(micro_id == 0, documents[0], documents[1]).reshape(count, TOK)
    docs = jnp.where(micro_id == 0, docs, jnp.roll(docs, half, axis=0))
    own_order = lax.dynamic_index_in_dim(order, member, 0, keepdims=False)
    docs = jnp.dot(docs.astype(BF16), own_order, preferred_element_type=F32).reshape(count, 1, TOK)

    hidden = own_rows(inputs)
    wide = D // count
    lift = up_bias[0].reshape(-1, wide)
    small = jnp.concatenate([norm_gains[0], biases[0], lift]).T.astype(BF16)
    small = jnp.pad(small, ((0, 0), (0, 128 - small.shape[1])))

    ff = w_up.shape[2]
    low_qkv = w_qkv[0].astype(BF16)
    columns = low_qkv.shape[1] // 2
    got = across(low_qkv[:, columns:], half_pairs(0, count))
    piece = jnp.where(lower, low_qkv[:, :columns], got)
    line = collect_line(jnp.concatenate([piece, small], axis=1))

    piece, w_up, w_down = lax.optimization_barrier((piece, w_up, w_down))
    up_shard = w_up[0].astype(BF16).reshape(wide, count, 4, wide).transpose(0, 2, 1, 3).reshape(wide, ff)
    down_shard = w_down[0].astype(BF16).reshape(4, wide, D).transpose(1, 0, 2).reshape(wide, 4 * D)
    shard = jnp.concatenate([up_shard, down_shard, w_out[0].astype(BF16), low_qkv], axis=1)
    rows, rest = wide // 2, 2 * ff + D
    got = section_swap(jnp.where(lower, shard[rows:], shard[:rows]))
    near = jnp.concatenate([jnp.where(lower, shard[:rows, :rest], got[:, :rest]), jnp.where(lower, got, shard[rows:])[:, rest:]], axis=1)
    far = jnp.where(lower, got[:, :rest], shard[rows:, :rest])
    near, far, line, hidden = lax.optimization_barrier((near, far, line, hidden))
    parts = collect_plane(line)
    qkv_first = jnp.concatenate([part[:, :columns] for part in parts], axis=1)
    near = lax.all_gather(near, ("seq", "section"), axis=0, tiled=True)
    rest_final = lax.all_gather(far, ("seq", "section"), axis=0, tiled=True)
    rest_first, qkv_final = near[:, :rest], near[:, rest:]

    def lines(columns):
        values = columns[:, :12].astype(F32).T
        return values[:2], values[2:8], values[8:].reshape(ff)

    lines_first, lines_final = lines(parts[0][:, columns:]), lines(parts[1][:, columns:])
    params_first = (qkv_first, rest_first[:, 2 * ff :], rest_first) + lines_first
    params_final = (qkv_final, rest_final[:, 2 * ff :], rest_final) + lines_final
    beyond = [(count + j, count + (j ^ half)) for j in range(count)]
    back_over = [(count + j, j ^ half) for j in range(count)]
    first, kept_first, start_back = cube_forward(
        hidden.astype(F32), params_first, order, docs, trade, own_rows(cotangent)
    )
    final, kept_final, far = cube_forward(
        first.astype(F32), params_final, order, docs, trade, across(first, back_over)
    )
    def placed(mine, other):
        return jnp.where(micro_id == 0, jnp.stack([mine, other]), jnp.stack([other, mine]))[None]

    def scattered_last(partial):
        return lax.psum_scatter(partial, ("seq", "section"), scatter_dimension=0, tiled=True)

    def scattered_near(partial):
        return lax.psum_scatter(partial, "seq", scatter_dimension=0, tiled=True)

    start_back, merged = lax.optimization_barrier((start_back, kept_final[4]))
    kept_final = kept_final[:4] + (merged,) + kept_final[5:]
    grad_final, terms_final, _, window = cube_backward(
        start_back, kept_final, params_final, order, docs, trade, None, lambda now: now,
        (across(final, half_pairs(0, count)), across(final, beyond)), scattered_near, 12,
    )
    layer_outputs = placed(jnp.where(lower, first, window[0]), jnp.where(lower, far, window[1]))
    rest_final = terms_final[1]
    sent, qkv_final, small_final = lax.optimization_barrier(
        (grad_final.astype(BF16), terms_final[0], terms_final[2])
    )
    grad_first, terms_first, qkv_final, window = cube_backward(
        sent, kept_first, params_first, order, docs, trade, reduce_core(qkv_final), reduce_plane,
        (across(sent, half_pairs(0, count)), across(sent, beyond)), scattered_last, 0,
    )

    smalls = (terms_first[2] + small_final).astype(BF16)
    smalls = fold(smalls.reshape(8, 2, wide, 128), 0, 1).reshape(4, 2, wide, 128)
    smalls = jnp.stack([smalls[:, 0], smalls[:, 1]] * 2)
    now = jnp.concatenate([reduce_core(terms_first[0]), smalls], axis=3)
    plane, far_back = lax.optimization_barrier((reduce_plane(now), across(grad_first.astype(BF16), back_over)))
    now = reduce_line(jnp.concatenate([plane, qkv_final], axis=2))
    columns = qkv_final.shape[2]
    qkv_first, smalls, qkv_final = now[:, :columns], now[:, columns : columns + 24], now[:, columns + 128 :]
    smalls = jnp.where(lower, smalls[:, :12], smalls[:, 12:]).T
    rest_first = terms_first[1]
    input_grads = placed(
        jnp.where(lower, grad_first, window[0].astype(F32)), jnp.where(lower, far_back, window[1]).astype(F32)
    )

    near = across(rest_final, half_pairs(0, count))
    away = across(rest_first, half_pairs(1, count))
    rest = jnp.where(
        lower, jnp.concatenate([rest_first, away]).astype(F32), rest_final.astype(F32) + near.astype(F32)
    )
    qkv_final, qkv_first, layer_outputs = lax.optimization_barrier((qkv_final, qkv_first, layer_outputs))
    away = section_swap(jnp.where(lower, qkv_final, qkv_first).astype(BF16)).astype(F32)
    qkv = jnp.where(
        lower, jnp.concatenate([qkv_first, away], axis=1), jnp.concatenate([away, qkv_final], axis=1)
    )
    up = rest[:, :ff].reshape(wide, 4, count, wide).transpose(0, 2, 1, 3).reshape(wide, ff)
    down = rest[:, ff : 2 * ff].reshape(wide, 4, D).transpose(1, 0, 2).reshape(4 * wide, D)
    return (
        layer_outputs,
        input_grads,
        qkv[None],
        rest[None, :, 2 * ff :],
        up[None],
        down[None],
        smalls[None, :2],
        smalls[None, 2:8],
        smalls[8:].reshape(1, -1),
    )


def solution(mesh):
    cube = mesh.shape["seq"] == 16
    return jax.shard_map(
        cube_body if cube else body,
        mesh=mesh,
        in_specs=(
            P(None, "seq", None),
            P(None, "seq", None),
            P(),
            P("section", "seq", None),
            P("section", "seq", None),
            P("section", "seq", None),
            P("section", "seq", None),
            P("section", None, "seq"),
            P("section", None, "seq"),
            P("section", "seq"),
        ),
        out_specs=(
            P("section", None, "seq", None),
            P("section", None, "seq", None),
            P("section", "seq", None),
            P("section", "seq", None),
            P("section", "seq", None),
            P("section", "seq", None),
            P("section", None, "seq"),
            P("section", None, "seq"),
            P("section", "seq"),
        ),
        check_vma=False,
    )
```

```python
import functools
import math

import jax
import jax.numpy as jnp
import numpy as np
from jax import lax
from jax.experimental import pallas as pl
from jax.experimental.pallas import tpu as pltpu
from jax.sharding import PartitionSpec as P

D = 768
HEADS = 16
HEAD_DIM = 48
SEG0 = 1024
BRANCHES = 5


epsilon = 1e-05
masked_score = -1e30
highest = lax.Precision.HIGHEST


def swapped(value, axis, apart):
    mask = 2**apart
    pairs = [(source, source ^ mask) for source in range(lax.axis_size(axis))]
    return lax.ppermute(value, axis, pairs)


def for_sending(array):
    return jax.tree.map(lambda a: a.astype(jnp.bfloat16) if a.dtype == jnp.float32 else a, array)


def passed_along(array, axis, by):
    peers = lax.axis_size(axis)
    pairs = [(i, i + by) for i in range(peers) if 0 <= i + by < peers]
    return lax.ppermute(array, axis, pairs)


def layer_norm_parts(values, gain_row, shift_row):
    center = values - jnp.mean(values, axis=-1, keepdims=True)
    spread = jnp.mean(center * center, axis=-1, keepdims=True)
    return center * lax.rsqrt(spread + epsilon) * gain_row + shift_row


def exact_gelu(values):
    return jax.nn.gelu(values, approximate=False)


def inner_rows(left, right):
    return jnp.einsum("ta,tb->ab", left, right, preferred_element_type=jnp.float32)


def geometry(tokens_dev, devices):
    groups = [
        min(SEG0 * 2**level_id, tokens_dev * devices) // tokens_dev for level_id in range(BRANCHES)
    ]
    return (groups, max(groups).bit_length() - 1)


def first_level(groups, step_id):
    return min((level_id for level_id in range(BRANCHES) if groups[level_id] > 2**step_id))


def pick_grid(level_id, dtype):
    dilation = 2**level_id
    return (jnp.arange(dilation)[:, None] == (jnp.arange(HEADS) % dilation)[None, :]).astype(dtype)


def select_rows(tensor, level_id):
    dilation = 2**level_id
    shaped = tensor.reshape((tensor.shape[0] // dilation, dilation) + tensor.shape[1:])
    if tensor.dtype == jnp.bfloat16:
        chosen = jnp.einsum(
            "jrh...,rh->jh...",
            shaped,
            pick_grid(level_id, jnp.bfloat16),
            preferred_element_type=jnp.float32,
        )
        return chosen.astype(jnp.bfloat16)
    return jnp.einsum(
        "jrh...,rh->jh...", shaped, pick_grid(level_id, jnp.float32), precision=highest
    )


def spread_rows(tensor, level_id):
    dilation = 2**level_id
    spread = jnp.einsum(
        "jh...,rh->jrh...", tensor, pick_grid(level_id, jnp.float32), precision=highest
    )
    return spread.reshape((tensor.shape[0] * dilation,) + tensor.shape[1:])


def spread_sums(tensor, level_id):
    dilation = 2**level_id
    grid = pick_grid(level_id, jnp.float32)
    spread = jnp.where(grid[None] > 0, tensor[:, None, :], masked_score)
    return spread.reshape(tensor.shape[0] * dilation, HEADS)


def doc_tables(documents_now, level_id, group, tokens_dev, seq_place):
    dilation = 2**level_id
    offsets = np.arange(HEADS) % dilation
    own_docs = lax.dynamic_slice_in_dim(documents_now, seq_place * tokens_dev, tokens_dev)
    own_docs = own_docs.reshape(tokens_dev // dilation, dilation)[:, offsets]
    seg_start = seq_place // group * group * tokens_dev
    seg_docs = lax.dynamic_slice_in_dim(documents_now, seg_start, group * tokens_dev)
    seg_docs = seg_docs.reshape(group * tokens_dev // dilation, dilation)[:, offsets]
    return (own_docs, seg_docs)


def head_bits(level_id):
    return jnp.arange(HEADS) >> level_id & 1


def halve(buffer, level_id):
    pairs = buffer.reshape(buffer.shape[0], buffer.shape[1] // 2, 2, HEADS, HEAD_DIM)
    chosen = head_bits(level_id)[None, None, :, None] == 1
    return jnp.where(chosen, pairs[:, :, 1], pairs[:, :, 0])


def widen(buffer, level_id):
    chosen = head_bits(level_id)[None, None, :, None] == 1
    empty = jnp.zeros_like(buffer)
    upper_part = jnp.where(chosen, buffer, empty)
    lower_part = jnp.where(chosen, empty, buffer)
    stacked = jnp.stack([lower_part, upper_part], axis=2)
    return stacked.reshape(buffer.shape[0], buffer.shape[1] * 2, HEADS, HEAD_DIM)


def thin_to(buffer, low_level, high_level):
    for level_id in range(low_level, high_level):
        buffer = halve(buffer, level_id)
    return buffer


def widen_to(buffer, low_level, high_level):
    for level_id in reversed(range(low_level, high_level)):
        buffer = widen(buffer, level_id)
    return buffer


def gather_keys(own_rows, groups, step_count, seq_place):
    results = [None] * BRANCHES
    current = own_rows
    level_now = 0
    for level_id in range(BRANCHES):
        pass
    for step_id in range(step_count):
        target = first_level(groups, step_id)
        current = thin_to(current, level_now, target)
        level_now = target
        row_count = current.shape[1]
        flat_rows = current.reshape(2, row_count, HEADS * HEAD_DIM)
        incoming = swapped(flat_rows, "seq", step_id).reshape(current.shape)
        upper_half = seq_place >> step_id & 1 == 1
        current = jnp.where(
            upper_half,
            jnp.concatenate([incoming, current], axis=1),
            jnp.concatenate([current, incoming], axis=1),
        )
        for level_id in range(BRANCHES):
            if groups[level_id] == 2 ** (step_id + 1):
                results[level_id] = thin_to(current, level_now, level_id)
    return results


def scatter_keys(key_grads, groups, step_count, seq_place):
    carried = None
    for step_id in reversed(range(step_count)):
        level_now = first_level(groups, step_id)
        total_grad = None
        if carried is not None:
            total_grad = widen_to(carried, level_now, first_level(groups, step_id + 1))
        for level_id in range(BRANCHES):
            if groups[level_id] == 2 ** (step_id + 1):
                branch_term = widen_to(key_grads[level_id], level_now, level_id)
                total_grad = branch_term if total_grad is None else total_grad + branch_term
        half_rows = total_grad.shape[1] // 2
        upper_half = seq_place >> step_id & 1 == 1
        own_half = jnp.where(upper_half, total_grad[:, half_rows:], total_grad[:, :half_rows])
        theirs = jnp.where(upper_half, total_grad[:, :half_rows], total_grad[:, half_rows:])
        flat_rows = theirs.reshape(2, half_rows, HEADS * HEAD_DIM)
        incoming = (
            swapped(for_sending(flat_rows), "seq", step_id)
            .astype(flat_rows.dtype)
            .reshape(own_half.shape)
        )
        carried = own_half + incoming
    own_grad = widen_to(carried, 0, first_level(groups, 0))
    for level_id in range(BRANCHES):
        pass
    return own_grad


def head_blocks(level_id):
    block_size = min(HEADS, 4 * 2**level_id)
    return (HEADS // block_size, block_size)


def to_blocks(tensor, block_count, block_size):
    moved = jnp.moveaxis(tensor, 1, 0)
    return moved.reshape((block_count, block_size) + moved.shape[1:])


def from_blocks(tensor):
    joined = tensor.reshape((tensor.shape[0] * tensor.shape[1],) + tensor.shape[2:])
    return jnp.moveaxis(joined, 0, 1)


def score_block(query_block, key_block, query_doc, key_doc):
    scores = jnp.einsum(
        "hqd,hkd->hqk", query_block, key_block, preferred_element_type=jnp.float32
    ) * HEAD_DIM ** (-0.5)
    return jnp.where(query_doc[:, :, None] == key_doc[:, None, :], scores, masked_score)


def forward_block(pieces):
    query_block, key_block, value_block, query_doc, key_doc = pieces
    scores = score_block(query_block, key_block, query_doc, key_doc)
    row_max = jnp.max(scores, axis=-1, keepdims=True)
    weights = jnp.exp(scores - row_max)
    row_total = jnp.sum(weights, axis=-1, keepdims=True)
    prob_rows = (weights / row_total).astype(jnp.bfloat16)
    result = jnp.einsum("hqk,hkd->hqd", prob_rows, value_block, preferred_element_type=jnp.float32)
    return (result, (row_max + jnp.log(row_total))[:, :, 0])


def backward_block(pieces):
    query_block, key_block, value_block, query_doc, key_doc, summary, out_grad, summary_grad = (
        pieces
    )
    scores = score_block(query_block, key_block, query_doc, key_doc)
    prob_rows = jnp.exp(scores - summary[:, :, None])
    prob_grad = jnp.einsum(
        "hqd,hkd->hqk", out_grad, value_block, preferred_element_type=jnp.float32
    )
    score_grad = prob_rows * (
        prob_grad
        - jnp.sum(prob_rows * prob_grad, axis=-1, keepdims=True)
        + summary_grad[:, :, None]
    )
    score_grad = score_grad.astype(jnp.bfloat16)
    score_scale = HEAD_DIM ** (-0.5)
    query_grad = (
        jnp.einsum("hqk,hkd->hqd", score_grad, key_block, preferred_element_type=jnp.float32)
        * score_scale
    )
    key_grad = (
        jnp.einsum("hqk,hqd->hkd", score_grad, query_block, preferred_element_type=jnp.float32)
        * score_scale
    )
    value_grad = jnp.einsum(
        "hqk,hqd->hkd", prob_rows.astype(jnp.bfloat16), out_grad, preferred_element_type=jnp.float32
    )
    return (query_grad, key_grad, value_grad)


def branch_forward(query_sel, key_value, query_docs, key_docs, level_id):
    block_count, block_size = head_blocks(level_id)
    pieces = (
        to_blocks(query_sel, block_count, block_size),
        to_blocks(key_value[0], block_count, block_size),
        to_blocks(key_value[1], block_count, block_size),
        to_blocks(query_docs, block_count, block_size),
        to_blocks(key_docs, block_count, block_size),
    )
    results, summaries = lax.map(forward_block, pieces)
    return (from_blocks(results), from_blocks(summaries))


def branch_backward(
    query_sel, key_value, query_docs, key_docs, summary, out_grad, summary_grad, level_id
):
    block_count, block_size = head_blocks(level_id)
    pieces = (
        to_blocks(query_sel, block_count, block_size),
        to_blocks(key_value[0], block_count, block_size),
        to_blocks(key_value[1], block_count, block_size),
        to_blocks(query_docs, block_count, block_size),
        to_blocks(key_docs, block_count, block_size),
        to_blocks(summary, block_count, block_size),
        to_blocks(out_grad, block_count, block_size),
        to_blocks(summary_grad, block_count, block_size),
    )
    query_grad, key_grad, value_grad = lax.map(backward_block, pieces)
    return (from_blocks(query_grad), jnp.stack([from_blocks(key_grad), from_blocks(value_grad)]))


def layer_forward(hidden, params, documents_now, groups, step_count, seq_place):
    w_qkv, w_out, w_up, w_down, gains, biases, up_bias = params
    gains = gains.astype(jnp.float32)
    biases = biases.astype(jnp.float32)
    tokens_dev = hidden.shape[0]
    normed = layer_norm_parts(hidden, gains[0], biases[0]).astype(jnp.bfloat16)
    mixed_rows = jnp.dot(normed, w_qkv, preferred_element_type=jnp.float32)
    queries = (mixed_rows[:, :D] + biases[1]).astype(jnp.bfloat16)
    key_part = mixed_rows[:, D : 2 * D].astype(jnp.bfloat16)
    values = (mixed_rows[:, 2 * D :] + biases[2]).astype(jnp.bfloat16)
    own_rows = jnp.stack([key_part, values]).reshape(2, tokens_dev, HEADS, HEAD_DIM)
    gathered = gather_keys(own_rows, groups, step_count, seq_place)
    query_heads = queries.reshape(tokens_dev, HEADS, HEAD_DIM)
    picked, branch_outs, branch_sums = ([], [], [])
    for level_id in range(BRANCHES):
        query_sel = select_rows(query_heads, level_id)
        query_docs, key_docs = doc_tables(
            documents_now, level_id, groups[level_id], tokens_dev, seq_place
        )
        result, summary = branch_forward(
            query_sel, gathered[level_id], query_docs, key_docs, level_id
        )
        picked.append(query_sel)
        branch_outs.append(result)
        branch_sums.append(summary)
    full_sums = jnp.stack(
        [spread_sums(branch_sums[level_id], level_id) for level_id in range(BRANCHES)]
    )
    row_max = jnp.max(full_sums, axis=0)
    shares = jnp.exp(full_sums - row_max)
    shares = shares / jnp.sum(shares, axis=0)
    merged = sum(
        (
            shares[level_id][:, :, None] * spread_rows(branch_outs[level_id], level_id)
            for level_id in range(BRANCHES)
        )
    )
    attended = merged.reshape(tokens_dev, D).astype(jnp.bfloat16)
    middle = hidden + jnp.dot(attended, w_out, preferred_element_type=jnp.float32) + biases[3]
    normed_two = layer_norm_parts(middle, gains[1], biases[4]).astype(jnp.bfloat16)
    upward = jnp.dot(normed_two, w_up, preferred_element_type=jnp.float32) + up_bias.astype(
        jnp.float32
    )
    activated = exact_gelu(upward).astype(jnp.bfloat16)
    result = middle + jnp.dot(activated, w_down, preferred_element_type=jnp.float32) + biases[5]
    kept_values = (
        hidden,
        normed,
        picked,
        gathered,
        branch_sums,
        branch_outs,
        shares,
        merged,
        attended,
        middle,
        normed_two,
        upward,
        activated,
    )
    return (result, kept_values)


def layer_backward(incoming, kept_values, params, documents_now, groups, step_count, seq_place):
    w_qkv, w_out, w_up, w_down, gains, biases, up_bias = params
    gains = gains.astype(jnp.float32)
    biases = biases.astype(jnp.float32)
    (
        hidden,
        normed,
        picked,
        gathered,
        branch_sums,
        branch_outs,
        shares,
        merged,
        attended,
        middle,
        normed_two,
        upward,
        activated,
    ) = kept_values
    tokens_dev = hidden.shape[0]
    down_grad = incoming.astype(jnp.bfloat16)
    grad_down = inner_rows(activated, down_grad)
    grad_bias_down = jnp.sum(down_grad.astype(jnp.float32), axis=0)
    act_grad = jnp.einsum("tb,ab->ta", down_grad, w_down, preferred_element_type=jnp.float32)
    gelu_pulled = jax.vjp(exact_gelu, upward)
    up_grad = gelu_pulled[1](act_grad)[0].astype(jnp.bfloat16)
    grad_up = inner_rows(normed_two, up_grad)
    grad_up_bias = jnp.sum(up_grad.astype(jnp.float32), axis=0)
    norm_two_grad = jnp.einsum("tb,ab->ta", up_grad, w_up, preferred_element_type=jnp.float32)
    norm_pulled = jax.vjp(layer_norm_parts, middle, gains[1], biases[4])
    middle_part, grad_gain_two, grad_shift_two = norm_pulled[1](norm_two_grad)
    middle_grad = incoming + middle_part
    branch_grad = middle_grad.astype(jnp.bfloat16)
    grad_out = inner_rows(attended, branch_grad)
    grad_bias_out = jnp.sum(branch_grad.astype(jnp.float32), axis=0)
    merged_grad = jnp.einsum("tb,ab->ta", branch_grad, w_out, preferred_element_type=jnp.float32)
    merged_grad = merged_grad.reshape(tokens_dev, HEADS, HEAD_DIM)
    query_grad = jnp.zeros((tokens_dev, HEADS, HEAD_DIM), jnp.float32)
    key_grads = []
    for level_id in range(BRANCHES):
        share_sel = select_rows(shares[level_id], level_id)
        merged_sel = select_rows(merged, level_id)
        grad_sel = select_rows(merged_grad, level_id)
        out_grad = (share_sel[:, :, None] * grad_sel).astype(jnp.bfloat16)
        summary_grad = share_sel * (
            jnp.sum(grad_sel * branch_outs[level_id], axis=-1)
            - jnp.sum(grad_sel * merged_sel, axis=-1)
        )
        query_docs, key_docs = doc_tables(
            documents_now, level_id, groups[level_id], tokens_dev, seq_place
        )
        query_part, key_value_grad = branch_backward(
            picked[level_id],
            gathered[level_id],
            query_docs,
            key_docs,
            branch_sums[level_id],
            out_grad,
            summary_grad,
            level_id,
        )
        query_grad = query_grad + spread_rows(query_part, level_id)
        key_grads.append(key_value_grad)
    own_grad = scatter_keys(key_grads, groups, step_count, seq_place)
    mixed_grad = jnp.concatenate(
        [
            query_grad.reshape(tokens_dev, D),
            own_grad[0].reshape(tokens_dev, D),
            own_grad[1].reshape(tokens_dev, D),
        ],
        axis=1,
    ).astype(jnp.bfloat16)
    grad_qkv = inner_rows(normed, mixed_grad)
    grad_bias_query = jnp.sum(mixed_grad[:, :D].astype(jnp.float32), axis=0)
    grad_bias_value = jnp.sum(mixed_grad[:, 2 * D :].astype(jnp.float32), axis=0)
    normed_grad = jnp.einsum("tb,ab->ta", mixed_grad, w_qkv, preferred_element_type=jnp.float32)
    norm_pulled = jax.vjp(layer_norm_parts, hidden, gains[0], biases[0])
    hidden_part, grad_gain_one, grad_shift_one = norm_pulled[1](normed_grad)
    start_grad = middle_grad + hidden_part
    gradients = (
        grad_qkv,
        grad_out,
        grad_up,
        grad_down,
        jnp.stack([grad_gain_one, grad_gain_two]),
        jnp.stack(
            [
                grad_shift_one,
                grad_bias_query,
                grad_bias_value,
                grad_bias_out,
                grad_shift_two,
                grad_bias_down,
            ]
        ),
        grad_up_bias,
    )
    return (start_grad, gradients)


def body(inputs, cotangent, documents, w_qkv, w_out, w_up, w_down, norm_gains, biases, up_bias):
    section_id = lax.axis_index("section")
    seq_place = lax.axis_index("seq")
    devices = lax.axis_size("seq")
    micro = inputs.shape[0]
    tokens_dev = inputs.shape[1]
    groups, step_count = geometry(tokens_dev, devices)
    params = (
        lax.all_gather(w_qkv[0].astype(jnp.bfloat16), "seq", axis=0, tiled=True),
        lax.all_gather(w_out[0].astype(jnp.bfloat16), "seq", axis=0, tiled=True),
        lax.all_gather(w_up[0].astype(jnp.bfloat16), "seq", axis=0, tiled=True),
        lax.all_gather(w_down[0].astype(jnp.bfloat16), "seq", axis=0, tiled=True),
        lax.all_gather(norm_gains[0].astype(jnp.bfloat16), "seq", axis=1, tiled=True),
        lax.all_gather(biases[0].astype(jnp.bfloat16), "seq", axis=1, tiled=True),
        lax.all_gather(up_bias[0].astype(jnp.bfloat16), "seq", axis=0, tiled=True),
    )
    empty_rows = jnp.zeros((tokens_dev, D), jnp.bfloat16)
    received = empty_rows
    saved = []
    produced = []
    for tick_id in range(micro + 1):
        batch_index = jnp.clip(tick_id - section_id, 0, micro - 1)
        documents_now = lax.dynamic_index_in_dim(documents, batch_index, 0, keepdims=False)
        fresh_rows = inputs[tick_id] if tick_id < micro else empty_rows
        start_rows = jnp.where(section_id == 0, fresh_rows, received).astype(jnp.float32)
        result, kept_values = layer_forward(
            start_rows, params, documents_now, groups, step_count, seq_place
        )
        sent_rows = result.astype(jnp.bfloat16)
        produced.append(sent_rows)
        saved.append((kept_values, documents_now))
        if tick_id < micro:
            received = passed_along(sent_rows, "section", 1)
    back_received = empty_rows
    start_grads = []
    sent_grads = []
    totals = None
    shards = None
    for tick_id in range(micro + 1):
        earlier_save = saved[max(tick_id - 1, 0)]
        later_save = saved[min(tick_id + 1, micro)]
        kept_values, documents_now = jax.tree.map(
            lambda earlier, latter: jnp.where(section_id == 0, earlier, latter),
            earlier_save,
            later_save,
        )
        fresh_rows = cotangent[tick_id] if tick_id < micro else empty_rows
        incoming = jnp.where(section_id == 1, fresh_rows, back_received).astype(jnp.float32)
        start_grad, gradients = layer_backward(
            incoming, kept_values, params, documents_now, groups, step_count, seq_place
        )
        sent_rows = start_grad.astype(jnp.bfloat16)
        start_grads.append(start_grad)
        sent_grads.append(sent_rows.astype(jnp.float32))
        if tick_id < micro:
            back_received = passed_along(sent_rows, "section", -1)
        totals = (
            list(gradients)
            if totals is None
            else [earlier + latter for earlier, latter in zip(totals, gradients)]
        )
    shards = (
        lax.psum_scatter(totals[0], "seq", scatter_dimension=0, tiled=True),
        lax.psum_scatter(totals[1], "seq", scatter_dimension=0, tiled=True),
        lax.psum_scatter(totals[2], "seq", scatter_dimension=0, tiled=True),
        lax.psum_scatter(totals[3], "seq", scatter_dimension=0, tiled=True),
        lax.psum_scatter(totals[4], "seq", scatter_dimension=1, tiled=True),
        lax.psum_scatter(totals[5], "seq", scatter_dimension=1, tiled=True),
        lax.psum_scatter(totals[6], "seq", scatter_dimension=0, tiled=True),
    )
    layer_outputs = jnp.stack(
        [
            jnp.where(section_id == 0, produced[batch_id], produced[batch_id + 1])
            for batch_id in range(micro)
        ]
    )[None]
    input_grads = jnp.stack(
        [
            jnp.where(section_id == 0, start_grads[batch_id + 1], sent_grads[batch_id])
            for batch_id in range(micro)
        ]
    )[None]
    return (
        layer_outputs,
        input_grads,
        shards[0][None],
        shards[1][None],
        shards[2][None],
        shards[3][None],
        shards[4][None],
        shards[5][None],
        shards[6][None],
    )


HD = 48
AUG = 128
IDS = 32
SRC = 16
TOK = 256
ROOT = HD ** -0.5
C2 = ROOT * math.log2(math.e)
AWAY = -(2.0 ** 100)
BLOCKS = (16, 8, 4, 2, 1)
FIRST = (0, 16, 24, 28, 30)
F32, BF16 = jnp.float32, jnp.bfloat16

UN = 16
MAIN = 1
QW = 4
TWO = False

def loop(n, f, u=None):
    u = min(u or UN, n)
    while n % u:
        u -= 1
    def many(i, _):
        for j in range(u):
            f(i * u + j, 0)
        return 0
    lax.fori_loop(0, n // u, many, 0)

def nt(a, b):
    return lax.dot_general(a, b, (((1,), (1,)), ((), ())), preferred_element_type=F32)

def nn(a, b):
    return jnp.dot(a, b, preferred_element_type=F32)

def eye(n):
    return (lax.broadcasted_iota(jnp.int32, (n, n), 0) == lax.broadcasted_iota(jnp.int32, (n, n), 1)).astype(BF16)

def pack_grid(c):
    col = lax.broadcasted_iota(jnp.int32, (256, 128), 1)
    row = lax.broadcasted_iota(jnp.int32, (256, 128), 0)
    return (row == (col // c) * (2 * c) + col % c).astype(BF16)

def spread_grid(c):
    row = lax.broadcasted_iota(jnp.int32, (128, 256), 0)
    col = lax.broadcasted_iota(jnp.int32, (128, 256), 1)
    return (col == (row // c) * (2 * c) + row % c).astype(BF16)

def split3(v):
    hi = v.astype(BF16)
    r = v - hi.astype(F32)
    mid = r.astype(BF16)
    lo = (r - mid.astype(F32)).astype(BF16)
    return hi, mid, lo

def spread(v, grid):
    hi, mid, lo = split3(v)
    return nn(hi, grid) + nn(mid, grid) + nn(lo, grid)

def pack_levels(stack):
    for level in range(1, 5):
        c = TOK >> level
        def step(g, _, level=level, c=c):
            a = stack[FIRST[level - 1] + 2 * g]
            b = stack[FIRST[level - 1] + 2 * g + 1]
            if level == 1:
                pa, pb = a[:, :128], b[:, :128]
            else:
                grid = pack_grid(c)
                pa, pb = nn(a, grid).astype(BF16), nn(b, grid).astype(BF16)
            stack[FIRST[level] + g] = jnp.concatenate([pa, pb], axis=1)
            return 0
        loop(BLOCKS[level], step)

def marks(doc_row, away):
    ids = lax.broadcasted_iota(jnp.int32, (IDS, TOK), 0).astype(F32)
    same = ids == doc_row
    return (jnp.where(same, 0.0, AWAY) if away else jnp.where(same, 1.0, 0.0)).astype(BF16)

def fwd_kernel(x_ref, docs_ref, o_ref, ob_ref, lse_ref, fm, ktm, part, *, kc):
    pad = jnp.zeros((AUG - HD - IDS, TOK), BF16)
    def load(s, _):
        x = x_ref[s]
        d = docs_ref[s]
        fm[s] = jnp.concatenate([x[0:HD], marks(d, False), pad, x[HD:2 * HD], marks(d, True), pad, x[2 * HD:]], axis=0)
        return 0
    loop(SRC, load)
    pack_levels(fm)
    iden = eye(TOK)
    def turn(i, _):
        ktm[i] = nt(iden, fm[i, AUG:2 * AUG, :]).astype(BF16)
        return 0
    loop(30, turn); turn(30, 0)

    def segment(first, count):
        for at in range(0, count, QW):
            n = min(QW, count - at)
            q = jnp.concatenate([fm[first + at + b, 0:AUG, :] for b in range(n)], axis=1)
            scores = [nn(ktm[first + t], q) for t in range(count)]
            top = functools.reduce(jnp.maximum, [jnp.max(x, axis=0, keepdims=True) for x in scores])
            ps = [jnp.exp2((x - top) * C2) for x in scores]
            total = functools.reduce(jnp.add, [jnp.sum(p, axis=0, keepdims=True) for p in ps])
            p = jnp.concatenate([p.astype(BF16) for p in ps], axis=0)
            v = jnp.concatenate([fm[first + t, 2 * AUG:2 * AUG + HD, :] for t in range(count)], axis=1)
            out = nn(v, p)
            for b in range(n):
                part[first + at + b, 0:HD] = out[:, b * TOK:(b + 1) * TOK]
                part[first + at + b, HD:HD + 8] = jnp.broadcast_to(total[:, b * TOK:(b + 1) * TOK], (8, TOK))
                part[first + at + b, HD + 8:HD + 16] = jnp.broadcast_to(top[:, b * TOK:(b + 1) * TOK] * C2, (8, TOK))
    loop(7, lambda i, _: segment(i * 4, 4), MAIN)
    segment(28, 2)
    segment(30, 1)

    for level in range(4, 0, -1):
        c = TOK >> level
        def join(g, _, level=level, c=c):
            child = FIRST[level] + g
            grid = spread_grid(c) if level > 1 else None
            for half in range(2):
                mine = FIRST[level - 1] + 2 * g + half
                got = part[child, :, half * 128:half * 128 + 128]
                if level > 1:
                    got = spread(got, grid)
                else:
                    got = jnp.concatenate([got, jnp.zeros_like(got)], axis=1)
                own = part[mine]
                cl, cm = got[HD:HD + 1], got[HD + 8:HD + 9]
                cm = jnp.where(cl > 0, cm, AWAY)
                ol, om = own[HD:HD + 1], own[HD + 8:HD + 9]
                top = jnp.maximum(cm, om)
                wc, wo = jnp.exp2(cm - top), jnp.exp2(om - top)
                part[mine, 0:HD] = got[0:HD] * wc + own[0:HD] * wo
                part[mine, HD:HD + 8] = jnp.broadcast_to(cl * wc + ol * wo, (8, TOK))
                part[mine, HD + 8:HD + 16] = jnp.broadcast_to(top, (8, TOK))
            return 0
        loop(BLOCKS[level], join)
    def finish(s, _):
        own = part[s]
        l, m = own[HD:HD + 1], own[HD + 8:HD + 9]
        out = own[0:HD] / l
        o_ref[s] = out
        ob_ref[s] = out.astype(BF16)
        lse_ref[s] = m + jnp.log2(l)
        return 0
    loop(SRC, finish)

def attn_fwd(x, docs):
    return pl.pallas_call(
        functools.partial(fwd_kernel, kc=256),
        out_shape=(jax.ShapeDtypeStruct((SRC, HD, TOK), F32), jax.ShapeDtypeStruct((SRC, HD, TOK), BF16), jax.ShapeDtypeStruct((SRC, 1, TOK), F32)),
        in_specs=[pl.BlockSpec(memory_space=pltpu.VMEM)] * 2,
        out_specs=[pl.BlockSpec(memory_space=pltpu.VMEM)] * 3,
        scratch_shapes=[
            pltpu.VMEM((31, 2 * AUG + HD, TOK), BF16),
            pltpu.VMEM((31, TOK, AUG), BF16),
            pltpu.VMEM((31, HD + 16, TOK), F32),
        ],
        compiler_params=pltpu.CompilerParams(vmem_limit_bytes=50 * 2**20),
        cost_estimate=pl.CostEstimate(flops=18 * 10**9, bytes_accessed=3 * 2**20, transcendentals=0),
        name="attend",
    )(x, docs)

def bwd_kernel(x_ref, g_ref, docs_ref, o_ref, lse_ref, e_ref, fm, tm, eq, ek, ev):
    pad = jnp.zeros((AUG - HD - IDS - 16, TOK), BF16)
    pad2 = jnp.zeros((AUG - HD - 16, TOK), BF16)
    row16 = lax.broadcasted_iota(jnp.int32, (16, TOK), 0)
    ones = jnp.where(row16 < 3, 1.0, 0.0).astype(BF16)
    def three(v):
        hi, mid, lo = split3(v)
        hi, mid, lo = hi.astype(F32), mid.astype(F32), lo.astype(F32)
        return jnp.where(row16 == 0, hi, jnp.where(row16 == 1, mid, jnp.where(row16 == 2, lo, 0.0))).astype(BF16)
    def load(s, _):
        x = x_ref[s]
        d = docs_ref[s]
        g = g_ref[s]
        dot = jnp.sum(g.astype(F32) * o_ref[s], axis=0, keepdims=True)
        low = three(lse_ref[s] * (-1.0 / C2))
        off = three(-dot)
        fm[s] = jnp.concatenate([
            x[0:HD], marks(d, False), low, pad,
            g, off, pad2,
            x[HD:2 * HD], marks(d, True), ones, pad,
            x[2 * HD:], ones, pad2], axis=0)
        return 0
    loop(SRC, load)
    pack_levels(fm)
    iden = eye(TOK)
    def turn(i, _):
        tm[i] = nt(iden, fm[i]).astype(BF16)
        return 0
    loop(30, turn); turn(30, 0)
    def segment(first, count):
        q = jnp.concatenate([fm[first + b, 0:AUG, :] for b in range(count)], axis=1)
        g = jnp.concatenate([fm[first + b, AUG:2 * AUG, :] for b in range(count)], axis=1)
        rows = pl.ds(first, count)
        qt = tm[rows, :, 0:AUG].reshape(count * TOK, AUG)
        gt = tm[rows, :, AUG:2 * AUG].reshape(count * TOK, AUG)
        parts = []
        for t in range(count):
            k = first + t
            p = jnp.exp2(nn(tm[k, :, 2 * AUG:3 * AUG], q) * C2)
            es = (p * nn(tm[k, :, 3 * AUG:], g)).astype(BF16)
            ev[k] = nn(p.astype(BF16), gt)
            ek[k] = nn(es, qt)
            parts.append(es)
        k = jnp.concatenate([fm[first + t, 2 * AUG:2 * AUG + HD, :] for t in range(count)], axis=1)
        out = nn(k, jnp.concatenate(parts, axis=0))
        for b in range(count):
            eq[first + b] = out[:, b * TOK:(b + 1) * TOK]
    loop(7, lambda i, _: segment(i * 4, 4), MAIN)
    segment(28, 2)
    segment(30, 1)

    for level in range(4, 0, -1):
        c = TOK >> level
        def join(g, _, level=level, c=c):
            child = FIRST[level] + g
            grid = spread_grid(c) if level > 1 else None
            for half in range(2):
                mine = FIRST[level - 1] + 2 * g + half
                got = eq[child, :, half * 128:half * 128 + 128]
                if level > 1:
                    eq[mine] += spread(got, grid)
                else:
                    eq[mine, :, 0:128] += got
                for s in range(128 // c):
                    ek[mine, 2 * c * s:2 * c * s + c, :] += ek[child, half * 128 + c * s:half * 128 + c * s + c, :]
                    ev[mine, 2 * c * s:2 * c * s + c, :] += ev[child, half * 128 + c * s:half * 128 + c * s + c, :]
            return 0
        loop(BLOCKS[level], join)
    small = (lax.broadcasted_iota(jnp.int32, (HD, AUG), 0) == lax.broadcasted_iota(jnp.int32, (HD, AUG), 1)).astype(BF16)
    def finish(s, _):
        a = (eq[s] * ROOT).astype(BF16)
        b = nt(small, (ek[s] * ROOT).astype(BF16)).astype(BF16)
        v = nt(small, ev[s].astype(BF16)).astype(BF16)
        e_ref[s] = jnp.concatenate([a, b, v], axis=0)
        return 0
    loop(SRC, finish)

def attn_bwd(x, g, docs, o, lse):
    return pl.pallas_call(
        bwd_kernel,
        out_shape=jax.ShapeDtypeStruct((SRC, 3 * HD, TOK), BF16),
        in_specs=[pl.BlockSpec(memory_space=pltpu.VMEM)] * 5,
        out_specs=pl.BlockSpec(memory_space=pltpu.VMEM),
        scratch_shapes=[
            pltpu.VMEM((31, 4 * AUG, TOK), BF16),
            pltpu.VMEM((31, TOK, 4 * AUG), BF16),
            pltpu.VMEM((31, HD, TOK), F32),
            pltpu.VMEM((31, TOK, AUG), F32),
            pltpu.VMEM((31, TOK, AUG), F32),
        ],
        compiler_params=pltpu.CompilerParams(vmem_limit_bytes=56 * 2**20),
        cost_estimate=pl.CostEstimate(flops=28 * 10**9, bytes_accessed=6 * 2**20, transcendentals=0),
        name="attend_back",
    )(x, g, docs, o, lse)


def layer_norm(values, gain_row, shift_row):
    center = values - jnp.mean(values, axis=-1, keepdims=True)
    scale = lax.rsqrt(jnp.mean(center * center, axis=-1, keepdims=True) + epsilon)
    unit = center * scale
    return unit, scale, (unit * gain_row + shift_row).astype(BF16)


def layer_norm_back(grad, unit, scale, gain_row):
    pulled = grad * gain_row
    return (
        pulled
        - jnp.mean(pulled, axis=-1, keepdims=True)
        - unit * jnp.mean(pulled * unit, axis=-1, keepdims=True)
    ) * scale


def gelu_parts(values):
    share = 0.5 * (1.0 + lax.erf(values * math.sqrt(0.5)))
    slope = share + values * jnp.exp(-0.5 * values * values) * (1.0 / math.sqrt(2 * math.pi))
    return (values * share).astype(BF16), slope


def head_order():
    block = np.array([int(f"{k:04b}"[::-1], 2) for k in range(16)])
    heads = np.arange(HEADS)[:, None, None]
    residue = (heads + block[None, :, None]) % 16
    return (np.arange(16)[None, None, :] * 16 + residue).reshape(HEADS, TOK)


def cube_forward(hidden, params, order, docs, trade, window):
    w_qkv, w_out, w_mlp, gains, biases, up_bias = params
    unit_one, scale_one, normed = layer_norm(hidden, gains[0], biases[0])
    mixed = jnp.einsum("df,td->ft", w_qkv, normed, preferred_element_type=F32)
    shift = jnp.concatenate([biases[1], jnp.zeros_like(biases[1]), biases[2]])
    mixed = (mixed + shift[:, None]).astype(BF16)
    mixed = mixed.reshape(3, HEADS, HEAD_DIM, TOK).transpose(1, 0, 2, 3).reshape(HEADS, 3 * HEAD_DIM, TOK)
    mixed = jnp.einsum("hft,htu->hfu", mixed, order, preferred_element_type=F32).astype(BF16)
    heads = trade(mixed)
    merged, merged_low, summary = attn_fwd(heads, docs)
    merged_low, window = lax.optimization_barrier((merged_low, window))
    attended = trade(merged_low)
    attended = jnp.einsum("hdu,htu->hdt", attended, order, preferred_element_type=F32).astype(BF16)
    attended = attended.reshape(D, TOK)
    middle = hidden + jnp.einsum("ft,fd->td", attended, w_out, preferred_element_type=F32) + biases[3]
    unit_two, scale_two, normed_two = layer_norm(middle, gains[1], biases[4])
    ff = up_bias.shape[0]
    upward = jnp.dot(normed_two, w_mlp[:, :ff], preferred_element_type=F32) + up_bias
    activated, slope = gelu_parts(upward)
    result = middle + biases[5]
    for at in range(0, ff, D):
        result = result + jnp.dot(activated[:, at : at + D], w_mlp[:, ff + at : ff + at + D], preferred_element_type=F32)
    kept = (unit_one, scale_one, normed, heads, merged, summary, attended, unit_two, scale_two, normed_two, slope, activated)
    return result.astype(BF16), kept, window


def columns_of(values, at, number, over=0):
    place = (jnp.arange(128)[None, :] == at + number).astype(values.dtype)
    place = jnp.broadcast_to(place, (values.shape[over], 128))
    precision = highest if values.dtype == F32 else None
    return lax.dot_general(values, place, (((over,), (0,)), ((), ())), precision=precision, preferred_element_type=F32)


def turned_rows(kept, turn):
    attended, normed_two, activated = kept[6], kept[9], kept[11]
    return (
        moved(normed_two, turn, "tf,fp->tp"),
        moved(attended, turn, "ft,fp->pt"),
        [moved(activated[:, k : k + D], turn, "tf,fp->tp") for k in range(0, activated.shape[1], D)],
    )


def cube_backward(incoming_low, kept, params, order, docs, trade, before, between, window, send_rest, at, turn):
    w_qkv, w_out, w_mlp, gains, biases, up_bias = params
    unit_one, scale_one, normed, heads, merged, summary, attended, unit_two, scale_two, normed_two, slope, activated = kept
    ff = up_bias.shape[0]
    incoming = incoming_low.astype(F32)
    act_grad = jnp.concatenate([
        jnp.einsum("tb,ab->ta", incoming_low, w_mlp[:, ff + at : ff + at + D], preferred_element_type=F32)
        for at in range(0, ff, D)
    ], axis=1)
    up_grad = (act_grad * slope).astype(BF16)
    norm_two_grad = jnp.einsum("tb,ab->ta", up_grad, w_mlp[:, :ff], preferred_element_type=F32)
    middle_grad = incoming + layer_norm_back(norm_two_grad, unit_two, scale_two, gains[1])
    branch_grad = middle_grad.astype(BF16)
    merged_grad = jnp.einsum("fd,td->ft", w_out, branch_grad, preferred_element_type=F32).astype(BF16)
    merged_grad = merged_grad.reshape(HEADS, HEAD_DIM, TOK)
    merged_grad = jnp.einsum("hdt,htu->hdu", merged_grad, order, preferred_element_type=F32).astype(BF16)
    turned_two, turned, hidden_units = turn
    grad_rest = jnp.concatenate(
        [inner_rows(turned_two, up_grad).astype(BF16)]
        + [inner_rows(part, incoming_low).astype(BF16) for part in hidden_units]
        + [jnp.einsum("pt,td->pd", turned, branch_grad, preferred_element_type=F32).astype(BF16)],
        axis=1,
    )
    lifts = sum(columns_of(up_grad[:, k * D : (k + 1) * D], at, 8 + k) for k in range(4))
    merged_grad = trade(merged_grad)
    small = (
        columns_of(norm_two_grad * unit_two, at, 1)
        + columns_of(branch_grad, at, 5)
        + columns_of(norm_two_grad, at, 6)
        + columns_of(incoming_low, at, 7)
        + lifts
    )
    merged_grad, grad_rest, before = lax.optimization_barrier((merged_grad, grad_rest, before))
    sums_rest = send_rest(grad_rest)
    back_heads = attn_bwd(heads, merged_grad, docs, merged, summary)
    back_heads, window = lax.optimization_barrier((back_heads, window))
    mixed_grad = trade(back_heads)
    mixed_grad, before, small = lax.optimization_barrier((mixed_grad, between(before), small))
    mixed_grad = jnp.einsum("hfu,htu->hft", mixed_grad, order, preferred_element_type=F32).astype(BF16)
    mixed_grad = mixed_grad.reshape(HEADS, 3, HEAD_DIM, TOK).transpose(1, 0, 2, 3).reshape(3 * D, TOK)
    grad_qkv = jnp.einsum("td,ft->df", normed, mixed_grad, preferred_element_type=F32).astype(BF16)
    normed_grad = jnp.einsum("ft,df->td", mixed_grad, w_qkv, preferred_element_type=F32)
    start_grad = middle_grad + layer_norm_back(normed_grad, unit_one, scale_one, gains[0])
    late = (
        columns_of(normed_grad * unit_one, at, 0)
        + columns_of(normed_grad, at, 2)
        + columns_of(mixed_grad[:D], at, 3, 1)
        + columns_of(mixed_grad[2 * D :], at, 4, 1)
    )
    return start_grad, (grad_qkv, sums_rest, small + late), before, window


def half_pairs(source, count):
    return [(source * count + j, (1 - source) * count + j) for j in range(count)]


def core_swap(value, bit):
    return lax.ppermute(value, "seq", [(j, j ^ (1 << bit)) for j in range(16)])


def section_swap(value):
    return lax.ppermute(value, "section", [(0, 1), (1, 0)])


def place_bit(bit):
    return (lax.axis_index("seq") >> bit) & 1


def team(kind):
    def device(x, z, y, c):
        return x * 16 + z * 4 + y * 2 + c
    two, four = range(2), range(4)
    if kind == "whole plane":
        return [[device(x, z, y, c) for x in two for y in two for c in two] for z in four]
    if kind == "plane":
        return [[device(x, z, y, c) for x in two for y in two] for z in four for c in two]
    return [[device(x, z, y, c) for z in four] for x in two for y in two for c in two]


def plane_order():
    index = np.arange(D).reshape(4, 2, 2, 2, D // 32).transpose(3, 1, 2, 0, 4).reshape(D)
    place = np.empty(D, np.int32)
    place[index] = np.arange(D)
    return place


def moved(values, turn, equation):
    return jnp.einsum(equation, values, turn, preferred_element_type=F32).astype(BF16)


def team_trade(value, kind):
    return lax.all_to_all(value, ("section", "seq"), 0, 0, axis_index_groups=team(kind), tiled=True)


def collect_line(piece):
    return team_trade(jnp.broadcast_to(piece[None], (4,) + piece.shape), "line")


def collect_plane(now):
    rows, columns = now.shape[1:]
    now = team_trade(jnp.broadcast_to(now[None], (4,) + now.shape), "plane")
    now = now.reshape(2, 2, 4, rows, columns)
    got = core_swap(now, 0)
    upper = place_bit(0) == 1
    halves = []
    for x in range(2):
        a, b = now[x].transpose(1, 0, 2, 3), got[x].transpose(1, 0, 2, 3)
        both = jnp.stack([jnp.where(upper, b, a), jnp.where(upper, a, b)], axis=2)
        halves.append(both.reshape(16 * rows, columns))
    return halves


def plus(own, got, dtype=BF16):
    return (own.astype(F32) + got.astype(F32)).astype(dtype)


def fold(value, bit, axis, dtype=BF16):
    mine = place_bit(bit)
    away = lax.dynamic_index_in_dim(value, 1 - mine, axis, keepdims=False)
    kept = lax.dynamic_index_in_dim(value, mine, axis, keepdims=False)
    return plus(kept, core_swap(away, bit), dtype)


def reduce_core(partial):
    rows, half = partial.shape[0] // 16, partial.shape[1] // 2
    now = fold(partial.reshape(8, 2, rows, 2 * half), 0, 1).reshape(4, 2, rows, 2 * half)
    return jnp.stack([now[:, y, :, x * half : x * half + half] for x in range(2) for y in range(2)])


def reduce_plane(now):
    return jnp.sum(team_trade(now, "plane").astype(F32), axis=0).astype(BF16)


def reduce_line(now):
    return jnp.sum(team_trade(now, "line").astype(F32), axis=0)


def cube_body(inputs, cotangent, documents, w_qkv, w_out, w_up, w_down, norm_gains, biases, up_bias):
    section_id = lax.axis_index("section")
    place = lax.axis_index("seq")
    count = lax.axis_size("seq")
    half = count // 2
    micro_id = place // half
    member = section_id * half + place % half
    teams = [[s * count + k * half + j for s in range(2) for j in range(half)] for k in range(2)]
    axes = ("section", "seq")
    lower = section_id == 0

    def trade(value):
        return lax.all_to_all(value, axes, 0, 0, axis_index_groups=teams, tiled=True)

    def across(value, pairs):
        return lax.ppermute(value, axes, pairs)

    def own_rows(pair):
        mine = jnp.where(micro_id == 0, pair[0], pair[1])
        other = jnp.where(micro_id == 0, pair[1], pair[0])
        swap = across(other, [(count + j, count + (j ^ half)) for j in range(count)])
        return jnp.where(lower, mine, swap)

    turn = (jnp.asarray(plane_order())[:, None] == jnp.arange(D)[None, :]).astype(BF16)
    table = jnp.asarray(head_order())
    order = (table[:, None, :] == jnp.arange(TOK)[None, :, None]).astype(BF16)
    docs = jnp.where(micro_id == 0, documents[0], documents[1]).reshape(count, TOK)
    docs = jnp.where(micro_id == 0, docs, jnp.roll(docs, half, axis=0))
    own_order = lax.dynamic_index_in_dim(order, member, 0, keepdims=False)
    docs = jnp.dot(docs.astype(BF16), own_order, preferred_element_type=F32).reshape(count, 1, TOK)

    hidden = own_rows(inputs)
    wide = D // count
    lift = up_bias[0].reshape(-1, wide)
    small = jnp.concatenate([norm_gains[0], biases[0], lift]).T.astype(BF16)
    small = jnp.pad(small, ((0, 0), (0, 128 - small.shape[1])))

    ff = w_up.shape[2]
    low_qkv = w_qkv[0].astype(BF16)
    columns = low_qkv.shape[1] // 2
    got = across(low_qkv[:, columns:], half_pairs(0, count))
    piece = jnp.where(lower, low_qkv[:, :columns], got)
    line = collect_line(jnp.concatenate([piece, small], axis=1))

    piece, w_up, w_down = lax.optimization_barrier((piece, w_up, w_down))
    up_shard = w_up[0].astype(BF16).reshape(wide, count, 4, wide).transpose(0, 2, 1, 3).reshape(wide, ff)
    down_shard = w_down[0].astype(BF16).reshape(4, wide, D).transpose(1, 0, 2).reshape(wide, 4 * D)
    shard = jnp.concatenate([up_shard, down_shard, w_out[0].astype(BF16), low_qkv], axis=1)
    rows, rest = wide // 2, 2 * ff + D
    got = section_swap(jnp.where(lower, shard[rows:], shard[:rows]))
    near = jnp.concatenate([jnp.where(lower, shard[:rows, :rest], got[:, :rest]), jnp.where(lower, got, shard[rows:])[:, rest:]], axis=1)
    far = jnp.where(lower, got[:, :rest], shard[rows:, :rest])
    near, far, line, hidden = lax.optimization_barrier((near, far, line, hidden))
    parts = collect_plane(line)
    qkv_first = jnp.concatenate([part[:, :columns] for part in parts], axis=1)
    near = lax.all_gather(near, ("seq", "section"), axis=0, tiled=True)
    rest_final = lax.all_gather(far, ("seq", "section"), axis=0, tiled=True)
    rest_first, qkv_final = near[:, :rest], near[:, rest:]

    def lines(columns):
        values = columns[:, :12].astype(F32).T
        return values[:2], values[2:8], values[8:].reshape(ff)

    lines_first, lines_final = lines(parts[0][:, columns:]), lines(parts[1][:, columns:])
    params_first = (qkv_first, rest_first[:, 2 * ff :], rest_first) + lines_first
    beyond = [(count + j, count + (j ^ half)) for j in range(count)]
    back_over = [(count + j, j ^ half) for j in range(count)]
    first, kept_first, start_back = cube_forward(
        hidden.astype(F32), params_first, order, docs, trade, own_rows(cotangent)
    )
    params_final = (qkv_final, rest_final[:, 2 * ff :], rest_final) + lines_final
    final, kept_final, (far, turned_first) = cube_forward(
        first.astype(F32), params_final, order, docs, trade, (across(first, back_over), turned_rows(kept_first, turn))
    )

    def placed(mine, other):
        return jnp.where(micro_id == 0, jnp.stack([mine, other]), jnp.stack([other, mine]))[None]

    def scattered(partial):
        return lax.psum_scatter(
            partial, axes, scatter_dimension=0, tiled=True, axis_index_groups=team("whole plane")
        )

    def fold_line(partial):
        return fold(partial.reshape(2, 2, rows, -1), 3, 0)

    start_back, merged = lax.optimization_barrier((start_back, kept_final[4]))
    kept_final = kept_final[:4] + (merged,) + kept_final[5:]
    grad_final, terms_final, _, window = cube_backward(
        start_back, kept_final, params_final, order, docs, trade, None, lambda now: now,
        (across(final, half_pairs(0, count)), across(final, beyond)), scattered, 12,
        turned_rows(kept_final, turn),
    )
    layer_outputs = placed(jnp.where(lower, first, window[0]), jnp.where(lower, far, window[1]))
    sent, qkv_final, small_final = lax.optimization_barrier(
        (grad_final.astype(BF16), terms_final[0], terms_final[2])
    )
    grad_first, terms_first, qkv_final, window = cube_backward(
        sent, kept_first, params_first, order, docs, trade, reduce_core(qkv_final), reduce_plane,
        (across(sent, half_pairs(0, count)), across(sent, beyond), fold_line(terms_final[1])), scattered, 0,
        turned_first,
    )
    rest_final = fold(window[2], 2, 0)

    smalls = (terms_first[2] + small_final).astype(BF16)
    smalls = fold(smalls.reshape(8, 2, wide, 128), 0, 1).reshape(4, 2, wide, 128)
    smalls = jnp.stack([smalls[:, 0], smalls[:, 1]] * 2)
    now = jnp.concatenate([reduce_core(terms_first[0]), smalls], axis=3)
    plane, far_back = lax.optimization_barrier((reduce_plane(now), across(grad_first.astype(BF16), back_over)))
    now = reduce_line(jnp.concatenate([plane, qkv_final], axis=2))
    now, rest_first = lax.optimization_barrier((now, fold_line(terms_first[1])))
    columns = qkv_final.shape[2]
    qkv_first, smalls, qkv_final = now[:, :columns], now[:, columns : columns + 24], now[:, columns + 128 :]
    smalls = jnp.where(lower, smalls[:, :12], smalls[:, 12:]).T
    rest_first = fold(rest_first, 2, 0)
    input_grads = placed(
        jnp.where(lower, grad_first, window[0].astype(F32)), jnp.where(lower, far_back, window[1]).astype(F32)
    )

    away = section_swap(jnp.where(lower, rest_final, rest_first))
    rest = jnp.where(lower, jnp.concatenate([rest_first, away]), jnp.concatenate([away, rest_final]))
    qkv_final, qkv_first, layer_outputs = lax.optimization_barrier((qkv_final, qkv_first, layer_outputs))
    away = section_swap(jnp.where(lower, qkv_final, qkv_first).astype(BF16)).astype(F32)
    qkv = jnp.where(
        lower, jnp.concatenate([qkv_first, away], axis=1), jnp.concatenate([away, qkv_final], axis=1)
    )
    up = rest[:, :ff].astype(F32).reshape(wide, 4, count, wide).transpose(0, 2, 1, 3).reshape(wide, ff)
    rest = rest[:, ff:].astype(F32)
    down = rest[:, :ff].reshape(wide, 4, D).transpose(1, 0, 2).reshape(4 * wide, D)
    return (
        layer_outputs,
        input_grads,
        qkv[None],
        rest[None, :, ff:],
        up[None],
        down[None],
        smalls[None, :2],
        smalls[None, 2:8],
        smalls[8:].reshape(1, -1),
    )


def solution(mesh):
    cube = mesh.shape["seq"] == 16
    return jax.shard_map(
        cube_body if cube else body,
        mesh=mesh,
        in_specs=(
            P(None, "seq", None),
            P(None, "seq", None),
            P(),
            P("section", "seq", None),
            P("section", "seq", None),
            P("section", "seq", None),
            P("section", "seq", None),
            P("section", None, "seq"),
            P("section", None, "seq"),
            P("section", "seq"),
        ),
        out_specs=(
            P("section", None, "seq", None),
            P("section", None, "seq", None),
            P("section", "seq", None),
            P("section", "seq", None),
            P("section", "seq", None),
            P("section", "seq", None),
            P("section", None, "seq"),
            P("section", None, "seq"),
            P("section", "seq"),
        ),
        check_vma=False,
    )
```

```python
import functools
import math

import jax
import jax.numpy as jnp
import numpy as np
from jax import lax
from jax.experimental import pallas as pl
from jax.experimental.pallas import tpu as pltpu
from jax.sharding import PartitionSpec as P

D = 768
HEADS = 16
HEAD_DIM = 48
SEG0 = 1024
BRANCHES = 5


epsilon = 1e-05
masked_score = -1e30
highest = lax.Precision.HIGHEST


def swapped(value, axis, apart):
    mask = 2**apart
    pairs = [(source, source ^ mask) for source in range(lax.axis_size(axis))]
    return lax.ppermute(value, axis, pairs)


def for_sending(array):
    return jax.tree.map(lambda a: a.astype(jnp.bfloat16) if a.dtype == jnp.float32 else a, array)


def passed_along(array, axis, by):
    peers = lax.axis_size(axis)
    pairs = [(i, i + by) for i in range(peers) if 0 <= i + by < peers]
    return lax.ppermute(array, axis, pairs)


def layer_norm_parts(values, gain_row, shift_row):
    center = values - jnp.mean(values, axis=-1, keepdims=True)
    spread = jnp.mean(center * center, axis=-1, keepdims=True)
    return center * lax.rsqrt(spread + epsilon) * gain_row + shift_row


def exact_gelu(values):
    return jax.nn.gelu(values, approximate=False)


def inner_rows(left, right):
    return jnp.einsum("ta,tb->ab", left, right, preferred_element_type=jnp.float32)


def geometry(tokens_dev, devices):
    groups = [
        min(SEG0 * 2**level_id, tokens_dev * devices) // tokens_dev for level_id in range(BRANCHES)
    ]
    return (groups, max(groups).bit_length() - 1)


def first_level(groups, step_id):
    return min((level_id for level_id in range(BRANCHES) if groups[level_id] > 2**step_id))


def pick_grid(level_id, dtype):
    dilation = 2**level_id
    return (jnp.arange(dilation)[:, None] == (jnp.arange(HEADS) % dilation)[None, :]).astype(dtype)


def select_rows(tensor, level_id):
    dilation = 2**level_id
    shaped = tensor.reshape((tensor.shape[0] // dilation, dilation) + tensor.shape[1:])
    if tensor.dtype == jnp.bfloat16:
        chosen = jnp.einsum(
            "jrh...,rh->jh...",
            shaped,
            pick_grid(level_id, jnp.bfloat16),
            preferred_element_type=jnp.float32,
        )
        return chosen.astype(jnp.bfloat16)
    return jnp.einsum(
        "jrh...,rh->jh...", shaped, pick_grid(level_id, jnp.float32), precision=highest
    )


def spread_rows(tensor, level_id):
    dilation = 2**level_id
    spread = jnp.einsum(
        "jh...,rh->jrh...", tensor, pick_grid(level_id, jnp.float32), precision=highest
    )
    return spread.reshape((tensor.shape[0] * dilation,) + tensor.shape[1:])


def spread_sums(tensor, level_id):
    dilation = 2**level_id
    grid = pick_grid(level_id, jnp.float32)
    spread = jnp.where(grid[None] > 0, tensor[:, None, :], masked_score)
    return spread.reshape(tensor.shape[0] * dilation, HEADS)


def doc_tables(documents_now, level_id, group, tokens_dev, seq_place):
    dilation = 2**level_id
    offsets = np.arange(HEADS) % dilation
    own_docs = lax.dynamic_slice_in_dim(documents_now, seq_place * tokens_dev, tokens_dev)
    own_docs = own_docs.reshape(tokens_dev // dilation, dilation)[:, offsets]
    seg_start = seq_place // group * group * tokens_dev
    seg_docs = lax.dynamic_slice_in_dim(documents_now, seg_start, group * tokens_dev)
    seg_docs = seg_docs.reshape(group * tokens_dev // dilation, dilation)[:, offsets]
    return (own_docs, seg_docs)


def head_bits(level_id):
    return jnp.arange(HEADS) >> level_id & 1


def halve(buffer, level_id):
    pairs = buffer.reshape(buffer.shape[0], buffer.shape[1] // 2, 2, HEADS, HEAD_DIM)
    chosen = head_bits(level_id)[None, None, :, None] == 1
    return jnp.where(chosen, pairs[:, :, 1], pairs[:, :, 0])


def widen(buffer, level_id):
    chosen = head_bits(level_id)[None, None, :, None] == 1
    empty = jnp.zeros_like(buffer)
    upper_part = jnp.where(chosen, buffer, empty)
    lower_part = jnp.where(chosen, empty, buffer)
    stacked = jnp.stack([lower_part, upper_part], axis=2)
    return stacked.reshape(buffer.shape[0], buffer.shape[1] * 2, HEADS, HEAD_DIM)


def thin_to(buffer, low_level, high_level):
    for level_id in range(low_level, high_level):
        buffer = halve(buffer, level_id)
    return buffer


def widen_to(buffer, low_level, high_level):
    for level_id in reversed(range(low_level, high_level)):
        buffer = widen(buffer, level_id)
    return buffer


def gather_keys(own_rows, groups, step_count, seq_place):
    results = [None] * BRANCHES
    current = own_rows
    level_now = 0
    for level_id in range(BRANCHES):
        pass
    for step_id in range(step_count):
        target = first_level(groups, step_id)
        current = thin_to(current, level_now, target)
        level_now = target
        row_count = current.shape[1]
        flat_rows = current.reshape(2, row_count, HEADS * HEAD_DIM)
        incoming = swapped(flat_rows, "seq", step_id).reshape(current.shape)
        upper_half = seq_place >> step_id & 1 == 1
        current = jnp.where(
            upper_half,
            jnp.concatenate([incoming, current], axis=1),
            jnp.concatenate([current, incoming], axis=1),
        )
        for level_id in range(BRANCHES):
            if groups[level_id] == 2 ** (step_id + 1):
                results[level_id] = thin_to(current, level_now, level_id)
    return results


def scatter_keys(key_grads, groups, step_count, seq_place):
    carried = None
    for step_id in reversed(range(step_count)):
        level_now = first_level(groups, step_id)
        total_grad = None
        if carried is not None:
            total_grad = widen_to(carried, level_now, first_level(groups, step_id + 1))
        for level_id in range(BRANCHES):
            if groups[level_id] == 2 ** (step_id + 1):
                branch_term = widen_to(key_grads[level_id], level_now, level_id)
                total_grad = branch_term if total_grad is None else total_grad + branch_term
        half_rows = total_grad.shape[1] // 2
        upper_half = seq_place >> step_id & 1 == 1
        own_half = jnp.where(upper_half, total_grad[:, half_rows:], total_grad[:, :half_rows])
        theirs = jnp.where(upper_half, total_grad[:, :half_rows], total_grad[:, half_rows:])
        flat_rows = theirs.reshape(2, half_rows, HEADS * HEAD_DIM)
        incoming = (
            swapped(for_sending(flat_rows), "seq", step_id)
            .astype(flat_rows.dtype)
            .reshape(own_half.shape)
        )
        carried = own_half + incoming
    own_grad = widen_to(carried, 0, first_level(groups, 0))
    for level_id in range(BRANCHES):
        pass
    return own_grad


def head_blocks(level_id):
    block_size = min(HEADS, 4 * 2**level_id)
    return (HEADS // block_size, block_size)


def to_blocks(tensor, block_count, block_size):
    moved = jnp.moveaxis(tensor, 1, 0)
    return moved.reshape((block_count, block_size) + moved.shape[1:])


def from_blocks(tensor):
    joined = tensor.reshape((tensor.shape[0] * tensor.shape[1],) + tensor.shape[2:])
    return jnp.moveaxis(joined, 0, 1)


def score_block(query_block, key_block, query_doc, key_doc):
    scores = jnp.einsum(
        "hqd,hkd->hqk", query_block, key_block, preferred_element_type=jnp.float32
    ) * HEAD_DIM ** (-0.5)
    return jnp.where(query_doc[:, :, None] == key_doc[:, None, :], scores, masked_score)


def forward_block(pieces):
    query_block, key_block, value_block, query_doc, key_doc = pieces
    scores = score_block(query_block, key_block, query_doc, key_doc)
    row_max = jnp.max(scores, axis=-1, keepdims=True)
    weights = jnp.exp(scores - row_max)
    row_total = jnp.sum(weights, axis=-1, keepdims=True)
    prob_rows = (weights / row_total).astype(jnp.bfloat16)
    result = jnp.einsum("hqk,hkd->hqd", prob_rows, value_block, preferred_element_type=jnp.float32)
    return (result, (row_max + jnp.log(row_total))[:, :, 0])


def backward_block(pieces):
    query_block, key_block, value_block, query_doc, key_doc, summary, out_grad, summary_grad = (
        pieces
    )
    scores = score_block(query_block, key_block, query_doc, key_doc)
    prob_rows = jnp.exp(scores - summary[:, :, None])
    prob_grad = jnp.einsum(
        "hqd,hkd->hqk", out_grad, value_block, preferred_element_type=jnp.float32
    )
    score_grad = prob_rows * (
        prob_grad
        - jnp.sum(prob_rows * prob_grad, axis=-1, keepdims=True)
        + summary_grad[:, :, None]
    )
    score_grad = score_grad.astype(jnp.bfloat16)
    score_scale = HEAD_DIM ** (-0.5)
    query_grad = (
        jnp.einsum("hqk,hkd->hqd", score_grad, key_block, preferred_element_type=jnp.float32)
        * score_scale
    )
    key_grad = (
        jnp.einsum("hqk,hqd->hkd", score_grad, query_block, preferred_element_type=jnp.float32)
        * score_scale
    )
    value_grad = jnp.einsum(
        "hqk,hqd->hkd", prob_rows.astype(jnp.bfloat16), out_grad, preferred_element_type=jnp.float32
    )
    return (query_grad, key_grad, value_grad)


def branch_forward(query_sel, key_value, query_docs, key_docs, level_id):
    block_count, block_size = head_blocks(level_id)
    pieces = (
        to_blocks(query_sel, block_count, block_size),
        to_blocks(key_value[0], block_count, block_size),
        to_blocks(key_value[1], block_count, block_size),
        to_blocks(query_docs, block_count, block_size),
        to_blocks(key_docs, block_count, block_size),
    )
    results, summaries = lax.map(forward_block, pieces)
    return (from_blocks(results), from_blocks(summaries))


def branch_backward(
    query_sel, key_value, query_docs, key_docs, summary, out_grad, summary_grad, level_id
):
    block_count, block_size = head_blocks(level_id)
    pieces = (
        to_blocks(query_sel, block_count, block_size),
        to_blocks(key_value[0], block_count, block_size),
        to_blocks(key_value[1], block_count, block_size),
        to_blocks(query_docs, block_count, block_size),
        to_blocks(key_docs, block_count, block_size),
        to_blocks(summary, block_count, block_size),
        to_blocks(out_grad, block_count, block_size),
        to_blocks(summary_grad, block_count, block_size),
    )
    query_grad, key_grad, value_grad = lax.map(backward_block, pieces)
    return (from_blocks(query_grad), jnp.stack([from_blocks(key_grad), from_blocks(value_grad)]))


def layer_forward(hidden, params, documents_now, groups, step_count, seq_place):
    w_qkv, w_out, w_up, w_down, gains, biases, up_bias = params
    gains = gains.astype(jnp.float32)
    biases = biases.astype(jnp.float32)
    tokens_dev = hidden.shape[0]
    normed = layer_norm_parts(hidden, gains[0], biases[0]).astype(jnp.bfloat16)
    mixed_rows = jnp.dot(normed, w_qkv, preferred_element_type=jnp.float32)
    queries = (mixed_rows[:, :D] + biases[1]).astype(jnp.bfloat16)
    key_part = mixed_rows[:, D : 2 * D].astype(jnp.bfloat16)
    values = (mixed_rows[:, 2 * D :] + biases[2]).astype(jnp.bfloat16)
    own_rows = jnp.stack([key_part, values]).reshape(2, tokens_dev, HEADS, HEAD_DIM)
    gathered = gather_keys(own_rows, groups, step_count, seq_place)
    query_heads = queries.reshape(tokens_dev, HEADS, HEAD_DIM)
    picked, branch_outs, branch_sums = ([], [], [])
    for level_id in range(BRANCHES):
        query_sel = select_rows(query_heads, level_id)
        query_docs, key_docs = doc_tables(
            documents_now, level_id, groups[level_id], tokens_dev, seq_place
        )
        result, summary = branch_forward(
            query_sel, gathered[level_id], query_docs, key_docs, level_id
        )
        picked.append(query_sel)
        branch_outs.append(result)
        branch_sums.append(summary)
    full_sums = jnp.stack(
        [spread_sums(branch_sums[level_id], level_id) for level_id in range(BRANCHES)]
    )
    row_max = jnp.max(full_sums, axis=0)
    shares = jnp.exp(full_sums - row_max)
    shares = shares / jnp.sum(shares, axis=0)
    merged = sum(
        (
            shares[level_id][:, :, None] * spread_rows(branch_outs[level_id], level_id)
            for level_id in range(BRANCHES)
        )
    )
    attended = merged.reshape(tokens_dev, D).astype(jnp.bfloat16)
    middle = hidden + jnp.dot(attended, w_out, preferred_element_type=jnp.float32) + biases[3]
    normed_two = layer_norm_parts(middle, gains[1], biases[4]).astype(jnp.bfloat16)
    upward = jnp.dot(normed_two, w_up, preferred_element_type=jnp.float32) + up_bias.astype(
        jnp.float32
    )
    activated = exact_gelu(upward).astype(jnp.bfloat16)
    result = middle + jnp.dot(activated, w_down, preferred_element_type=jnp.float32) + biases[5]
    kept_values = (
        hidden,
        normed,
        picked,
        gathered,
        branch_sums,
        branch_outs,
        shares,
        merged,
        attended,
        middle,
        normed_two,
        upward,
        activated,
    )
    return (result, kept_values)


def layer_backward(incoming, kept_values, params, documents_now, groups, step_count, seq_place):
    w_qkv, w_out, w_up, w_down, gains, biases, up_bias = params
    gains = gains.astype(jnp.float32)
    biases = biases.astype(jnp.float32)
    (
        hidden,
        normed,
        picked,
        gathered,
        branch_sums,
        branch_outs,
        shares,
        merged,
        attended,
        middle,
        normed_two,
        upward,
        activated,
    ) = kept_values
    tokens_dev = hidden.shape[0]
    down_grad = incoming.astype(jnp.bfloat16)
    grad_down = inner_rows(activated, down_grad)
    grad_bias_down = jnp.sum(down_grad.astype(jnp.float32), axis=0)
    act_grad = jnp.einsum("tb,ab->ta", down_grad, w_down, preferred_element_type=jnp.float32)
    gelu_pulled = jax.vjp(exact_gelu, upward)
    up_grad = gelu_pulled[1](act_grad)[0].astype(jnp.bfloat16)
    grad_up = inner_rows(normed_two, up_grad)
    grad_up_bias = jnp.sum(up_grad.astype(jnp.float32), axis=0)
    norm_two_grad = jnp.einsum("tb,ab->ta", up_grad, w_up, preferred_element_type=jnp.float32)
    norm_pulled = jax.vjp(layer_norm_parts, middle, gains[1], biases[4])
    middle_part, grad_gain_two, grad_shift_two = norm_pulled[1](norm_two_grad)
    middle_grad = incoming + middle_part
    branch_grad = middle_grad.astype(jnp.bfloat16)
    grad_out = inner_rows(attended, branch_grad)
    grad_bias_out = jnp.sum(branch_grad.astype(jnp.float32), axis=0)
    merged_grad = jnp.einsum("tb,ab->ta", branch_grad, w_out, preferred_element_type=jnp.float32)
    merged_grad = merged_grad.reshape(tokens_dev, HEADS, HEAD_DIM)
    query_grad = jnp.zeros((tokens_dev, HEADS, HEAD_DIM), jnp.float32)
    key_grads = []
    for level_id in range(BRANCHES):
        share_sel = select_rows(shares[level_id], level_id)
        merged_sel = select_rows(merged, level_id)
        grad_sel = select_rows(merged_grad, level_id)
        out_grad = (share_sel[:, :, None] * grad_sel).astype(jnp.bfloat16)
        summary_grad = share_sel * (
            jnp.sum(grad_sel * branch_outs[level_id], axis=-1)
            - jnp.sum(grad_sel * merged_sel, axis=-1)
        )
        query_docs, key_docs = doc_tables(
            documents_now, level_id, groups[level_id], tokens_dev, seq_place
        )
        query_part, key_value_grad = branch_backward(
            picked[level_id],
            gathered[level_id],
            query_docs,
            key_docs,
            branch_sums[level_id],
            out_grad,
            summary_grad,
            level_id,
        )
        query_grad = query_grad + spread_rows(query_part, level_id)
        key_grads.append(key_value_grad)
    own_grad = scatter_keys(key_grads, groups, step_count, seq_place)
    mixed_grad = jnp.concatenate(
        [
            query_grad.reshape(tokens_dev, D),
            own_grad[0].reshape(tokens_dev, D),
            own_grad[1].reshape(tokens_dev, D),
        ],
        axis=1,
    ).astype(jnp.bfloat16)
    grad_qkv = inner_rows(normed, mixed_grad)
    grad_bias_query = jnp.sum(mixed_grad[:, :D].astype(jnp.float32), axis=0)
    grad_bias_value = jnp.sum(mixed_grad[:, 2 * D :].astype(jnp.float32), axis=0)
    normed_grad = jnp.einsum("tb,ab->ta", mixed_grad, w_qkv, preferred_element_type=jnp.float32)
    norm_pulled = jax.vjp(layer_norm_parts, hidden, gains[0], biases[0])
    hidden_part, grad_gain_one, grad_shift_one = norm_pulled[1](normed_grad)
    start_grad = middle_grad + hidden_part
    gradients = (
        grad_qkv,
        grad_out,
        grad_up,
        grad_down,
        jnp.stack([grad_gain_one, grad_gain_two]),
        jnp.stack(
            [
                grad_shift_one,
                grad_bias_query,
                grad_bias_value,
                grad_bias_out,
                grad_shift_two,
                grad_bias_down,
            ]
        ),
        grad_up_bias,
    )
    return (start_grad, gradients)


def body(inputs, cotangent, documents, w_qkv, w_out, w_up, w_down, norm_gains, biases, up_bias):
    section_id = lax.axis_index("section")
    seq_place = lax.axis_index("seq")
    devices = lax.axis_size("seq")
    micro = inputs.shape[0]
    tokens_dev = inputs.shape[1]
    groups, step_count = geometry(tokens_dev, devices)
    params = (
        lax.all_gather(w_qkv[0].astype(jnp.bfloat16), "seq", axis=0, tiled=True),
        lax.all_gather(w_out[0].astype(jnp.bfloat16), "seq", axis=0, tiled=True),
        lax.all_gather(w_up[0].astype(jnp.bfloat16), "seq", axis=0, tiled=True),
        lax.all_gather(w_down[0].astype(jnp.bfloat16), "seq", axis=0, tiled=True),
        lax.all_gather(norm_gains[0].astype(jnp.bfloat16), "seq", axis=1, tiled=True),
        lax.all_gather(biases[0].astype(jnp.bfloat16), "seq", axis=1, tiled=True),
        lax.all_gather(up_bias[0].astype(jnp.bfloat16), "seq", axis=0, tiled=True),
    )
    empty_rows = jnp.zeros((tokens_dev, D), jnp.bfloat16)
    received = empty_rows
    saved = []
    produced = []
    for tick_id in range(micro + 1):
        batch_index = jnp.clip(tick_id - section_id, 0, micro - 1)
        documents_now = lax.dynamic_index_in_dim(documents, batch_index, 0, keepdims=False)
        fresh_rows = inputs[tick_id] if tick_id < micro else empty_rows
        start_rows = jnp.where(section_id == 0, fresh_rows, received).astype(jnp.float32)
        result, kept_values = layer_forward(
            start_rows, params, documents_now, groups, step_count, seq_place
        )
        sent_rows = result.astype(jnp.bfloat16)
        produced.append(sent_rows)
        saved.append((kept_values, documents_now))
        if tick_id < micro:
            received = passed_along(sent_rows, "section", 1)
    back_received = empty_rows
    start_grads = []
    sent_grads = []
    totals = None
    shards = None
    for tick_id in range(micro + 1):
        earlier_save = saved[max(tick_id - 1, 0)]
        later_save = saved[min(tick_id + 1, micro)]
        kept_values, documents_now = jax.tree.map(
            lambda earlier, latter: jnp.where(section_id == 0, earlier, latter),
            earlier_save,
            later_save,
        )
        fresh_rows = cotangent[tick_id] if tick_id < micro else empty_rows
        incoming = jnp.where(section_id == 1, fresh_rows, back_received).astype(jnp.float32)
        start_grad, gradients = layer_backward(
            incoming, kept_values, params, documents_now, groups, step_count, seq_place
        )
        sent_rows = start_grad.astype(jnp.bfloat16)
        start_grads.append(start_grad)
        sent_grads.append(sent_rows.astype(jnp.float32))
        if tick_id < micro:
            back_received = passed_along(sent_rows, "section", -1)
        totals = (
            list(gradients)
            if totals is None
            else [earlier + latter for earlier, latter in zip(totals, gradients)]
        )
    shards = (
        lax.psum_scatter(totals[0], "seq", scatter_dimension=0, tiled=True),
        lax.psum_scatter(totals[1], "seq", scatter_dimension=0, tiled=True),
        lax.psum_scatter(totals[2], "seq", scatter_dimension=0, tiled=True),
        lax.psum_scatter(totals[3], "seq", scatter_dimension=0, tiled=True),
        lax.psum_scatter(totals[4], "seq", scatter_dimension=1, tiled=True),
        lax.psum_scatter(totals[5], "seq", scatter_dimension=1, tiled=True),
        lax.psum_scatter(totals[6], "seq", scatter_dimension=0, tiled=True),
    )
    layer_outputs = jnp.stack(
        [
            jnp.where(section_id == 0, produced[batch_id], produced[batch_id + 1])
            for batch_id in range(micro)
        ]
    )[None]
    input_grads = jnp.stack(
        [
            jnp.where(section_id == 0, start_grads[batch_id + 1], sent_grads[batch_id])
            for batch_id in range(micro)
        ]
    )[None]
    return (
        layer_outputs,
        input_grads,
        shards[0][None],
        shards[1][None],
        shards[2][None],
        shards[3][None],
        shards[4][None],
        shards[5][None],
        shards[6][None],
    )


HD = 48
AUG = 128
IDS = 32
SRC = 16
TOK = 256
ROOT = HD ** -0.5
C2 = ROOT * math.log2(math.e)
AWAY = -(2.0 ** 100)
BLOCKS = (16, 8, 4, 2, 1)
FIRST = (0, 16, 24, 28, 30)
F32, BF16 = jnp.float32, jnp.bfloat16

UN = 16
MAIN = 1
QW = 4
TWO = False

def loop(n, f, u=None):
    u = min(u or UN, n)
    while n % u:
        u -= 1
    def many(i, _):
        for j in range(u):
            f(i * u + j, 0)
        return 0
    lax.fori_loop(0, n // u, many, 0)

def nt(a, b):
    return lax.dot_general(a, b, (((1,), (1,)), ((), ())), preferred_element_type=F32)

def nn(a, b):
    return jnp.dot(a, b, preferred_element_type=F32)

def eye(n):
    return (lax.broadcasted_iota(jnp.int32, (n, n), 0) == lax.broadcasted_iota(jnp.int32, (n, n), 1)).astype(BF16)

def pack_grid(c):
    col = lax.broadcasted_iota(jnp.int32, (256, 128), 1)
    row = lax.broadcasted_iota(jnp.int32, (256, 128), 0)
    return (row == (col // c) * (2 * c) + col % c).astype(BF16)

def spread_grid(c):
    row = lax.broadcasted_iota(jnp.int32, (128, 256), 0)
    col = lax.broadcasted_iota(jnp.int32, (128, 256), 1)
    return (col == (row // c) * (2 * c) + row % c).astype(BF16)

def split3(v):
    hi = v.astype(BF16)
    r = v - hi.astype(F32)
    mid = r.astype(BF16)
    lo = (r - mid.astype(F32)).astype(BF16)
    return hi, mid, lo

def spread(v, grid):
    hi, mid, lo = split3(v)
    return nn(hi, grid) + nn(mid, grid) + nn(lo, grid)

def pack_levels(stack):
    for level in range(1, 5):
        c = TOK >> level
        def step(g, _, level=level, c=c):
            a = stack[FIRST[level - 1] + 2 * g]
            b = stack[FIRST[level - 1] + 2 * g + 1]
            if level == 1:
                pa, pb = a[:, :128], b[:, :128]
            else:
                grid = pack_grid(c)
                pa, pb = nn(a, grid).astype(BF16), nn(b, grid).astype(BF16)
            stack[FIRST[level] + g] = jnp.concatenate([pa, pb], axis=1)
            return 0
        loop(BLOCKS[level], step)

def marks(doc_row, away):
    ids = lax.broadcasted_iota(jnp.int32, (IDS, TOK), 0).astype(F32)
    same = ids == doc_row
    return (jnp.where(same, 0.0, AWAY) if away else jnp.where(same, 1.0, 0.0)).astype(BF16)

def fwd_kernel(x_ref, docs_ref, ob_ref, lse_ref, fm, ktm, part, *, kc):
    pad = jnp.zeros((AUG - HD - IDS, TOK), BF16)
    def load(s, _):
        x = x_ref[s]
        d = docs_ref[s]
        fm[s] = jnp.concatenate([x[0:HD], marks(d, False), pad, x[HD:2 * HD], marks(d, True), pad, x[2 * HD:]], axis=0)
        return 0
    loop(SRC, load)
    pack_levels(fm)
    iden = eye(TOK)
    def turn(i, _):
        ktm[i] = nt(iden, fm[i, AUG:2 * AUG, :]).astype(BF16)
        return 0
    loop(30, turn); turn(30, 0)

    def segment(first, count):
        for at in range(0, count, QW):
            n = min(QW, count - at)
            q = jnp.concatenate([fm[first + at + b, 0:AUG, :] for b in range(n)], axis=1)
            scores = [nn(ktm[first + t], q) for t in range(count)]
            top = functools.reduce(jnp.maximum, [jnp.max(x, axis=0, keepdims=True) for x in scores])
            ps = [jnp.exp2((x - top) * C2) for x in scores]
            total = functools.reduce(jnp.add, [jnp.sum(p, axis=0, keepdims=True) for p in ps])
            p = jnp.concatenate([p.astype(BF16) for p in ps], axis=0)
            v = jnp.concatenate([fm[first + t, 2 * AUG:2 * AUG + HD, :] for t in range(count)], axis=1)
            out = nn(v, p)
            for b in range(n):
                part[first + at + b, 0:HD] = out[:, b * TOK:(b + 1) * TOK]
                part[first + at + b, HD:HD + 8] = jnp.broadcast_to(total[:, b * TOK:(b + 1) * TOK], (8, TOK))
                part[first + at + b, HD + 8:HD + 16] = jnp.broadcast_to(top[:, b * TOK:(b + 1) * TOK] * C2, (8, TOK))
    loop(7, lambda i, _: segment(i * 4, 4), MAIN)
    segment(28, 2)
    segment(30, 1)

    for level in range(4, 0, -1):
        c = TOK >> level
        def join(g, _, level=level, c=c):
            child = FIRST[level] + g
            grid = spread_grid(c) if level > 1 else None
            for half in range(2):
                mine = FIRST[level - 1] + 2 * g + half
                got = part[child, :, half * 128:half * 128 + 128]
                if level > 1:
                    got = spread(got, grid)
                else:
                    got = jnp.concatenate([got, jnp.zeros_like(got)], axis=1)
                own = part[mine]
                cl, cm = got[HD:HD + 1], got[HD + 8:HD + 9]
                cm = jnp.where(cl > 0, cm, AWAY)
                ol, om = own[HD:HD + 1], own[HD + 8:HD + 9]
                top = jnp.maximum(cm, om)
                wc, wo = jnp.exp2(cm - top), jnp.exp2(om - top)
                part[mine, 0:HD] = got[0:HD] * wc + own[0:HD] * wo
                part[mine, HD:HD + 8] = jnp.broadcast_to(cl * wc + ol * wo, (8, TOK))
                part[mine, HD + 8:HD + 16] = jnp.broadcast_to(top, (8, TOK))
            return 0
        loop(BLOCKS[level], join)
    def finish(s, _):
        own = part[s]
        l, m = own[HD:HD + 1], own[HD + 8:HD + 9]
        out = own[0:HD] / l
        ob_ref[s] = out.astype(BF16)
        lse_ref[s] = m + jnp.log2(l)
        return 0
    loop(SRC, finish)

def attn_fwd(x, docs):
    return pl.pallas_call(
        functools.partial(fwd_kernel, kc=256),
        out_shape=(jax.ShapeDtypeStruct((SRC, HD, TOK), BF16), jax.ShapeDtypeStruct((SRC, 1, TOK), F32)),
        in_specs=[pl.BlockSpec(memory_space=pltpu.VMEM)] * 2,
        out_specs=[pl.BlockSpec(memory_space=pltpu.VMEM)] * 2,
        scratch_shapes=[
            pltpu.VMEM((31, 2 * AUG + HD, TOK), BF16),
            pltpu.VMEM((31, TOK, AUG), BF16),
            pltpu.VMEM((31, HD + 16, TOK), F32),
        ],
        compiler_params=pltpu.CompilerParams(vmem_limit_bytes=50 * 2**20),
        cost_estimate=pl.CostEstimate(flops=18 * 10**9, bytes_accessed=3 * 2**20, transcendentals=0),
        name="attend",
    )(x, docs)

def bwd_kernel(x_ref, g_ref, docs_ref, o_ref, lse_ref, e_ref, fm, tm, eq, ek, ev):
    pad = jnp.zeros((AUG - HD - IDS - 16, TOK), BF16)
    pad2 = jnp.zeros((AUG - HD - 16, TOK), BF16)
    row16 = lax.broadcasted_iota(jnp.int32, (16, TOK), 0)
    ones = jnp.where(row16 < 3, 1.0, 0.0).astype(BF16)
    def three(v):
        hi, mid, lo = split3(v)
        hi, mid, lo = hi.astype(F32), mid.astype(F32), lo.astype(F32)
        return jnp.where(row16 == 0, hi, jnp.where(row16 == 1, mid, jnp.where(row16 == 2, lo, 0.0))).astype(BF16)
    def load(s, _):
        x = x_ref[s]
        d = docs_ref[s]
        g = g_ref[s]
        dot = jnp.sum(g.astype(F32) * o_ref[s].astype(F32), axis=0, keepdims=True)
        low = three(lse_ref[s] * (-1.0 / C2))
        off = three(-dot)
        fm[s] = jnp.concatenate([
            x[0:HD], marks(d, False), low, pad,
            g, off, pad2,
            x[HD:2 * HD], marks(d, True), ones, pad,
            x[2 * HD:], ones, pad2], axis=0)
        return 0
    loop(SRC, load)
    pack_levels(fm)
    iden = eye(TOK)
    def turn(i, _):
        tm[i] = nt(iden, fm[i]).astype(BF16)
        return 0
    loop(30, turn); turn(30, 0)
    def segment(first, count):
        q = jnp.concatenate([fm[first + b, 0:AUG, :] for b in range(count)], axis=1)
        g = jnp.concatenate([fm[first + b, AUG:2 * AUG, :] for b in range(count)], axis=1)
        rows = pl.ds(first, count)
        qt = tm[rows, :, 0:AUG].reshape(count * TOK, AUG)
        gt = tm[rows, :, AUG:2 * AUG].reshape(count * TOK, AUG)
        parts = []
        for t in range(count):
            k = first + t
            p = jnp.exp2(nn(tm[k, :, 2 * AUG:3 * AUG], q) * C2)
            es = (p * nn(tm[k, :, 3 * AUG:], g)).astype(BF16)
            ev[k] = nn(p.astype(BF16), gt)
            ek[k] = nn(es, qt)
            parts.append(es)
        k = jnp.concatenate([fm[first + t, 2 * AUG:2 * AUG + HD, :] for t in range(count)], axis=1)
        out = nn(k, jnp.concatenate(parts, axis=0))
        for b in range(count):
            eq[first + b] = out[:, b * TOK:(b + 1) * TOK]
    loop(7, lambda i, _: segment(i * 4, 4), MAIN)
    segment(28, 2)
    segment(30, 1)

    for level in range(4, 0, -1):
        c = TOK >> level
        def join(g, _, level=level, c=c):
            child = FIRST[level] + g
            grid = spread_grid(c) if level > 1 else None
            for half in range(2):
                mine = FIRST[level - 1] + 2 * g + half
                got = eq[child, :, half * 128:half * 128 + 128]
                if level > 1:
                    eq[mine] += spread(got, grid)
                else:
                    eq[mine, :, 0:128] += got
                for s in range(128 // c):
                    ek[mine, 2 * c * s:2 * c * s + c, :] += ek[child, half * 128 + c * s:half * 128 + c * s + c, :]
                    ev[mine, 2 * c * s:2 * c * s + c, :] += ev[child, half * 128 + c * s:half * 128 + c * s + c, :]
            return 0
        loop(BLOCKS[level], join)
    small = (lax.broadcasted_iota(jnp.int32, (HD, AUG), 0) == lax.broadcasted_iota(jnp.int32, (HD, AUG), 1)).astype(BF16)
    def finish(s, _):
        a = (eq[s] * ROOT).astype(BF16)
        b = nt(small, (ek[s] * ROOT).astype(BF16)).astype(BF16)
        v = nt(small, ev[s].astype(BF16)).astype(BF16)
        e_ref[s] = jnp.concatenate([a, b, v], axis=0)
        return 0
    loop(SRC, finish)

def attn_bwd(x, g, docs, o, lse):
    return pl.pallas_call(
        bwd_kernel,
        out_shape=jax.ShapeDtypeStruct((SRC, 3 * HD, TOK), BF16),
        in_specs=[pl.BlockSpec(memory_space=pltpu.VMEM)] * 5,
        out_specs=pl.BlockSpec(memory_space=pltpu.VMEM),
        scratch_shapes=[
            pltpu.VMEM((31, 4 * AUG, TOK), BF16),
            pltpu.VMEM((31, TOK, 4 * AUG), BF16),
            pltpu.VMEM((31, HD, TOK), F32),
            pltpu.VMEM((31, TOK, AUG), F32),
            pltpu.VMEM((31, TOK, AUG), F32),
        ],
        compiler_params=pltpu.CompilerParams(vmem_limit_bytes=56 * 2**20),
        cost_estimate=pl.CostEstimate(flops=28 * 10**9, bytes_accessed=6 * 2**20, transcendentals=0),
        name="attend_back",
    )(x, g, docs, o, lse)


def layer_norm(values, gain_row, shift_row):
    center = values - jnp.mean(values, axis=-1, keepdims=True)
    scale = lax.rsqrt(jnp.mean(center * center, axis=-1, keepdims=True) + epsilon)
    unit = center * scale
    return unit, scale, (unit * gain_row + shift_row).astype(BF16)


def layer_norm_back(grad, unit, scale, gain_row):
    pulled = grad * gain_row
    return (
        pulled
        - jnp.mean(pulled, axis=-1, keepdims=True)
        - unit * jnp.mean(pulled * unit, axis=-1, keepdims=True)
    ) * scale


def gelu_parts(values):
    share = 0.5 * (1.0 + lax.erf(values * math.sqrt(0.5)))
    slope = share + values * jnp.exp(-0.5 * values * values) * (1.0 / math.sqrt(2 * math.pi))
    return (values * share).astype(BF16), slope


def head_order():
    block = np.array([int(f"{k:04b}"[::-1], 2) for k in range(16)])
    heads = np.arange(HEADS)[:, None, None]
    residue = (heads + block[None, :, None]) % 16
    return (np.arange(16)[None, None, :] * 16 + residue).reshape(HEADS, TOK)


def cube_forward(hidden, params, order, docs, trade, window):
    w_qkv, w_out, w_mlp, gains, biases, up_bias = params
    unit_one, scale_one, normed = layer_norm(hidden, gains[0], biases[0])
    mixed = jnp.einsum("df,td->ft", w_qkv, normed, preferred_element_type=F32)
    shift = jnp.concatenate([biases[1], jnp.zeros_like(biases[1]), biases[2]])
    mixed = (mixed + shift[:, None]).astype(BF16)
    mixed = mixed.reshape(3, HEADS, HEAD_DIM, TOK).transpose(1, 0, 2, 3).reshape(HEADS, 3 * HEAD_DIM, TOK)
    mixed = jnp.einsum("hft,htu->hfu", mixed, order, preferred_element_type=F32).astype(BF16)
    heads = trade(mixed)
    merged_low, summary = attn_fwd(heads, docs)
    merged_low, window = lax.optimization_barrier((merged_low, window))
    merged = merged_low
    attended = trade(merged_low)
    attended = jnp.einsum("hdu,htu->hdt", attended, order, preferred_element_type=F32).astype(BF16)
    attended = attended.reshape(D, TOK)
    middle = hidden + jnp.einsum("ft,fd->td", attended, w_out, preferred_element_type=F32) + biases[3]
    unit_two, scale_two, normed_two = layer_norm(middle, gains[1], biases[4])
    ff = up_bias.shape[0]
    upward = jnp.dot(normed_two, w_mlp[:, :ff], preferred_element_type=F32) + up_bias
    activated, slope = gelu_parts(upward)
    result = middle + biases[5]
    for at in range(0, ff, D):
        result = result + jnp.dot(activated[:, at : at + D], w_mlp[:, ff + at : ff + at + D], preferred_element_type=F32)
    kept = (unit_one, scale_one, normed, heads, merged, summary, attended, unit_two, scale_two, normed_two, slope, activated)
    return result.astype(BF16), kept, window


def columns_of(values, at, number, over=0):
    place = (jnp.arange(128)[None, :] == at + number).astype(values.dtype)
    place = jnp.broadcast_to(place, (values.shape[over], 128))
    precision = highest if values.dtype == F32 else None
    return lax.dot_general(values, place, (((over,), (0,)), ((), ())), precision=precision, preferred_element_type=F32)


def turned_rows(kept, turn):
    attended, normed_two, activated = kept[6], kept[9], kept[11]
    return (
        moved(normed_two, turn, "tf,fp->tp"),
        moved(attended, turn, "ft,fp->pt"),
        [moved(activated[:, k : k + D], turn, "tf,fp->tp") for k in range(0, activated.shape[1], D)],
    )


def cube_backward(incoming_low, kept, params, order, docs, trade, before, between, window, send_rest, at, turn):
    w_qkv, w_out, w_mlp, gains, biases, up_bias = params
    unit_one, scale_one, normed, heads, merged, summary, attended, unit_two, scale_two, normed_two, slope, activated = kept
    ff = up_bias.shape[0]
    incoming = incoming_low.astype(F32)
    act_grad = jnp.concatenate([
        jnp.einsum("tb,ab->ta", incoming_low, w_mlp[:, ff + at : ff + at + D], preferred_element_type=F32)
        for at in range(0, ff, D)
    ], axis=1)
    up_grad = (act_grad * slope).astype(BF16)
    norm_two_grad = jnp.einsum("tb,ab->ta", up_grad, w_mlp[:, :ff], preferred_element_type=F32)
    middle_grad = incoming + layer_norm_back(norm_two_grad, unit_two, scale_two, gains[1])
    branch_grad = middle_grad.astype(BF16)
    merged_grad = jnp.einsum("fd,td->ft", w_out, branch_grad, preferred_element_type=F32).astype(BF16)
    merged_grad = merged_grad.reshape(HEADS, HEAD_DIM, TOK)
    merged_grad = jnp.einsum("hdt,htu->hdu", merged_grad, order, preferred_element_type=F32).astype(BF16)
    turned_two, turned, hidden_units = turn
    grad_rest = jnp.concatenate(
        [inner_rows(turned_two, up_grad).astype(BF16)]
        + [inner_rows(part, incoming_low).astype(BF16) for part in hidden_units]
        + [jnp.einsum("pt,td->pd", turned, branch_grad, preferred_element_type=F32).astype(BF16)],
        axis=1,
    )
    lifts = sum(columns_of(up_grad[:, k * D : (k + 1) * D], at, 8 + k) for k in range(4))
    merged_grad = trade(merged_grad)
    small = (
        columns_of(norm_two_grad * unit_two, at, 1)
        + columns_of(branch_grad, at, 5)
        + columns_of(norm_two_grad, at, 6)
        + columns_of(incoming_low, at, 7)
        + lifts
    )
    merged_grad, grad_rest, before = lax.optimization_barrier((merged_grad, grad_rest, before))
    sums_rest = send_rest(grad_rest)
    back_heads = attn_bwd(heads, merged_grad, docs, merged, summary)
    back_heads, window = lax.optimization_barrier((back_heads, window))
    mixed_grad = trade(back_heads)
    mixed_grad, before, small = lax.optimization_barrier((mixed_grad, between(before), small))
    mixed_grad = jnp.einsum("hfu,htu->hft", mixed_grad, order, preferred_element_type=F32).astype(BF16)
    mixed_grad = mixed_grad.reshape(HEADS, 3, HEAD_DIM, TOK).transpose(1, 0, 2, 3).reshape(3 * D, TOK)
    grad_qkv = jnp.einsum("td,ft->df", normed, mixed_grad, preferred_element_type=F32).astype(BF16)
    normed_grad = jnp.einsum("ft,df->td", mixed_grad, w_qkv, preferred_element_type=F32)
    start_grad = middle_grad + layer_norm_back(normed_grad, unit_one, scale_one, gains[0])
    late = (
        columns_of(normed_grad * unit_one, at, 0)
        + columns_of(normed_grad, at, 2)
        + columns_of(mixed_grad[:D], at, 3, 1)
        + columns_of(mixed_grad[2 * D :], at, 4, 1)
    )
    return start_grad, (grad_qkv, sums_rest, small + late), before, window


def half_pairs(source, count):
    return [(source * count + j, (1 - source) * count + j) for j in range(count)]


def core_swap(value, bit):
    return lax.ppermute(value, "seq", [(j, j ^ (1 << bit)) for j in range(16)])


def section_swap(value):
    return lax.ppermute(value, "section", [(0, 1), (1, 0)])


def place_bit(bit):
    return (lax.axis_index("seq") >> bit) & 1


def team(kind):
    def device(x, z, y, c):
        return x * 16 + z * 4 + y * 2 + c
    two, four = range(2), range(4)
    if kind == "whole plane":
        return [[device(x, z, y, c) for x in two for y in two for c in two] for z in four]
    if kind == "plane":
        return [[device(x, z, y, c) for x in two for y in two] for z in four for c in two]
    return [[device(x, z, y, c) for z in four] for x in two for y in two for c in two]


def plane_order():
    index = np.arange(D).reshape(4, 2, 2, 2, D // 32).transpose(3, 1, 2, 0, 4).reshape(D)
    place = np.empty(D, np.int32)
    place[index] = np.arange(D)
    return place


def moved(values, turn, equation):
    return jnp.einsum(equation, values, turn, preferred_element_type=F32).astype(BF16)


def team_trade(value, kind):
    return lax.all_to_all(value, ("section", "seq"), 0, 0, axis_index_groups=team(kind), tiled=True)


def collect_line(piece):
    return team_trade(jnp.broadcast_to(piece[None], (4,) + piece.shape), "line")


def collect_plane(now):
    rows, columns = now.shape[1:]
    now = team_trade(jnp.broadcast_to(now[None], (4,) + now.shape), "plane")
    now = now.reshape(2, 2, 4, rows, columns)
    got = core_swap(now, 0)
    upper = place_bit(0) == 1
    halves = []
    for x in range(2):
        a, b = now[x].transpose(1, 0, 2, 3), got[x].transpose(1, 0, 2, 3)
        both = jnp.stack([jnp.where(upper, b, a), jnp.where(upper, a, b)], axis=2)
        halves.append(both.reshape(16 * rows, columns))
    return halves


def plus(own, got, dtype=BF16):
    return (own.astype(F32) + got.astype(F32)).astype(dtype)


def fold(value, bit, axis, dtype=BF16):
    mine = place_bit(bit)
    away = lax.dynamic_index_in_dim(value, 1 - mine, axis, keepdims=False)
    kept = lax.dynamic_index_in_dim(value, mine, axis, keepdims=False)
    return plus(kept, core_swap(away, bit), dtype)


def reduce_core(partial):
    rows, half = partial.shape[0] // 16, partial.shape[1] // 2
    now = fold(partial.reshape(8, 2, rows, 2 * half), 0, 1).reshape(4, 2, rows, 2 * half)
    return jnp.stack([now[:, y, :, x * half : x * half + half] for x in range(2) for y in range(2)])


def reduce_plane(now):
    return jnp.sum(team_trade(now, "plane").astype(F32), axis=0).astype(BF16)


def reduce_line(now):
    return jnp.sum(team_trade(now, "line").astype(F32), axis=0)


def cube_body(inputs, cotangent, documents, w_qkv, w_out, w_up, w_down, norm_gains, biases, up_bias):
    section_id = lax.axis_index("section")
    place = lax.axis_index("seq")
    count = lax.axis_size("seq")
    half = count // 2
    micro_id = place // half
    member = section_id * half + place % half
    teams = [[s * count + k * half + j for s in range(2) for j in range(half)] for k in range(2)]
    axes = ("section", "seq")
    lower = section_id == 0

    def trade(value):
        return lax.all_to_all(value, axes, 0, 0, axis_index_groups=teams, tiled=True)

    def across(value, pairs):
        return lax.ppermute(value, axes, pairs)

    def own_rows(pair):
        mine = jnp.where(micro_id == 0, pair[0], pair[1])
        other = jnp.where(micro_id == 0, pair[1], pair[0])
        swap = across(other, [(count + j, count + (j ^ half)) for j in range(count)])
        return jnp.where(lower, mine, swap)

    turn = (jnp.asarray(plane_order())[:, None] == jnp.arange(D)[None, :]).astype(BF16)
    table = jnp.asarray(head_order())
    order = (table[:, None, :] == jnp.arange(TOK)[None, :, None]).astype(BF16)
    docs = jnp.where(micro_id == 0, documents[0], documents[1]).reshape(count, TOK)
    docs = jnp.where(micro_id == 0, docs, jnp.roll(docs, half, axis=0))
    own_order = lax.dynamic_index_in_dim(order, member, 0, keepdims=False)
    docs = jnp.dot(docs.astype(BF16), own_order, preferred_element_type=F32).reshape(count, 1, TOK)

    hidden = own_rows(inputs)
    wide = D // count
    lift = up_bias[0].reshape(-1, wide)
    small = jnp.concatenate([norm_gains[0], biases[0], lift]).T.astype(BF16)
    small = jnp.pad(small, ((0, 0), (0, 128 - small.shape[1])))

    ff = w_up.shape[2]
    low_qkv = w_qkv[0].astype(BF16)
    columns = low_qkv.shape[1] // 2
    got = across(low_qkv[:, columns:], half_pairs(0, count))
    piece = jnp.where(lower, low_qkv[:, :columns], got)
    line = collect_line(jnp.concatenate([piece, small], axis=1))

    piece, w_up, w_down = lax.optimization_barrier((piece, w_up, w_down))
    up_shard = w_up[0].astype(BF16).reshape(wide, count, 4, wide).transpose(0, 2, 1, 3).reshape(wide, ff)
    down_shard = w_down[0].astype(BF16).reshape(4, wide, D).transpose(1, 0, 2).reshape(wide, 4 * D)
    shard = jnp.concatenate([up_shard, down_shard, w_out[0].astype(BF16), low_qkv], axis=1)
    rows, rest = wide // 2, 2 * ff + D
    got = section_swap(jnp.where(lower, shard[rows:], shard[:rows]))
    near = jnp.concatenate([jnp.where(lower, shard[:rows, :rest], got[:, :rest]), jnp.where(lower, got, shard[rows:])[:, rest:]], axis=1)
    far = jnp.where(lower, got[:, :rest], shard[rows:, :rest])
    near, far, line, hidden = lax.optimization_barrier((near, far, line, hidden))
    parts = collect_plane(line)
    qkv_first = jnp.concatenate([part[:, :columns] for part in parts], axis=1)
    near = lax.all_gather(near, ("seq", "section"), axis=0, tiled=True)
    rest_final = lax.all_gather(far, ("seq", "section"), axis=0, tiled=True)
    rest_first, qkv_final = near[:, :rest], near[:, rest:]

    def lines(columns):
        values = columns[:, :12].astype(F32).T
        return values[:2], values[2:8], values[8:].reshape(ff)

    lines_first, lines_final = lines(parts[0][:, columns:]), lines(parts[1][:, columns:])
    params_first = (qkv_first, rest_first[:, 2 * ff :], rest_first) + lines_first
    beyond = [(count + j, count + (j ^ half)) for j in range(count)]
    back_over = [(count + j, j ^ half) for j in range(count)]
    first, kept_first, start_back = cube_forward(
        hidden.astype(F32), params_first, order, docs, trade, own_rows(cotangent)
    )
    params_final = (qkv_final, rest_final[:, 2 * ff :], rest_final) + lines_final
    final, kept_final, (far, turned_first) = cube_forward(
        first.astype(F32), params_final, order, docs, trade, (across(first, back_over), turned_rows(kept_first, turn))
    )

    def placed(mine, other):
        return jnp.where(micro_id == 0, jnp.stack([mine, other]), jnp.stack([other, mine]))[None]

    def scattered(partial):
        return lax.psum_scatter(
            partial, axes, scatter_dimension=0, tiled=True, axis_index_groups=team("whole plane")
        )

    def fold_line(partial):
        return fold(partial.reshape(2, 2, rows, -1), 3, 0)

    start_back, merged = lax.optimization_barrier((start_back, kept_final[4]))
    kept_final = kept_final[:4] + (merged,) + kept_final[5:]
    grad_final, terms_final, _, window = cube_backward(
        start_back, kept_final, params_final, order, docs, trade, None, lambda now: now,
        (across(final, half_pairs(0, count)), across(final, beyond)), scattered, 12,
        turned_rows(kept_final, turn),
    )
    layer_outputs = placed(jnp.where(lower, first, window[0]), jnp.where(lower, far, window[1]))
    sent, qkv_final, small_final = lax.optimization_barrier(
        (grad_final.astype(BF16), terms_final[0], terms_final[2])
    )
    grad_first, terms_first, qkv_final, window = cube_backward(
        sent, kept_first, params_first, order, docs, trade, reduce_core(qkv_final), reduce_plane,
        (across(sent, half_pairs(0, count)), across(sent, beyond), fold_line(terms_final[1])), scattered, 0,
        turned_first,
    )
    rest_final = fold(window[2], 2, 0)

    smalls = (terms_first[2] + small_final).astype(BF16)
    smalls = fold(smalls.reshape(8, 2, wide, 128), 0, 1).reshape(4, 2, wide, 128)
    smalls = jnp.stack([smalls[:, 0], smalls[:, 1]] * 2)
    now = jnp.concatenate([reduce_core(terms_first[0]), smalls], axis=3)
    plane, far_back = lax.optimization_barrier((reduce_plane(now), across(grad_first.astype(BF16), back_over)))
    now = reduce_line(jnp.concatenate([plane, qkv_final], axis=2))
    now, rest_first = lax.optimization_barrier((now, fold_line(terms_first[1])))
    columns = qkv_final.shape[2]
    qkv_first, smalls, qkv_final = now[:, :columns], now[:, columns : columns + 24], now[:, columns + 128 :]
    smalls = jnp.where(lower, smalls[:, :12], smalls[:, 12:]).T
    rest_first = fold(rest_first, 2, 0)
    input_grads = placed(
        jnp.where(lower, grad_first, window[0].astype(F32)), jnp.where(lower, far_back, window[1]).astype(F32)
    )

    away = section_swap(jnp.where(lower, rest_final, rest_first))
    rest = jnp.where(lower, jnp.concatenate([rest_first, away]), jnp.concatenate([away, rest_final]))
    qkv_final, qkv_first, layer_outputs = lax.optimization_barrier((qkv_final, qkv_first, layer_outputs))
    away = section_swap(jnp.where(lower, qkv_final, qkv_first).astype(BF16)).astype(F32)
    qkv = jnp.where(
        lower, jnp.concatenate([qkv_first, away], axis=1), jnp.concatenate([away, qkv_final], axis=1)
    )
    up = rest[:, :ff].astype(F32).reshape(wide, 4, count, wide).transpose(0, 2, 1, 3).reshape(wide, ff)
    rest = rest[:, ff:].astype(F32)
    down = rest[:, :ff].reshape(wide, 4, D).transpose(1, 0, 2).reshape(4 * wide, D)
    return (
        layer_outputs,
        input_grads,
        qkv[None],
        rest[None, :, ff:],
        up[None],
        down[None],
        smalls[None, :2],
        smalls[None, 2:8],
        smalls[8:].reshape(1, -1),
    )


def solution(mesh):
    cube = mesh.shape["seq"] == 16
    return jax.shard_map(
        cube_body if cube else body,
        mesh=mesh,
        in_specs=(
            P(None, "seq", None),
            P(None, "seq", None),
            P(),
            P("section", "seq", None),
            P("section", "seq", None),
            P("section", "seq", None),
            P("section", "seq", None),
            P("section", None, "seq"),
            P("section", None, "seq"),
            P("section", "seq"),
        ),
        out_specs=(
            P("section", None, "seq", None),
            P("section", None, "seq", None),
            P("section", "seq", None),
            P("section", "seq", None),
            P("section", "seq", None),
            P("section", "seq", None),
            P("section", None, "seq"),
            P("section", None, "seq"),
            P("section", "seq"),
        ),
        check_vma=False,
    )
```
